128 devices in a mesh: tiles: 16 (over x, z), cols: 8 (over y, core).
Axes of the slice: x: 4, y: 4, z: 4, core: 2. Of those that a mesh axis runs over, the one named last changes fastest.
Arguments:
- object_field: float32 [2, 2, 4096, 2048], P(None, None, 'tiles', 'cols')
- probe: float32 [2, 4, 128, 128], replicated, may hold values from -3 to 3
- row_offsets: int32 [16, 8, 8], P('tiles', 'cols'), may hold values from 0 to 255, as said below
- col_offsets: int32 [16, 8, 8], P('tiles', 'cols'), may hold values from 0 to 255, as said below
- counts: int32 [16, 8], P('tiles', 'cols'), may hold values from 1 to 8, as said below
- measured: float32 [16, 8, 8, 128, 128], P('tiles', 'cols'), may hold values from 0.25 to 2.5
Outputs:
- new_object: float32 [2, 2, 4096, 2048], P(None, None, 'tiles', 'cols')
- new_probe: float32 [2, 4, 128, 128], replicated
The draws below stay inside these ranges and needn't reach their ends.
Inputs may be any that keep to these rules, and one draw needn't show every extreme that they name: `row_offsets`: A patch never leaves the object region: on the last row of tiles the offset is at most 128; elsewhere it may reach into the tile below. `col_offsets`: A patch never leaves the object region: on the last column of tiles the offset is at most 128; elsewhere it may reach into the tile to the right. `counts`: slots from a device's count on are unused; some device has 8 live positions.
All inputs are finite; a program needn't handle non-finite values.
Results may differ from the reference program's by a relative error of at most 0.0001.
Values sent between devices are 32-bit elements; how exact they have to be, the bound alone decides.
A program may use at most 128 MiB of HBM per device.

```python
import math
import jax
import jax.numpy as jnp
from jax import lax

P_SIZE = 128
MODES = 4
SLICES = 2
ITERS = 2
POS_CAP = 8
TR = 256
TC = 256
NR = 4096
NC = 2048
N_TILES = 16
N_COLS = 8


def draw_object_field(key, part):
    key = jax.random.fold_in(key, 11)
    first, second = jax.random.split(key)
    shape = (SLICES, NR, NC)
    real_part = jax.random.uniform(first, shape, jnp.float32, 0.7, 1.1)
    imag_part = jax.random.uniform(second, shape, jnp.float32, -0.3, 0.3)
    return jnp.stack([real_part, imag_part])


def offsets_draw(key, tile_len, grid_len, other_len, along_rows):
    first, second, third, fourth = jax.random.split(key, 4)
    if along_rows:
        place = jnp.arange(grid_len, dtype=jnp.int32)[:, None, None] + jnp.zeros((grid_len, other_len, POS_CAP), jnp.int32)
        shape = (grid_len, other_len, POS_CAP)
    else:
        place = jnp.arange(grid_len, dtype=jnp.int32)[None, :, None] + jnp.zeros((other_len, grid_len, POS_CAP), jnp.int32)
        shape = (other_len, grid_len, POS_CAP)
    top = jnp.where(place < grid_len - 1, tile_len, tile_len - P_SIZE + 1)
    values = jax.random.randint(first, shape, 0, top, dtype=jnp.int32)
    flat = values.reshape(-1)
    inner = jax.random.randint(second, (), 0, grid_len - 1, dtype=jnp.int32)
    across = jax.random.randint(third, (), 0, other_len, dtype=jnp.int32)
    if along_rows:
        spot = (inner * other_len + across) * POS_CAP
    else:
        spot = (across * grid_len + inner) * POS_CAP
    flat = flat.at[spot].set(tile_len - 1)
    low_spot = jax.random.randint(fourth, (), 0, flat.shape[0] // POS_CAP, dtype=jnp.int32) * POS_CAP + 1
    flat = flat.at[low_spot].set(0)
    return flat.reshape(shape)


def draw_row_offsets(key, part):
    key = jax.random.fold_in(key, 23)
    return offsets_draw(key, TR, N_TILES, N_COLS, True)


def draw_col_offsets(key, part):
    key = jax.random.fold_in(key, 37)
    return offsets_draw(key, TC, N_COLS, N_TILES, False)


def draw_counts(key, part):
    key = jax.random.fold_in(key, 41)
    first, second, third, fourth = jax.random.split(key, 4)
    shape = (N_TILES * N_COLS,)
    left = jax.random.randint(first, shape, 0, POS_CAP, dtype=jnp.int32)
    right = jax.random.randint(second, shape, 0, POS_CAP, dtype=jnp.int32)
    loads = 1 + left * right // (POS_CAP - 1)
    busy = jax.random.randint(third, (), 0, N_TILES * N_COLS, dtype=jnp.int32)
    light = (busy + 1 + jax.random.randint(fourth, (), 0, N_TILES * N_COLS - 1, dtype=jnp.int32)) % (N_TILES * N_COLS)
    loads = loads.at[busy].set(POS_CAP)
    loads = loads.at[light].set(1)
    return loads.reshape(N_TILES, N_COLS)


def shard_levels(rng, dims, pieces, least, largest):
    factor_of = 1.0
    for dim, parts in pieces:
        steps = jax.random.uniform(jax.random.fold_in(jax.random.fold_in(rng, 6), dim), (parts,), jnp.float32, least / len(pieces), largest / len(pieces))
        factor_of = factor_of * jnp.repeat(jnp.exp(steps), dims[dim] // parts).reshape((-1,) + (1,) * (len(dims) - 1 - dim))
    return factor_of


def gaussian(own_key, shape, scale, bound, kind=jnp.bfloat16):
    entries = jax.random.normal(own_key, shape, jnp.float32) * scale
    return jnp.minimum(jnp.maximum(entries, -bound), bound).astype(kind)


def setup_inputs(seed: int = 0) -> dict:
    streams_of = jax.random.split(jax.random.key(seed), 7)
    return {
        "object_field": draw_object_field(jax.random.fold_in(streams_of[6], 71), 0),
        "probe": gaussian(streams_of[1], (2, MODES, P_SIZE, P_SIZE), 0.4, 3.0, jnp.float32),
        "row_offsets": draw_row_offsets(jax.random.fold_in(streams_of[6], 71), 0),
        "col_offsets": draw_col_offsets(jax.random.fold_in(streams_of[6], 71), 0),
        "counts": draw_counts(jax.random.fold_in(streams_of[6], 71), 0),
        "measured": jnp.clip(jnp.exp(math.log(2.5) - 2.3025851 * jax.random.uniform(streams_of[5], (N_TILES, N_COLS, POS_CAP, P_SIZE, P_SIZE), jnp.float32) ** shard_levels(streams_of[5], (N_TILES, N_COLS, POS_CAP, P_SIZE, P_SIZE), ((0, 16), (1, 8)), -0.2, 0.2)), 0.25, 2.5),
    }


step_object = 0.25


def fresnel_kernel(size):
    index_line = jnp.arange(size, dtype=jnp.int32)
    freq = jnp.where(index_line < size // 2, index_line, index_line - size)
    square = freq * freq
    phase_index = (square[:, None] + square[None, :]) % (4 * size)
    angle = (-2.0 * math.pi / (4 * size)) * phase_index.astype(jnp.float32)
    return lax.complex(jnp.cos(angle), jnp.sin(angle))


def forward_fft(field):
    return jnp.fft.fft2(field, norm="ortho")


def inverse_fft(field):
    return jnp.fft.ifft2(field, norm="ortho")


def iteration(obj_c, probe_c, kernel, row_offsets, col_offsets, counts, measured):
    row_glob = (jnp.arange(N_TILES, dtype=jnp.int32)[:, None, None] * TR + row_offsets).reshape(-1).astype(jnp.int32)
    col_glob = (jnp.arange(N_COLS, dtype=jnp.int32)[None, :, None] * TC + col_offsets).reshape(-1).astype(jnp.int32)
    alive_all = (jnp.arange(POS_CAP, dtype=jnp.int32)[None, None, :] < counts[:, :, None]).reshape(-1).astype(jnp.float32)
    data_all = measured.reshape(-1, P_SIZE, P_SIZE)
    zero = jnp.zeros((), jnp.int32)

    def visit(carry, scan_entry):
        grad_obj, grad_probe = carry
        row_index, column_index, active_flag, measured_amplitude = scan_entry
        patch = lax.dynamic_slice(obj_c, (zero, row_index, column_index), (SLICES, P_SIZE, P_SIZE))
        psi = probe_c * patch[0]
        carried = []
        for s in range(1, SLICES):
            spread = inverse_fft(kernel * forward_fft(psi))
            carried.append(spread)
            psi = patch[s] * spread
        far = forward_fft(psi)
        intensity_pattern = jnp.sum(jnp.real(far) ** 2 + jnp.imag(far) ** 2, axis=0)
        residual_error = (intensity_pattern - measured_amplitude) * active_flag
        back = inverse_fft(residual_error * far)
        grads = [back[0]] * SLICES
        for s in range(SLICES - 1, 0, -1):
            grads[s] = jnp.sum(jnp.conj(carried[s - 1]) * back, axis=0)
            back = jnp.conj(patch[s]) * back
            back = inverse_fft(jnp.conj(kernel) * forward_fft(back))
        grads[0] = jnp.sum(jnp.conj(probe_c) * back, axis=0)
        probe_term = jnp.conj(patch[0]) * back
        current = lax.dynamic_slice(grad_obj, (zero, row_index, column_index), (SLICES, P_SIZE, P_SIZE))
        grad_obj = lax.dynamic_update_slice(grad_obj, current + jnp.stack(grads), (zero, row_index, column_index))
        return (grad_obj, grad_probe + probe_term), None

    start = (jnp.zeros_like(obj_c), jnp.zeros_like(probe_c))
    (grad_obj, grad_probe), _ = lax.scan(visit, start, (row_glob, col_glob, alive_all, data_all))
    return grad_obj, grad_probe


def reference(object_field, probe, row_offsets, col_offsets, counts, measured):
    obj_c = lax.complex(object_field[0], object_field[1])
    probe_c = lax.complex(probe[0], probe[1])
    kernel = fresnel_kernel(P_SIZE)
    step_probe = 1.0 / (N_TILES * N_COLS * POS_CAP)
    for sweep in range(ITERS):
        grad_obj, grad_probe = iteration(obj_c, probe_c, kernel, row_offsets, col_offsets, counts, measured)
        obj_c = obj_c - step_object * grad_obj
        probe_c = probe_c - step_probe * grad_probe
    new_object = jnp.stack([jnp.real(obj_c), jnp.imag(obj_c)])
    new_probe = jnp.stack([jnp.real(probe_c), jnp.imag(probe_c)])
    return new_object, new_probe
```

```python
import functools
import math

import jax
import jax.numpy as jnp
import ml_dtypes
import numpy as np
from jax import lax
from jax.experimental import pallas as pl
from jax.experimental.pallas import tpu as pltpu
from jax.sharding import PartitionSpec as P

ITERS = 2
STEP_OBJECT = 0.25
f32, bf16 = jnp.float32, jnp.bfloat16
MESH = pl.DeviceIdType.MESH
VMEM_LIMIT = 56 * 2**20

A_PLUS, A_MINUS, F_PLUS, F_MINUS = 0, 2, 4, 6


def split_table(table):
    high = table.astype(np.float32).astype(ml_dtypes.bfloat16)
    low = (table - high.astype(np.float64)).astype(np.float32).astype(ml_dtypes.bfloat16)
    return [high, low]


def transform_tables(size):
    line = np.arange(size)
    dft = np.exp(-2j * np.pi * (np.outer(line, line) % size) / size) / math.sqrt(size)
    freq = np.where(line < size // 2, line, line - size)
    chirp = np.exp(-2j * np.pi * ((freq * freq) % (4 * size)) / (4 * size))
    propagator = np.conj(dft) @ (chirp[:, None] * dft)
    parts = []
    for matrix in (propagator, dft):
        real, imag = matrix.real, matrix.imag
        plus = np.block([[real, imag], [-imag, real]])
        parts += split_table(plus) + split_table(plus.T)
    return np.stack(parts)


def split(value):
    high = value.astype(bf16)
    return high, (value - high.astype(f32)).astype(bf16)


def product(first, second):
    dot = functools.partial(jnp.dot, preferred_element_type=f32)
    return dot(first[0], second[0]) + (dot(first[1], second[0]) + dot(first[0], second[1]))


def two_sided(fields, table, left, right):
    n = fields[0][0].shape[0]
    modes = range(len(fields))
    stacked = [jnp.concatenate(field, axis=0) for field in fields]
    middle = product((table[left], table[left + 1]), split(jnp.concatenate(stacked, axis=1)))
    columns = [middle[:, n * m : n * m + n] for m in modes]
    beside = [jnp.concatenate([c[:n], c[n:]], axis=1) for c in columns]
    result = product(split(jnp.concatenate(beside, axis=0)), (table[right], table[right + 1]))
    rows = [result[n * m : n * m + n] for m in modes]
    return [(row[:, :n], row[:, n:]) for row in rows]


def times(a, b):
    return (a[0] * b[0] - a[1] * b[1], a[0] * b[1] + a[1] * b[0])


def conj_times(a, b):
    return (a[0] * b[0] + a[1] * b[1], a[0] * b[1] - a[1] * b[0])


def total(terms):
    real, imag = terms[0]
    for term in terms[1:]:
        real, imag = real + term[0], imag + term[1]
    return real, imag


GROUP = 4


def gradient_kernel(rows, cols, counts, extended, probe, measured, table, grad, grad_probe):
    n = probe.shape[-1]
    modes = range(probe.shape[1])
    grad[...] = jnp.zeros_like(grad)
    grad_probe[...] = jnp.zeros_like(grad_probe)
    lane = lax.broadcasted_iota(jnp.int32, (n, n), 1)
    count = counts[0]

    def visit(step, carry):
        beams = [(probe[0, m], probe[1, m]) for m in modes]
        slots = []
        for k in range(GROUP):
            slot = step * GROUP + k
            live = slot < count
            row = jnp.where(live, rows[slot], 0)
            col = jnp.where(live, cols[slot], 0)
            block = lax.shift_right_logical(col, 7)
            slots.append((slot, jnp.where(live, 1.0, 0.0).astype(f32), row, block, col - block * n))

        def window(plane, slot):
            _, _, row, block, shift = slot
            back = jnp.bitwise_and(n - shift, n - 1)
            near = pltpu.roll(extended[plane, block, pl.ds(row, n), :], back, 1)
            far = pltpu.roll(extended[plane, block + 1, pl.ds(row, n), :], back, 1)
            return jnp.where(lane < n - shift, near, far)

        first = [(window(0, s), window(2, s)) for s in slots]
        spread = [two_sided([times(b, o) for b in beams], table, A_MINUS, A_PLUS) for o in first]
        second = [(window(1, s), window(3, s)) for s in slots]
        far = [
            two_sided([times(o, x) for x in fields], table, F_MINUS, F_PLUS)
            for o, fields in zip(second, spread)
        ]
        residual = []
        for slot, fields in zip(slots, far):
            intensity = sum(y[0] * y[0] + y[1] * y[1] for y in fields)
            residual.append((intensity - measured[slot[0]]) * slot[1])
        back = [
            two_sided([(r * y[0], r * y[1]) for y in fields], table, F_PLUS, F_MINUS)
            for r, fields in zip(residual, far)
        ]
        grad_second = [
            total([conj_times(x, g) for x, g in zip(fields, backs)])
            for fields, backs in zip(spread, back)
        ]
        back = [
            two_sided([conj_times(o, g) for g in backs], table, A_PLUS, A_MINUS)
            for o, backs in zip(second, back)
        ]
        grad_first = [total([conj_times(b, g) for b, g in zip(beams, backs)]) for backs in back]
        for m in modes:
            real, imag = total([conj_times(o, backs[m]) for o, backs in zip(first, back)])
            grad_probe[0, m] += real
            grad_probe[1, m] += imag
        for (_, _, row, block, shift), g0, g1 in zip(slots, grad_first, grad_second):
            kept = lane >= shift
            for plane, value in enumerate((g0[0], g1[0], g0[1], g1[1])):
                moved = pltpu.roll(value, shift, 1)
                grad[plane, block, pl.ds(row, n), :] += jnp.where(kept, moved, 0.0)
                grad[plane, block + 1, pl.ds(row, n), :] += jnp.where(kept, 0.0, moved)
        return carry

    lax.fori_loop(0, (count + GROUP - 1) // GROUP, visit, 0)


SMEM_SPEC = pl.BlockSpec(memory_space=pltpu.SMEM)
VMEM_SPEC = pl.BlockSpec(memory_space=pltpu.VMEM)
ANY_SPEC = pl.BlockSpec(memory_space=pl.ANY)


def gradients(rows, cols, counts, extended, probe, measured, table):
    slots = rows.shape[0]
    work = slots * probe.shape[1] * 8 * 3 * 2 * 256 * 256 * 128
    return pl.pallas_call(
        gradient_kernel,
        out_shape=[
            jax.ShapeDtypeStruct(extended.shape, f32),
            jax.ShapeDtypeStruct(probe.shape, f32),
        ],
        in_specs=[SMEM_SPEC] * 3 + [VMEM_SPEC] * 4,
        out_specs=[VMEM_SPEC] * 2,
        compiler_params=pltpu.CompilerParams(vmem_limit_bytes=VMEM_LIMIT),
        cost_estimate=pl.CostEstimate(flops=work, bytes_accessed=8 * 2**20, transcendentals=0),
        name="gradients",
    )(rows, cols, counts, extended, probe, measured, table)


class Place:
    def __init__(self, tiles, cols):
        self.tiles, self.cols = tiles, cols
        self.t, self.c = lax.axis_index("tiles"), lax.axis_index("cols")

    def at(self, down, right):
        return (
            lax.rem(self.t + (down + self.tiles), self.tiles),
            lax.rem(self.c + (right + self.cols), self.cols),
        )


def greet(devices):
    barrier = pltpu.get_barrier_semaphore()
    for device in devices:
        pl.semaphore_signal(barrier, inc=1, device_id=device, device_id_type=MESH)
    pl.semaphore_wait(barrier, len(devices))


class Copies:
    def __init__(self, send, recv):
        self.send, self.recv, self.used, self.started = send, recv, 0, []

    def start(self, source, target, device):
        k = self.used
        self.used += 1
        copy = pltpu.make_async_remote_copy(
            src_ref=source,
            dst_ref=target,
            send_sem=self.send.at[k],
            recv_sem=self.recv.at[k],
            device_id=device,
            device_id_type=MESH,
        )
        copy.start()
        self.started.append(copy)
        return copy

    def finish(self):
        for copy in self.started:
            copy.wait_send()


def widen_kernel(tiles, cols, size, field, extended, local_sem, send, recv):
    planes, height, width = field.shape
    blocks = width // size
    place = Place(tiles, cols)
    own = []
    for j in range(blocks):
        copy = pltpu.make_async_copy(
            field.at[:, :, pl.ds(j * size, size)],
            extended.at[:, j, pl.ds(0, height), :],
            local_sem.at[j],
        )
        copy.start()
        own.append(copy)
    greet([place.at(d, r) for d, r in ((-1, -1), (-1, 0), (0, -1), (1, 1), (1, 0), (0, 1))])
    copies = Copies(send, recv)
    up, left, corner = place.at(-1, 0), place.at(0, -1), place.at(-1, -1)
    top = pl.ds(0, size)
    below = pl.ds(height, size)
    for j in range(blocks):
        copies.start(field.at[:, top, pl.ds(j * size, size)], extended.at[:, j, below, :], up)
    copies.start(field.at[:, top, pl.ds(0, size)], extended.at[:, blocks, below, :], corner)
    copies.start(
        field.at[:, :, pl.ds(0, size)], extended.at[:, blocks, pl.ds(0, height), :], left
    )
    for copy in own:
        copy.wait()
    for copy in copies.started:
        copy.wait_recv()
    copies.finish()


def widen(field, size, tiles, cols):
    planes, height, width = field.shape
    blocks = width // size
    return pl.pallas_call(
        functools.partial(widen_kernel, tiles, cols, size),
        out_shape=jax.ShapeDtypeStruct((planes, blocks + 1, height + size, size), f32),
        in_specs=[ANY_SPEC],
        out_specs=VMEM_SPEC,
        scratch_shapes=[
            pltpu.SemaphoreType.DMA((blocks,)),
            pltpu.SemaphoreType.DMA((blocks + 2,)),
            pltpu.SemaphoreType.DMA((blocks + 2,)),
        ],
        compiler_params=pltpu.CompilerParams(
            collective_id=0, has_side_effects=True, vmem_limit_bytes=VMEM_LIMIT
        ),
        name="widen",
    )(field)


class ProbeSum:
    def __init__(self, place, copies, grad, pair, pieces, column, halves):
        self.place, self.copies = place, copies
        self.grad, self.pair, self.pieces, self.column, self.halves = grad, pair, pieces, column, halves
        self.half = grad.shape[0] // 2
        self.piece = self.half // place.tiles
        self.core = lax.rem(place.c, 2)
        self.partner = (place.t, place.c + 1 - 2 * self.core)
        self.mine = pl.ds(self.core * self.half, self.half)
        self.others = pl.ds((1 - self.core) * self.half, self.half)

    def scatter_pair(self):
        self.step = self.copies.start(self.grad.at[self.others], self.pair, self.partner)

    def scatter_tiles(self):
        self.step.wait_recv()
        self.grad[self.mine] += self.pair[...]
        place, piece = self.place, self.piece
        self.steps = []
        for k in range(1, place.tiles):
            peer = lax.rem(place.t + k, place.tiles)
            source = self.grad.at[pl.ds(self.core * self.half + peer * piece, piece)]
            self.steps.append(
                self.copies.start(source, self.pieces.at[k - 1], (peer, place.c))
            )

    def sum_column(self):
        place, piece = self.place, self.piece
        value = self.grad[pl.ds(self.core * self.half + place.t * piece, piece)]
        for k, step in enumerate(self.steps):
            step.wait_recv()
            value += self.pieces[k]
        chips = place.cols // 2
        chip = place.c // 2
        self.column[chip] = value
        self.steps = []
        for k in range(1, chips):
            peer = (place.t, lax.rem(place.c + 2 * k, place.cols))
            self.steps.append(
                self.copies.start(self.column.at[chip], self.column.at[chip], peer)
            )

    def gather_tiles(self):
        for step in self.steps:
            step.wait_recv()
        place, piece = self.place, self.piece
        value = self.column[0]
        for k in range(1, place.cols // 2):
            value += self.column[k]
        own = pl.ds(self.core * self.half + place.t * piece, piece)
        self.halves[own] = value
        self.steps = []
        for k in range(1, place.tiles):
            peer = lax.rem(place.t + k, place.tiles)
            self.steps.append(
                self.copies.start(self.halves.at[own], self.halves.at[own], (peer, place.c))
            )

    def gather_pair(self):
        for step in self.steps:
            step.wait_recv()
        self.step = self.copies.start(
            self.halves.at[self.mine], self.halves.at[self.mine], self.partner
        )

    def result(self):
        self.step.wait_recv()
        return self.halves[...]

    @staticmethod
    def copies_needed(tiles, cols):
        return 2 * tiles + cols // 2 - 1

    @staticmethod
    def scratch(rows, lanes, tiles, cols):
        half = rows // 2
        piece = half // tiles
        return [
            pltpu.VMEM((half, lanes), f32),
            pltpu.VMEM((tiles - 1, piece, lanes), f32),
            pltpu.VMEM((cols // 2, piece, lanes), f32),
            pltpu.VMEM((rows, lanes), f32),
        ]


def met(place):
    devices = [place.at(k, 0) for k in range(1, place.tiles)]
    return devices + [
        place.at(0, k) for k in range(1, place.cols) if k % 2 == 0 or k in (1, place.cols - 1)
    ]


def exchange_kernel(
    tiles,
    cols,
    grad,
    extended,
    grad_probe,
    probe,
    new_extended,
    new_probe,
    from_left,
    from_right,
    from_up,
    from_down,
    from_corner,
    pair,
    pieces,
    column,
    halves,
    send,
    recv,
):
    planes, count, tall, size = grad.shape
    last = count - 1
    height = tall - size
    top, middle, below = pl.ds(0, size), pl.ds(size, height - size), pl.ds(height, size)
    place = Place(tiles, cols)
    greet(met(place))
    copies = Copies(send, recv)
    up, down, left, right = place.at(-1, 0), place.at(1, 0), place.at(0, -1), place.at(0, 1)
    reduce = ProbeSum(place, copies, grad_probe, pair, pieces, column, halves)
    every = range(planes)
    reduce.scatter_pair()
    sides = [copies.start(grad.at[p, last], from_left.at[p], right) for p in every]
    ups, downs = {}, {}
    for j in list(range(1, last)) + [0]:
        for p in every:
            if j == 0:
                sides[p].wait_recv()
                grad[p, 0] += from_left[p]
            ups[p, j] = copies.start(grad.at[p, j, below], from_up.at[p, j], down)
            downs[p, j] = copies.start(grad.at[p, j, top], from_down.at[p, j], up)
        if j == 1:
            reduce.scatter_tiles()
    middles = [copies.start(grad.at[p, 0, middle], from_right.at[p], left) for p in every]
    reduce.sum_column()
    reduce.gather_tiles()
    corners = {}
    for j in [0] + list(range(1, last)):
        for p in every:
            ups[p, j].wait_recv()
            downs[p, j].wait_recv()
            ups[p, j].wait_send()
            downs[p, j].wait_send()
            if j == 0:
                grad[p, j, top] += from_up[p, j]
                grad[p, j, below] += from_down[p, j]
                for k, rows in enumerate((top, below)):
                    corners[p, k] = copies.start(grad.at[p, j, rows], from_corner.at[p, k], left)
                new_extended[p, j] = extended[p, j] - STEP_OBJECT * grad[p, j]
            else:
                new = extended[p, j] - STEP_OBJECT * grad[p, j]
                new_extended[p, j] = new
                new_extended[p, j, top] -= STEP_OBJECT * from_up[p, j]
                new_extended[p, j, below] -= STEP_OBJECT * from_down[p, j]
    reduce.gather_pair()
    for p in every:
        middles[p].wait_recv()
        new_extended[p, last, middle] = extended[p, last, middle] - STEP_OBJECT * from_right[p]
        for k, rows in enumerate((top, below)):
            corners[p, k].wait_recv()
            new_extended[p, last, rows] = extended[p, last, rows] - STEP_OBJECT * from_corner[p, k]
    positions = 8 * tiles * cols
    new_probe[...] = probe[...] - (1.0 / positions) * reduce.result()
    waited = {id(copy) for copy in list(ups.values()) + list(downs.values())}
    for copy in copies.started:
        if id(copy) not in waited:
            copy.wait_send()


def exchange(grad, extended, grad_probe, probe, tiles, cols):
    planes, count, tall, size = grad.shape
    last = count - 1
    height = tall - size
    rows, lanes = probe.shape
    needed = ProbeSum.copies_needed(tiles, cols) + planes * (1 + 2 * last + 1 + 2)
    return pl.pallas_call(
        functools.partial(exchange_kernel, tiles, cols),
        out_shape=[
            jax.ShapeDtypeStruct(extended.shape, f32),
            jax.ShapeDtypeStruct(probe.shape, f32),
        ],
        in_specs=[VMEM_SPEC] * 4,
        out_specs=[VMEM_SPEC] * 2,
        scratch_shapes=[
            pltpu.VMEM((planes, tall, size), f32),
            pltpu.VMEM((planes, height - size, size), f32),
            pltpu.VMEM((planes, last, size, size), f32),
            pltpu.VMEM((planes, last, size, size), f32),
            pltpu.VMEM((planes, 2, size, size), f32),
            *ProbeSum.scratch(rows, lanes, tiles, cols),
            pltpu.SemaphoreType.DMA((needed,)),
            pltpu.SemaphoreType.DMA((needed,)),
        ],
        compiler_params=pltpu.CompilerParams(
            collective_id=1, has_side_effects=True, vmem_limit_bytes=VMEM_LIMIT
        ),
        name="exchange",
    )(grad, extended, grad_probe, probe)


def narrow_kernel(
    tiles,
    cols,
    grad,
    extended,
    grad_probe,
    probe,
    new_field,
    new_probe,
    from_left,
    from_up,
    pair,
    pieces,
    column,
    halves,
    send,
    recv,
):
    planes, count, tall, size = grad.shape
    last = count - 1
    height = tall - size
    top, own, below = pl.ds(0, size), pl.ds(0, height), pl.ds(height, size)
    place = Place(tiles, cols)
    greet(met(place))
    copies = Copies(send, recv)
    down, right = place.at(1, 0), place.at(0, 1)
    reduce = ProbeSum(place, copies, grad_probe, pair, pieces, column, halves)
    every = range(planes)
    reduce.scatter_pair()
    sides = [copies.start(grad.at[p, last], from_left.at[p], right) for p in every]
    ups = {}
    for j in list(range(1, last)) + [0]:
        for p in every:
            if j == 0:
                sides[p].wait_recv()
                grad[p, 0] += from_left[p]
            ups[p, j] = copies.start(grad.at[p, j, below], from_up.at[p, j], down)
        if j == 1:
            reduce.scatter_tiles()
    for j in range(last):
        for p in every:
            new_field[p, :, pl.ds(j * size, size)] = extended[p, j, own] - STEP_OBJECT * grad[p, j, own]
    reduce.sum_column()
    reduce.gather_tiles()
    reduce.gather_pair()
    for j in list(range(1, last)) + [0]:
        for p in every:
            ups[p, j].wait_recv()
            new_field[p, top, pl.ds(j * size, size)] -= STEP_OBJECT * from_up[p, j]
    positions = 8 * tiles * cols
    new_probe[...] = probe[...] - (1.0 / positions) * reduce.result()
    copies.finish()


def narrow(grad, extended, grad_probe, probe, tiles, cols):
    planes, count, tall, size = grad.shape
    last = count - 1
    height = tall - size
    rows, lanes = probe.shape
    needed = ProbeSum.copies_needed(tiles, cols) + planes * (1 + last)
    return pl.pallas_call(
        functools.partial(narrow_kernel, tiles, cols),
        out_shape=[
            jax.ShapeDtypeStruct((planes, height, last * size), f32),
            jax.ShapeDtypeStruct(probe.shape, f32),
        ],
        in_specs=[VMEM_SPEC] * 4,
        out_specs=[VMEM_SPEC] * 2,
        scratch_shapes=[
            pltpu.VMEM((planes, tall, size), f32),
            pltpu.VMEM((planes, last, size, size), f32),
            *ProbeSum.scratch(rows, lanes, tiles, cols),
            pltpu.SemaphoreType.DMA((needed,)),
            pltpu.SemaphoreType.DMA((needed,)),
        ],
        compiler_params=pltpu.CompilerParams(
            collective_id=2, has_side_effects=True, vmem_limit_bytes=VMEM_LIMIT
        ),
        name="narrow",
    )(grad, extended, grad_probe, probe)


def local(table, tiles, cols, object_field, probe, row_offsets, col_offsets, counts, measured):
    size = probe.shape[-1]
    height, width = object_field.shape[2:]
    slots = row_offsets.shape[-1]
    rows = row_offsets.reshape(slots)
    columns = col_offsets.reshape(slots)
    count = counts.reshape(1)
    data = measured.reshape(slots, size, size)
    field = object_field.reshape(4, height, width)
    beam = probe
    flat = (probe.shape[0] * probe.shape[1] * size, size)
    extended = widen(field, size, tiles, cols)
    for sweep in range(ITERS):
        grad, grad_beam = gradients(rows, columns, count, extended, beam, data, table)
        combine = narrow if sweep == ITERS - 1 else exchange
        extended, beam = combine(
            grad, extended, grad_beam.reshape(flat), beam.reshape(flat), tiles, cols
        )
        beam = beam.reshape(probe.shape)
    return extended.reshape(object_field.shape), beam


def solution(mesh):
    table = jnp.asarray(transform_tables(128))
    tiles, cols = mesh.shape["tiles"], mesh.shape["cols"]
    in_specs = (
        P(None, None, "tiles", "cols"),
        P(),
        P("tiles", "cols", None),
        P("tiles", "cols", None),
        P("tiles", "cols"),
        P("tiles", "cols", None, None, None),
    )
    out_specs = (P(None, None, "tiles", "cols"), P())
    body = functools.partial(local, table, tiles, cols)
    return jax.shard_map(body, mesh=mesh, in_specs=in_specs, out_specs=out_specs, check_vma=False)
```

```python
import functools
import math

import jax
import jax.numpy as jnp
import ml_dtypes
import numpy as np
from jax import lax
from jax.experimental import pallas as pl
from jax.experimental.pallas import tpu as pltpu
from jax.sharding import PartitionSpec as P

ITERS = 2
STEP_OBJECT = 0.25
f32, bf16 = jnp.float32, jnp.bfloat16
MESH = pl.DeviceIdType.MESH
VMEM_LIMIT = 56 * 2**20

A_PLUS, A_MINUS, F_PLUS, F_MINUS = 0, 2, 4, 6


def split_table(table):
    high = table.astype(np.float32).astype(ml_dtypes.bfloat16)
    low = (table - high.astype(np.float64)).astype(np.float32).astype(ml_dtypes.bfloat16)
    return [high, low]


def transform_tables(size):
    line = np.arange(size)
    dft = np.exp(-2j * np.pi * (np.outer(line, line) % size) / size) / math.sqrt(size)
    freq = np.where(line < size // 2, line, line - size)
    chirp = np.exp(-2j * np.pi * ((freq * freq) % (4 * size)) / (4 * size))
    propagator = np.conj(dft) @ (chirp[:, None] * dft)
    parts = []
    for matrix in (propagator, dft):
        real, imag = matrix.real, matrix.imag
        plus = np.block([[real, imag], [-imag, real]])
        parts += split_table(plus) + split_table(plus.T)
    return np.stack(parts)


def split(value):
    high = value.astype(bf16)
    return high, (value - high.astype(f32)).astype(bf16)


def product(first, second):
    dot = functools.partial(jnp.dot, preferred_element_type=f32)
    return dot(first[0], second[0]) + (dot(first[1], second[0]) + dot(first[0], second[1]))


def two_sided(fields, table, left, right):
    n = fields[0][0].shape[0]
    modes = range(len(fields))
    stacked = [jnp.concatenate(field, axis=0) for field in fields]
    middle = product((table[left], table[left + 1]), split(jnp.concatenate(stacked, axis=1)))
    columns = [middle[:, n * m : n * m + n] for m in modes]
    beside = [jnp.concatenate([c[:n], c[n:]], axis=1) for c in columns]
    result = product(split(jnp.concatenate(beside, axis=0)), (table[right], table[right + 1]))
    rows = [result[n * m : n * m + n] for m in modes]
    return [(row[:, :n], row[:, n:]) for row in rows]


def times(a, b):
    return (a[0] * b[0] - a[1] * b[1], a[0] * b[1] + a[1] * b[0])


def conj_times(a, b):
    return (a[0] * b[0] + a[1] * b[1], a[0] * b[1] - a[1] * b[0])


def total(terms):
    real, imag = terms[0]
    for term in terms[1:]:
        real, imag = real + term[0], imag + term[1]
    return real, imag


GROUP = 4


def add_gradients(rows, cols, counts, measured, extended, beam, table, grad, grad_beam, slots):
    planes, count_blocks, tall, n = grad.shape
    modes = range(beam.shape[0] // (2 * n))
    part = len(modes) * n
    grad[...] = jnp.zeros_like(grad)
    grad_beam[...] = jnp.zeros_like(grad_beam)
    lane = lax.broadcasted_iota(jnp.int32, (n, n), 1)
    offset = lax.broadcasted_iota(jnp.int32, (tall, n), 0) - lax.broadcasted_iota(
        jnp.int32, (tall, n), 1
    )
    count = counts[0]
    real_rows = [pl.ds(m * n, n) for m in modes]
    imag_rows = [pl.ds(part + m * n, n) for m in modes]

    def visit(step, carry):
        beams = [(beam[a], beam[b]) for a, b in zip(real_rows, imag_rows)]
        spots = []
        for k in range(GROUP):
            slot = step * GROUP + k
            live = slot < count
            row = jnp.where(live, rows[slot], 0)
            col = jnp.where(live, cols[slot], 0)
            block = lax.shift_right_logical(col, 7)
            weight = jnp.where(live, 1.0, 0.0).astype(f32)
            spots.append((slot, weight, row, block, col - block * n))

        def window(plane, spot):
            _, _, row, block, shift = spot
            back = jnp.bitwise_and(n - shift, n - 1)
            near = pltpu.roll(extended[plane, block, pl.ds(row, n), :], back, 1)
            far = pltpu.roll(extended[plane, block + 1, pl.ds(row, n), :], back, 1)
            return jnp.where(lane < n - shift, near, far)

        first = [(window(0, s), window(2, s)) for s in spots]
        spread = [two_sided([times(b, o) for b in beams], table, A_MINUS, A_PLUS) for o in first]
        second = [(window(1, s), window(3, s)) for s in spots]
        far = [
            two_sided([times(o, x) for x in fields], table, F_MINUS, F_PLUS)
            for o, fields in zip(second, spread)
        ]
        residual = []
        for spot, fields in zip(spots, far):
            intensity = sum(y[0] * y[0] + y[1] * y[1] for y in fields)
            residual.append((intensity - measured[spot[0]]) * spot[1])
        back = [
            two_sided([(r * y[0], r * y[1]) for y in fields], table, F_PLUS, F_MINUS)
            for r, fields in zip(residual, far)
        ]
        grad_second = [
            total([conj_times(x, g) for x, g in zip(fields, backs)])
            for fields, backs in zip(spread, back)
        ]
        back = [
            two_sided([conj_times(o, g) for g in backs], table, A_PLUS, A_MINUS)
            for o, backs in zip(second, back)
        ]
        grad_first = [total([conj_times(b, g) for b, g in zip(beams, backs)]) for backs in back]
        for m in modes:
            real, imag = total([conj_times(o, backs[m]) for o, backs in zip(first, back)])
            grad_beam[real_rows[m]] += real
            grad_beam[imag_rows[m]] += imag
        put, pieces = [], [[] for _ in range(count_blocks)]
        for (_, _, row, block, shift), g0, g1 in zip(spots, grad_first, grad_second):
            put += [jnp.where(offset == row, 1.0, 0.0).astype(bf16)] * 2
            kept = lane >= shift
            beside = [[] for _ in range(count_blocks)]
            for value in (g0[0], g1[0], g0[1], g1[1]):
                moved = pltpu.roll(value, shift, 1)
                near, over = jnp.where(kept, moved, 0.0), jnp.where(kept, 0.0, moved)
                for b in range(count_blocks):
                    if b == 0:
                        placed = jnp.where(block == 0, near, 0.0)
                    elif b == count_blocks - 1:
                        placed = jnp.where(block == b - 1, over, 0.0)
                    else:
                        placed = jnp.where(block == b, near, jnp.where(block == b - 1, over, 0.0))
                    beside[b].append(placed)
            for b in range(count_blocks):
                pieces[b] += split(jnp.concatenate(beside[b], axis=1))
        put = jnp.concatenate(put, axis=1)
        for b in range(count_blocks):
            sums = jnp.dot(put, jnp.concatenate(pieces[b], axis=0), preferred_element_type=f32)
            for p in range(planes):
                grad[p, b] += sums[:, p * n : p * n + n]
        return carry

    lax.fori_loop(0, slots // GROUP, visit, 0)


class Place:
    def __init__(self, tiles, cols):
        self.tiles, self.cols = tiles, cols
        self.t, self.c = lax.axis_index("tiles"), lax.axis_index("cols")

    def at(self, down, right):
        return (
            lax.rem(self.t + (down + self.tiles), self.tiles),
            lax.rem(self.c + (right + self.cols), self.cols),
        )


def greet(devices):
    barrier = pltpu.get_barrier_semaphore()
    for device in devices:
        pl.semaphore_signal(barrier, inc=1, device_id=device, device_id_type=MESH)
    pl.semaphore_wait(barrier, len(devices))


class Copies:
    def __init__(self, send, recv):
        self.send, self.recv, self.used, self.started = send, recv, 0, []

    def start(self, source, target, device):
        k = self.used
        self.used += 1
        copy = pltpu.make_async_remote_copy(
            src_ref=source,
            dst_ref=target,
            send_sem=self.send.at[k],
            recv_sem=self.recv.at[k],
            device_id=device,
            device_id_type=MESH,
        )
        copy.start()
        self.started.append(copy)
        return copy

    def sent(self, copy):
        copy.wait_send()
        self.started = [other for other in self.started if other is not copy]

    def finish(self):
        for copy in self.started:
            copy.wait_send()
        self.started = []


class ProbeSum:
    def __init__(self, place, copies, grad, pair, pieces, column, halves):
        self.place, self.copies = place, copies
        self.grad, self.pair, self.pieces, self.column, self.halves = grad, pair, pieces, column, halves
        self.half = grad.shape[0] // 2
        self.piece = self.half // place.tiles
        self.core = lax.rem(place.c, 2)
        self.partner = (place.t, place.c + 1 - 2 * self.core)
        self.mine = pl.ds(self.core * self.half, self.half)
        self.others = pl.ds((1 - self.core) * self.half, self.half)

    def scatter_pair(self):
        self.step = self.copies.start(self.grad.at[self.others], self.pair, self.partner)

    def scatter_tiles(self):
        self.step.wait_recv()
        self.grad[self.mine] += self.pair[...]
        place, piece = self.place, self.piece
        self.steps = []
        for k in range(1, place.tiles):
            peer = lax.rem(place.t + k, place.tiles)
            source = self.grad.at[pl.ds(self.core * self.half + peer * piece, piece)]
            self.steps.append(
                self.copies.start(source, self.pieces.at[k - 1], (peer, place.c))
            )

    def sum_column(self):
        place, piece = self.place, self.piece
        value = self.grad[pl.ds(self.core * self.half + place.t * piece, piece)]
        for k, step in enumerate(self.steps):
            step.wait_recv()
            value += self.pieces[k]
        chips = place.cols // 2
        chip = place.c // 2
        self.column[chip] = value
        self.steps = []
        for k in range(1, chips):
            peer = (place.t, lax.rem(place.c + 2 * k, place.cols))
            self.steps.append(
                self.copies.start(self.column.at[chip], self.column.at[chip], peer)
            )

    def gather_tiles(self):
        for step in self.steps:
            step.wait_recv()
        place, piece = self.place, self.piece
        value = self.column[0]
        for k in range(1, place.cols // 2):
            value += self.column[k]
        own = pl.ds(self.core * self.half + place.t * piece, piece)
        self.halves[own] = value
        self.steps = []
        for k in range(1, place.tiles):
            peer = lax.rem(place.t + k, place.tiles)
            self.steps.append(
                self.copies.start(self.halves.at[own], self.halves.at[own], (peer, place.c))
            )

    def gather_pair(self):
        for step in self.steps:
            step.wait_recv()
        self.step = self.copies.start(
            self.halves.at[self.mine], self.halves.at[self.mine], self.partner
        )

    def result(self):
        self.step.wait_recv()
        return self.halves[...]

    @staticmethod
    def copies_needed(tiles, cols):
        return 2 * tiles + cols // 2 - 1

    @staticmethod
    def scratch(rows, lanes, tiles, cols):
        half = rows // 2
        piece = half // tiles
        return [
            pltpu.VMEM((half, lanes), f32),
            pltpu.VMEM((tiles - 1, piece, lanes), f32),
            pltpu.VMEM((cols // 2, piece, lanes), f32),
            pltpu.VMEM((rows, lanes), f32),
        ]


def met(place):
    devices = [place.at(k, 0) for k in range(1, place.tiles)]
    return devices + [
        place.at(0, k) for k in range(1, place.cols) if k % 2 == 0 or k in (1, place.cols - 1)
    ]


def met(place):
    devices = [place.at(k, 0) for k in range(1, place.tiles)]
    return devices + [
        place.at(0, k) for k in range(1, place.cols) if k % 2 == 0 or k in (1, place.cols - 1)
    ]


def program_kernel(
    tiles,
    cols,
    rows,
    columns,
    counts,
    field,
    probe_hbm,
    measured_hbm,
    table_hbm,
    new_field,
    new_probe,
    extended,
    grad,
    beam,
    grad_beam,
    measured,
    table,
    from_left,
    from_up,
    from_right,
    from_down,
    from_corner,
    *rest,
):
    sums, (local_sem, send, recv) = rest[:-3], rest[-3:]
    sums = [sums[: len(sums) // 2], sums[len(sums) // 2 :]]
    planes, count, tall, size = grad.shape
    last = count - 1
    height = tall - size
    slots = measured.shape[0]
    step_probe = 1.0 / (slots * tiles * cols)
    top, middle, below = pl.ds(0, size), pl.ds(size, height - size), pl.ds(height, size)
    own = pl.ds(0, height)
    block = [pl.ds(j * size, size) for j in range(last)]
    every = range(planes)
    place = Place(tiles, cols)
    copies = Copies(send, recv)
    up, down, left, right = place.at(-1, 0), place.at(1, 0), place.at(0, -1), place.at(0, 1)

    loads = [(field.at[:, :, block[j]], extended.at[:, j, own, :]) for j in range(last)]
    loads += [(probe_hbm, beam), (table_hbm, table), (measured_hbm, measured)]
    loads = [
        pltpu.make_async_copy(source, target, local_sem.at[k])
        for k, (source, target) in enumerate(loads)
    ]
    for load in loads:
        load.start()
    greet(met(place))

    halos = {
        (p, j): copies.start(field.at[p, top, block[j]], extended.at[p, j, below], up)
        for j in range(last)
        for p in every
    }
    sides = [
        copies.start(field.at[p, :, block[0]], extended.at[p, last, own], left) for p in every
    ]
    corners = []
    for p in every:
        halos[p, 0].wait_recv()
        corners.append(
            copies.start(extended.at[p, 0, below], extended.at[p, last, below], left)
        )
    for load in loads:
        load.wait()
    for copy in list(halos.values())[planes:] + sides + corners:
        copy.wait_recv()
    copies.finish()

    for sweep in range(ITERS):
        add_gradients(
            rows, columns, counts, measured, extended, beam, table, grad, grad_beam, slots
        )
        final = sweep == ITERS - 1
        reduce = ProbeSum(place, copies, grad_beam, *sums[sweep])
        reduce.scatter_pair()
        sides = [
            copies.start(grad.at[p, last], from_left.at[sweep, p], right) for p in every
        ]
        ups, downs = {}, {}

        def send_rows(p, j):
            ups[p, j] = copies.start(grad.at[p, j, below], from_up.at[sweep, p, j], down)
            if not final:
                downs[p, j] = copies.start(grad.at[p, j, top], from_down.at[p, j], up)

        for j in range(1, last):
            for p in every:
                send_rows(p, j)
        reduce.scatter_tiles()
        for p in every:
            sides[p].wait_recv()
            grad[p, 0] += from_left[sweep, p]
            send_rows(p, 0)
        if final:
            reduce.sum_column()
            for j in range(last):
                for p in every:
                    new_field[p, :, block[j]] = extended[p, j, own] - STEP_OBJECT * grad[p, j, own]
            reduce.gather_tiles()
            for j in list(range(1, last)) + [0]:
                for p in every:
                    ups[p, j].wait_recv()
                    new_field[p, top, block[j]] -= STEP_OBJECT * from_up[sweep, p, j]
            reduce.gather_pair()
            new_probe[...] = beam[...] - step_probe * reduce.result()
        else:
            middles = [
                copies.start(grad.at[p, 0, middle], from_right.at[p], left) for p in every
            ]
            reduce.sum_column()
            reduce.gather_tiles()
            corners = {}
            for p in every:
                copies.sent(ups[p, 0])
                copies.sent(downs[p, 0])
                for way, landed, lines in ((ups, from_up.at[sweep], top), (downs, from_down, below)):
                    way[p, 0].wait_recv()
                    grad[p, 0, lines] += landed[p, 0]
                for k, lines in enumerate((top, below)):
                    corners[p, k] = copies.start(
                        grad.at[p, 0, lines], from_corner.at[p, k], left
                    )
                extended[p, 0] -= STEP_OBJECT * grad[p, 0]
            reduce.gather_pair()
            for j in range(1, last):
                for p in every:
                    ups[p, j].wait_recv()
                    downs[p, j].wait_recv()
                    extended[p, j, middle] -= STEP_OBJECT * grad[p, j, middle]
                    extended[p, j, top] -= STEP_OBJECT * (grad[p, j, top] + from_up[sweep, p, j])
                    extended[p, j, below] -= STEP_OBJECT * (grad[p, j, below] + from_down[p, j])
            for p in every:
                middles[p].wait_recv()
                extended[p, last, middle] -= STEP_OBJECT * from_right[p]
                for k, lines in enumerate((top, below)):
                    corners[p, k].wait_recv()
                    extended[p, last, lines] -= STEP_OBJECT * from_corner[p, k]
            beam[...] -= step_probe * reduce.result()
        copies.finish()


def local(table, tiles, cols, object_field, probe, row_offsets, col_offsets, counts, measured):
    size = probe.shape[-1]
    height, width = object_field.shape[2:]
    slots = row_offsets.shape[-1]
    field = object_field.reshape(4, height, width)
    flat = (probe.shape[0] * probe.shape[1] * size, size)
    planes, last, tall = 4, width // size, height + size
    needed = planes * (2 * last + 2) + ITERS * ProbeSum.copies_needed(tiles, cols)
    needed += planes * (1 + 2 * last + 1 + 2) + planes * (1 + last)
    work = ITERS * slots * probe.shape[1] * 8 * 3 * 2 * 256 * 256 * 128
    smem = pl.BlockSpec(memory_space=pltpu.SMEM)
    hbm = pl.BlockSpec(memory_space=pl.ANY)
    vmem = pl.BlockSpec(memory_space=pltpu.VMEM)
    new_field, new_probe = pl.pallas_call(
        functools.partial(program_kernel, tiles, cols),
        out_shape=[jax.ShapeDtypeStruct(field.shape, f32), jax.ShapeDtypeStruct(flat, f32)],
        in_specs=[smem] * 3 + [hbm] * 4,
        out_specs=[vmem] * 2,
        scratch_shapes=[
            pltpu.VMEM((planes, last + 1, tall, size), f32),
            pltpu.VMEM((planes, last + 1, tall, size), f32),
            pltpu.VMEM(flat, f32),
            pltpu.VMEM(flat, f32),
            pltpu.VMEM((slots, size, size), f32),
            pltpu.VMEM(table.shape, bf16),
            pltpu.VMEM((ITERS, planes, tall, size), f32),
            pltpu.VMEM((ITERS, planes, last, size, size), f32),
            pltpu.VMEM((planes, height - size, size), f32),
            pltpu.VMEM((planes, last, size, size), f32),
            pltpu.VMEM((planes, 2, size, size), f32),
            *ProbeSum.scratch(*flat, tiles, cols),
            *ProbeSum.scratch(*flat, tiles, cols),
            pltpu.SemaphoreType.DMA((last + 3,)),
            pltpu.SemaphoreType.DMA((needed,)),
            pltpu.SemaphoreType.DMA((needed,)),
        ],
        compiler_params=pltpu.CompilerParams(
            collective_id=0, has_side_effects=True, vmem_limit_bytes=VMEM_LIMIT
        ),
        cost_estimate=pl.CostEstimate(flops=work, bytes_accessed=5 * 2**20, transcendentals=0),
        name="ptychography",
    )(
        row_offsets.reshape(slots),
        col_offsets.reshape(slots),
        counts.reshape(1),
        field,
        probe.reshape(flat),
        measured.reshape(slots, size, size),
        table,
    )
    return new_field.reshape(object_field.shape), new_probe.reshape(probe.shape)


def solution(mesh):
    table = jnp.asarray(transform_tables(128))
    tiles, cols = mesh.shape["tiles"], mesh.shape["cols"]
    in_specs = (
        P(None, None, "tiles", "cols"),
        P(),
        P("tiles", "cols", None),
        P("tiles", "cols", None),
        P("tiles", "cols"),
        P("tiles", "cols", None, None, None),
    )
    out_specs = (P(None, None, "tiles", "cols"), P())
    body = functools.partial(local, table, tiles, cols)
    return jax.shard_map(body, mesh=mesh, in_specs=in_specs, out_specs=out_specs, check_vma=False)
```

```python
import functools
import math

import jax
import jax.numpy as jnp
import ml_dtypes
import numpy as np
from jax import lax
from jax.experimental import pallas as pl
from jax.experimental.pallas import tpu as pltpu
from jax.sharding import PartitionSpec as P

ITERS = 2
STEP_OBJECT = 0.25
f32, bf16 = jnp.float32, jnp.bfloat16
MESH = pl.DeviceIdType.MESH
VMEM_LIMIT = 56 * 2**20

A_PLUS, A_MINUS, F_PLUS, F_MINUS = 0, 2, 4, 6


def split_table(table):
    high = table.astype(np.float32).astype(ml_dtypes.bfloat16)
    low = (table - high.astype(np.float64)).astype(np.float32).astype(ml_dtypes.bfloat16)
    return [high, low]


def transform_tables(size):
    line = np.arange(size)
    dft = np.exp(-2j * np.pi * (np.outer(line, line) % size) / size) / math.sqrt(size)
    freq = np.where(line < size // 2, line, line - size)
    chirp = np.exp(-2j * np.pi * ((freq * freq) % (4 * size)) / (4 * size))
    propagator = np.conj(dft) @ (chirp[:, None] * dft)
    parts = []
    for matrix in (propagator, dft):
        real, imag = matrix.real, matrix.imag
        plus = np.block([[real, imag], [-imag, real]])
        parts += split_table(plus) + split_table(plus.T)
    return np.stack(parts)


def split(value):
    high = value.astype(bf16)
    return high, (value - high.astype(f32)).astype(bf16)


def product(first, second):
    dot = functools.partial(jnp.dot, preferred_element_type=f32)
    return dot(first[0], second[0]) + (dot(first[1], second[0]) + dot(first[0], second[1]))


def two_sided(fields, table, left, right):
    n = fields[0][0].shape[0]
    modes = range(len(fields))
    stacked = [jnp.concatenate(field, axis=0) for field in fields]
    middle = product((table[left], table[left + 1]), split(jnp.concatenate(stacked, axis=1)))
    columns = [middle[:, n * m : n * m + n] for m in modes]
    beside = [jnp.concatenate([c[:n], c[n:]], axis=1) for c in columns]
    result = product(split(jnp.concatenate(beside, axis=0)), (table[right], table[right + 1]))
    rows = [result[n * m : n * m + n] for m in modes]
    return [(row[:, :n], row[:, n:]) for row in rows]


def times(a, b):
    return (a[0] * b[0] - a[1] * b[1], a[0] * b[1] + a[1] * b[0])


def conj_times(a, b):
    return (a[0] * b[0] + a[1] * b[1], a[0] * b[1] - a[1] * b[0])


def total(terms):
    real, imag = terms[0]
    for term in terms[1:]:
        real, imag = real + term[0], imag + term[1]
    return real, imag


GROUP = 4


class Positions:
    def __init__(self, refs, n, slots):
        self.rows, self.cols, self.counts, self.measured = refs[:4]
        self.extended, self.beam, self.table, self.grad, self.grad_beam = refs[4:9]
        self.windows, self.spread, self.back, self.patches = refs[9:]
        self.n, self.slots = n, slots
        self.modes = range(self.spread.shape[1])
        self.groups = slots // GROUP

    def beams(self):
        n, part = self.n, len(self.modes) * self.n
        return [(self.beam[pl.ds(m * n, n)], self.beam[pl.ds(part + m * n, n)]) for m in self.modes]

    def spots(self, step):
        found = []
        for k in range(GROUP):
            slot = step * GROUP + k
            live = slot < self.counts[0]
            row = jnp.where(live, self.rows[slot], 0)
            col = jnp.where(live, self.cols[slot], 0)
            block = lax.shift_right_logical(col, 7)
            weight = jnp.where(live, 1.0, 0.0).astype(f32)
            found.append((slot, weight, row, block, col - block * self.n))
        return found

    def lane(self):
        return lax.broadcasted_iota(jnp.int32, (self.n, self.n), 1)

    def window(self, plane, spot):
        n = self.n
        _, _, row, block, shift = spot
        back = jnp.bitwise_and(n - shift, n - 1)
        near = pltpu.roll(self.extended[plane % 2][plane // 2, block, pl.ds(row, n), :], back, 1)
        far = pltpu.roll(self.extended[plane % 2][plane // 2, block + 1, pl.ds(row, n), :], back, 1)
        return jnp.where(self.lane() < n - shift, near, far)

    def propagate(self, step):
        spots, beams = self.spots(step), self.beams()
        first = [(self.window(0, s), self.window(2, s)) for s in spots]
        for spot, field in zip(spots, first):
            self.windows[spot[0], 0], self.windows[spot[0], 1] = field
            result = two_sided([times(b, field) for b in beams], self.table, A_MINUS, A_PLUS)
            for m in self.modes:
                self.spread[spot[0], m, 0], self.spread[spot[0], m, 1] = result[m]

    def diffract(self, step):
        spots = self.spots(step)
        spread = [
            [(self.spread[s[0], m, 0], self.spread[s[0], m, 1]) for m in self.modes] for s in spots
        ]
        second = [(self.window(1, s), self.window(3, s)) for s in spots]
        far = [
            two_sided([times(o, x) for x in fields], self.table, F_MINUS, F_PLUS)
            for o, fields in zip(second, spread)
        ]
        residual = []
        for spot, fields in zip(spots, far):
            intensity = sum(y[0] * y[0] + y[1] * y[1] for y in fields)
            residual.append((intensity - self.measured[spot[0]]) * spot[1])
        back = [
            two_sided([(r * y[0], r * y[1]) for y in fields], self.table, F_PLUS, F_MINUS)
            for r, fields in zip(residual, far)
        ]
        patches = [
            total([conj_times(x, g) for x, g in zip(fields, backs)])
            for fields, backs in zip(spread, back)
        ]
        for spot, o, backs in zip(spots, second, back):
            for m in self.modes:
                self.back[spot[0], m, 0], self.back[spot[0], m, 1] = conj_times(o, backs[m])
        self.put(spots, patches, (1, 3), False)

    def return_back(self, step):
        spots, beams = self.spots(step), self.beams()
        n, part = self.n, len(self.modes) * self.n
        back = []
        for spot in spots:
            fields = [(self.back[spot[0], m, 0], self.back[spot[0], m, 1]) for m in self.modes]
            back.append(two_sided(fields, self.table, A_PLUS, A_MINUS))
        first = [(self.windows[s[0], 0], self.windows[s[0], 1]) for s in spots]
        for m in self.modes:
            terms = total([conj_times(o, backs[m]) for o, backs in zip(first, back)])
            for term, start in zip(terms, (m * n, part + m * n)):
                if step == 0:
                    self.grad_beam[pl.ds(start, n)] = term
                else:
                    self.grad_beam[pl.ds(start, n)] += term
        for spot, backs in zip(spots, back):
            patch = total([conj_times(b, g) for b, g in zip(beams, backs)])
            self.patches[spot[0], 0], self.patches[spot[0], 1] = patch

    def put_first(self, step):
        spots = self.spots(step)
        patches = [(self.patches[s[0], 0], self.patches[s[0], 1]) for s in spots]
        self.put(spots, patches, (0, 2), step == 0)

    def clear(self, planes):
        for p in planes:
            self.grad[p] = jnp.zeros(self.grad.shape[1:], f32)

    def put(self, spots, patches, planes, fresh):
        n = self.n
        count, tall = self.grad.shape[1:3]
        offset = lax.broadcasted_iota(jnp.int32, (tall, n), 0) - lax.broadcasted_iota(
            jnp.int32, (tall, n), 1
        )
        ones, pieces = [], [[] for _ in range(count)]
        for (_, _, row, block, shift), patch in zip(spots, patches):
            ones += [jnp.where(offset == row, 1.0, 0.0).astype(bf16)] * 2
            kept = self.lane() >= shift
            beside = [[] for _ in range(count)]
            for value in patch:
                moved = pltpu.roll(value, shift, 1)
                near, over = jnp.where(kept, moved, 0.0), jnp.where(kept, 0.0, moved)
                for b in range(count):
                    if b == 0:
                        placed = jnp.where(block == 0, near, 0.0)
                    elif b == count - 1:
                        placed = jnp.where(block == b - 1, over, 0.0)
                    else:
                        placed = jnp.where(block == b, near, jnp.where(block == b - 1, over, 0.0))
                    beside[b].append(placed)
            for b in range(count):
                pieces[b] += split(jnp.concatenate(beside[b], axis=1))
        ones = jnp.concatenate(ones, axis=1)
        for b in range(count):
            sums = jnp.dot(ones, jnp.concatenate(pieces[b], axis=0), preferred_element_type=f32)
            for k, p in enumerate(planes):
                if fresh:
                    self.grad[p, b] = sums[:, k * n : k * n + n]
                else:
                    self.grad[p, b] += sums[:, k * n : k * n + n]


class Place:
    def __init__(self, tiles, cols):
        self.tiles, self.cols = tiles, cols
        self.t, self.c = lax.axis_index("tiles"), lax.axis_index("cols")

    def at(self, down, right):
        return (
            lax.rem(self.t + (down + self.tiles), self.tiles),
            lax.rem(self.c + (right + self.cols), self.cols),
        )


def greet(devices):
    barrier = pltpu.get_barrier_semaphore()
    for device in devices:
        pl.semaphore_signal(barrier, inc=1, device_id=device, device_id_type=MESH)
    pl.semaphore_wait(barrier, len(devices))


class Copies:
    def __init__(self, send, recv):
        self.send, self.recv, self.used, self.started = send, recv, 0, []

    def start(self, source, target, device):
        k = self.used
        self.used += 1
        copy = pltpu.make_async_remote_copy(
            src_ref=source,
            dst_ref=target,
            send_sem=self.send.at[k],
            recv_sem=self.recv.at[k],
            device_id=device,
            device_id_type=MESH,
        )
        copy.start()
        self.started.append(copy)
        return copy

    def sent(self, copy):
        copy.wait_send()
        self.started = [other for other in self.started if other is not copy]

    def finish(self):
        for copy in self.started:
            copy.wait_send()
        self.started = []


class ProbeSum:
    def __init__(self, place, copies, grad, pair, pieces, column, halves):
        self.place, self.copies = place, copies
        self.grad, self.pair, self.pieces, self.column, self.halves = grad, pair, pieces, column, halves
        self.half = grad.shape[0] // 2
        self.piece = self.half // place.tiles
        self.core = lax.rem(place.c, 2)
        self.partner = (place.t, place.c + 1 - 2 * self.core)
        self.mine = pl.ds(self.core * self.half, self.half)
        self.others = pl.ds((1 - self.core) * self.half, self.half)

    def scatter_pair(self):
        self.step = self.copies.start(self.grad.at[self.others], self.pair, self.partner)

    def scatter_tiles(self):
        self.step.wait_recv()
        self.grad[self.mine] += self.pair[...]
        place, piece = self.place, self.piece
        self.steps = []
        for k in range(1, place.tiles):
            peer = lax.rem(place.t + k, place.tiles)
            source = self.grad.at[pl.ds(self.core * self.half + peer * piece, piece)]
            self.steps.append(
                self.copies.start(source, self.pieces.at[k - 1], (peer, place.c))
            )

    def sum_column(self):
        place, piece = self.place, self.piece
        value = self.grad[pl.ds(self.core * self.half + place.t * piece, piece)]
        for k, step in enumerate(self.steps):
            step.wait_recv()
            value += self.pieces[k]
        chips = place.cols // 2
        chip = place.c // 2
        self.column[chip] = value
        self.steps = []
        for k in range(1, chips):
            peer = (place.t, lax.rem(place.c + 2 * k, place.cols))
            self.steps.append(
                self.copies.start(self.column.at[chip], self.column.at[chip], peer)
            )

    def gather_tiles(self):
        for step in self.steps:
            step.wait_recv()
        place, piece = self.place, self.piece
        value = self.column[0]
        for k in range(1, place.cols // 2):
            value += self.column[k]
        own = pl.ds(self.core * self.half + place.t * piece, piece)
        self.halves[own] = value
        self.steps = []
        for k in range(1, place.tiles):
            peer = lax.rem(place.t + k, place.tiles)
            self.steps.append(
                self.copies.start(self.halves.at[own], self.halves.at[own], (peer, place.c))
            )

    def gather_pair(self):
        for step in self.steps:
            step.wait_recv()
        self.step = self.copies.start(
            self.halves.at[self.mine], self.halves.at[self.mine], self.partner
        )

    def result(self):
        self.step.wait_recv()
        return self.halves[...]

    @staticmethod
    def copies_needed(tiles, cols):
        return 2 * tiles + cols // 2 - 1

    @staticmethod
    def scratch(rows, lanes, tiles, cols):
        half = rows // 2
        piece = half // tiles
        return [
            pltpu.VMEM((half, lanes), f32),
            pltpu.VMEM((tiles - 1, piece, lanes), f32),
            pltpu.VMEM((cols // 2, piece, lanes), f32),
            pltpu.VMEM((rows, lanes), f32),
        ]


def met(place):
    devices = [place.at(k, 0) for k in range(1, place.tiles)]
    return devices + [
        place.at(0, k) for k in range(1, place.cols) if k % 2 == 0 or k in (1, place.cols - 1)
    ]


def met(place):
    devices = [place.at(k, 0) for k in range(1, place.tiles)]
    return devices + [
        place.at(0, k) for k in range(1, place.cols) if k % 2 == 0 or k in (1, place.cols - 1)
    ]


class Overlap:
    def __init__(self, place, copies, planes, grad, extended, buffers, final):
        self.place, self.copies, self.planes, self.final = place, copies, planes, final
        self.grad, self.extended = grad, extended
        self.from_left, self.from_up, self.from_right, self.from_down, self.from_corner = buffers
        count, tall, size = grad.shape[1:]
        self.last, height = count - 1, tall - size
        self.top, self.middle = pl.ds(0, size), pl.ds(size, height - size)
        self.below, self.own = pl.ds(height, size), pl.ds(0, height)
        self.block = [pl.ds(j * size, size) for j in range(self.last)]
        self.ups, self.downs = {}, {}

    def rows(self, j):
        up, down = self.place.at(-1, 0), self.place.at(1, 0)
        for p in self.planes:
            self.ups[p, j] = self.copies.start(
                self.grad.at[p, j, self.below], self.from_up.at[p, j], down
            )
            if not self.final:
                self.downs[p, j] = self.copies.start(
                    self.grad.at[p, j, self.top], self.from_down.at[p, j], up
                )

    def start(self):
        right = self.place.at(0, 1)
        self.sides = [
            self.copies.start(self.grad.at[p, self.last], self.from_left.at[p], right)
            for p in self.planes
        ]
        for j in range(1, self.last):
            self.rows(j)

    def first(self):
        for p, side in zip(self.planes, self.sides):
            side.wait_recv()
            self.grad[p, 0] += self.from_left[p]
        self.rows(0)
        if not self.final:
            left = self.place.at(0, -1)
            self.middles = [
                self.copies.start(self.grad.at[p, 0, self.middle], self.from_right.at[p], left)
                for p in self.planes
            ]

    def corner(self):
        left = self.place.at(0, -1)
        self.corners = {}
        for p in self.planes:
            self.copies.sent(self.ups[p, 0])
            self.copies.sent(self.downs[p, 0])
            self.ups[p, 0].wait_recv()
            self.grad[p, 0, self.top] += self.from_up[p, 0]
            self.downs[p, 0].wait_recv()
            self.grad[p, 0, self.below] += self.from_down[p, 0]
            for k, lines in enumerate((self.top, self.below)):
                self.corners[p, k] = self.copies.start(
                    self.grad.at[p, 0, lines], self.from_corner.at[p, k], left
                )

    def update(self):
        grad, extended, last = self.grad, self.extended, self.last
        top, middle, below = self.top, self.middle, self.below
        for p in self.planes:
            extended[p % 2][p // 2, 0] -= STEP_OBJECT * grad[p, 0]
        for j in range(1, last):
            for p in self.planes:
                self.ups[p, j].wait_recv()
                self.downs[p, j].wait_recv()
                extended[p % 2][p // 2, j, middle] -= STEP_OBJECT * grad[p, j, middle]
                extended[p % 2][p // 2, j, top] -= STEP_OBJECT * (grad[p, j, top] + self.from_up[p, j])
                extended[p % 2][p // 2, j, below] -= STEP_OBJECT * (grad[p, j, below] + self.from_down[p, j])
        for p, copy in zip(self.planes, self.middles):
            copy.wait_recv()
            extended[p % 2][p // 2, last, middle] -= STEP_OBJECT * self.from_right[p]
            for k, lines in enumerate((top, below)):
                self.corners[p, k].wait_recv()
                extended[p % 2][p // 2, last, lines] -= STEP_OBJECT * self.from_corner[p, k]

    def keep(self, new_field):
        for j in range(self.last):
            for p in self.planes:
                new_field[p, :, self.block[j]] = (
                    self.extended[p % 2][p // 2, j, self.own] - STEP_OBJECT * self.grad[p, j, self.own]
                )

    def complete(self, new_field):
        for j in list(range(1, self.last)) + [0]:
            for p in self.planes:
                self.ups[p, j].wait_recv()
                new_field[p, self.top, self.block[j]] -= STEP_OBJECT * self.from_up[p, j]


SLICE_PLANES = ((0, 2), (1, 3))


def program_kernel(
    tiles,
    cols,
    rows,
    columns,
    counts,
    field,
    probe_hbm,
    measured_hbm,
    table_hbm,
    new_field,
    new_probe,
    object_first,
    object_second,
    grad,
    beam,
    grad_beam,
    measured,
    table,
    windows,
    spread,
    back,
    patches,
    from_left,
    from_up,
    from_right,
    from_down,
    from_corner,
    *rest,
):
    sums, (local_sem, send, recv) = rest[:-3], rest[-3:]
    sums = [sums[: len(sums) // 2], sums[len(sums) // 2 :]]
    extended = (object_first, object_second)
    planes, count, tall, size = grad.shape
    last = count - 1
    height = tall - size
    slots = measured.shape[0]
    step_probe = 1.0 / (slots * tiles * cols)
    top, below, own = pl.ds(0, size), pl.ds(height, size), pl.ds(0, height)
    block = [pl.ds(j * size, size) for j in range(last)]
    place = Place(tiles, cols)
    copies = Copies(send, recv)
    up, left = place.at(-1, 0), place.at(0, -1)

    loads = [
        (field.at[p, :, block[j]], extended[p % 2].at[p // 2, j, own])
        for p in range(planes)
        for j in range(last)
    ]
    loads += [(probe_hbm, beam), (table_hbm, table), (measured_hbm, measured)]
    loads = [
        pltpu.make_async_copy(source, target, local_sem.at[k])
        for k, (source, target) in enumerate(loads)
    ]
    for load in loads:
        load.start()
    greet(met(place))

    halos, sides, corners = {}, {}, {}

    def send_halo(p, j):
        halos[p, j] = copies.start(
            field.at[p, top, block[j]], extended[p % 2].at[p // 2, j, below], up
        )

    def pass_corners(which):
        for p in SLICE_PLANES[which]:
            halos[p, 0].wait_recv()
            corners[p] = copies.start(
                extended[p % 2].at[p // 2, 0, below], extended[p % 2].at[p // 2, last, below], left
            )

    def take_halo(which):
        for p in SLICE_PLANES[which]:
            for copy in [halos[p, j] for j in range(1, last)] + [sides[p], corners[p]]:
                copy.wait_recv()

    for which in SLICE_PLANES:
        for p in which:
            send_halo(p, 0)
        for p in which:
            sides[p] = copies.start(
                field.at[p, :, block[0]], extended[p % 2].at[p // 2, last, own], left
            )
        for j in range(1, last):
            for p in which:
                send_halo(p, j)
    pass_corners(0)
    for load in loads:
        load.wait()
    take_halo(0)

    refs = (rows, columns, counts, measured, extended, beam, table, grad, grad_beam)
    work = Positions(refs + (windows, spread, back, patches), size, slots)
    waiting = None
    for sweep in range(ITERS):
        final = sweep == ITERS - 1
        landed = (from_left.at[sweep], from_up.at[sweep], from_right, from_down, from_corner)
        zeroth, first = [
            Overlap(place, copies, which, grad, extended, landed, final) for which in SLICE_PLANES
        ]
        for step in range(work.groups):
            work.propagate(step)
            if step == 0 and sweep == 0:
                pass_corners(1)
        if sweep == 0:
            take_halo(1)
        else:
            waiting.update()
        copies.finish()
        work.clear(SLICE_PLANES[1])
        lax.fori_loop(0, work.groups, lambda step, carry: (work.diffract(step), carry)[1], 0)
        first.start()
        for step in range(work.groups):
            work.return_back(step)
            if step == 0:
                first.first()
        reduce = ProbeSum(place, copies, grad_beam, *sums[sweep])
        reduce.scatter_pair()
        for step in range(work.groups):
            work.put_first(step)
            if step == 0:
                reduce.scatter_tiles()
        zeroth.start()
        if final:
            zeroth.first()
            reduce.sum_column()
            first.keep(new_field)
            zeroth.keep(new_field)
            reduce.gather_tiles()
            first.complete(new_field)
            zeroth.complete(new_field)
            reduce.gather_pair()
            new_probe[...] = beam[...] - step_probe * reduce.result()
            copies.finish()
        else:
            first.corner()
            zeroth.first()
            reduce.sum_column()
            reduce.gather_tiles()
            zeroth.corner()
            reduce.gather_pair()
            zeroth.update()
            beam[...] -= step_probe * reduce.result()
            waiting = first


def local(table, tiles, cols, object_field, probe, row_offsets, col_offsets, counts, measured):
    size = probe.shape[-1]
    height, width = object_field.shape[2:]
    slots = row_offsets.shape[-1]
    field = object_field.reshape(4, height, width)
    flat = (probe.shape[0] * probe.shape[1] * size, size)
    planes, last, tall = 4, width // size, height + size
    needed = planes * (2 * last + 2) + ITERS * ProbeSum.copies_needed(tiles, cols)
    needed += planes * (1 + 2 * last + 1 + 2) + planes * (1 + last)
    work = ITERS * slots * probe.shape[1] * 8 * 3 * 2 * 256 * 256 * 128
    smem = pl.BlockSpec(memory_space=pltpu.SMEM)
    hbm = pl.BlockSpec(memory_space=pl.ANY)
    vmem = pl.BlockSpec(memory_space=pltpu.VMEM)
    new_field, new_probe = pl.pallas_call(
        functools.partial(program_kernel, tiles, cols),
        out_shape=[jax.ShapeDtypeStruct(field.shape, f32), jax.ShapeDtypeStruct(flat, f32)],
        in_specs=[smem] * 3 + [hbm] * 4,
        out_specs=[vmem] * 2,
        scratch_shapes=[
            pltpu.VMEM((planes // 2, last + 1, tall, size), f32),
            pltpu.VMEM((planes // 2, last + 1, tall, size), f32),
            pltpu.VMEM((planes, last + 1, tall, size), f32),
            pltpu.VMEM(flat, f32),
            pltpu.VMEM(flat, f32),
            pltpu.VMEM((slots, size, size), f32),
            pltpu.VMEM(table.shape, bf16),
            pltpu.VMEM((slots, 2, size, size), f32),
            pltpu.VMEM((slots, probe.shape[1], 2, size, size), f32),
            pltpu.VMEM((slots, probe.shape[1], 2, size, size), f32),
            pltpu.VMEM((slots, 2, size, size), f32),
            pltpu.VMEM((ITERS, planes, tall, size), f32),
            pltpu.VMEM((ITERS, planes, last, size, size), f32),
            pltpu.VMEM((planes, height - size, size), f32),
            pltpu.VMEM((planes, last, size, size), f32),
            pltpu.VMEM((planes, 2, size, size), f32),
            *ProbeSum.scratch(*flat, tiles, cols),
            *ProbeSum.scratch(*flat, tiles, cols),
            pltpu.SemaphoreType.DMA((planes * last + 3,)),
            pltpu.SemaphoreType.DMA((needed,)),
            pltpu.SemaphoreType.DMA((needed,)),
        ],
        compiler_params=pltpu.CompilerParams(
            collective_id=0, has_side_effects=True, vmem_limit_bytes=VMEM_LIMIT
        ),
        cost_estimate=pl.CostEstimate(flops=work, bytes_accessed=5 * 2**20, transcendentals=0),
        name="ptychography",
    )(
        row_offsets.reshape(slots),
        col_offsets.reshape(slots),
        counts.reshape(1),
        field,
        probe.reshape(flat),
        measured.reshape(slots, size, size),
        table,
    )
    return new_field.reshape(object_field.shape), new_probe.reshape(probe.shape)


def solution(mesh):
    table = jnp.asarray(transform_tables(128))
    tiles, cols = mesh.shape["tiles"], mesh.shape["cols"]
    in_specs = (
        P(None, None, "tiles", "cols"),
        P(),
        P("tiles", "cols", None),
        P("tiles", "cols", None),
        P("tiles", "cols"),
        P("tiles", "cols", None, None, None),
    )
    out_specs = (P(None, None, "tiles", "cols"), P())
    body = functools.partial(local, table, tiles, cols)
    return jax.shard_map(body, mesh=mesh, in_specs=in_specs, out_specs=out_specs, check_vma=False)
```

```python
import functools
import math

import jax
import jax.numpy as jnp
import ml_dtypes
import numpy as np
from jax import lax
from jax.experimental import pallas as pl
from jax.experimental.pallas import tpu as pltpu
from jax.sharding import PartitionSpec as P

ITERS = 2
STEP_OBJECT = 0.25
f32, bf16 = jnp.float32, jnp.bfloat16
MESH = pl.DeviceIdType.MESH
VMEM_LIMIT = 56 * 2**20

A_PLUS, A_MINUS, F_PLUS, F_MINUS = 0, 2, 4, 6


def split_table(table):
    high = table.astype(np.float32).astype(ml_dtypes.bfloat16)
    low = (table - high.astype(np.float64)).astype(np.float32).astype(ml_dtypes.bfloat16)
    return [high, low]


def transform_tables(size):
    line = np.arange(size)
    dft = np.exp(-2j * np.pi * (np.outer(line, line) % size) / size) / math.sqrt(size)
    freq = np.where(line < size // 2, line, line - size)
    chirp = np.exp(-2j * np.pi * ((freq * freq) % (4 * size)) / (4 * size))
    propagator = np.conj(dft) @ (chirp[:, None] * dft)
    parts = []
    for matrix in (propagator, dft):
        real, imag = matrix.real, matrix.imag
        plus = np.block([[real, imag], [-imag, real]])
        parts += split_table(plus) + split_table(plus.T)
    return np.stack(parts)


def split(value):
    high = value.astype(bf16)
    return high, (value - high.astype(f32)).astype(bf16)


def product(first, second):
    dot = functools.partial(jnp.dot, preferred_element_type=f32)
    return dot(first[0], second[0]) + (dot(first[1], second[0]) + dot(first[0], second[1]))


def two_sided(fields, table, left, right):
    n = fields[0][0].shape[0]
    modes = range(len(fields))
    stacked = [jnp.concatenate(field, axis=0) for field in fields]
    middle = product((table[left], table[left + 1]), split(jnp.concatenate(stacked, axis=1)))
    columns = [middle[:, n * m : n * m + n] for m in modes]
    beside = [jnp.concatenate([c[:n], c[n:]], axis=1) for c in columns]
    result = product(split(jnp.concatenate(beside, axis=0)), (table[right], table[right + 1]))
    rows = [result[n * m : n * m + n] for m in modes]
    return [(row[:, :n], row[:, n:]) for row in rows]


def times(a, b):
    return (a[0] * b[0] - a[1] * b[1], a[0] * b[1] + a[1] * b[0])


def conj_times(a, b):
    return (a[0] * b[0] + a[1] * b[1], a[0] * b[1] - a[1] * b[0])


def total(terms):
    real, imag = terms[0]
    for term in terms[1:]:
        real, imag = real + term[0], imag + term[1]
    return real, imag


GROUP = 4
LINE = 4


class Positions:
    def __init__(self, refs, n, slots):
        self.rows, self.cols, self.counts, self.measured = refs[:4]
        self.extended, self.beam, self.table, self.grad, self.grad_beam = refs[4:9]
        self.windows, self.spread, self.back, self.patches = refs[9:]
        self.n, self.slots = n, slots
        self.modes = range(self.spread.shape[1])
        self.groups = slots // GROUP

    def beams(self):
        n, part = self.n, len(self.modes) * self.n
        return [(self.beam[pl.ds(m * n, n)], self.beam[pl.ds(part + m * n, n)]) for m in self.modes]

    def spots(self, step):
        found = []
        for k in range(GROUP):
            slot = step * GROUP + k
            live = slot < self.counts[0]
            row = jnp.where(live, self.rows[slot], 0)
            col = jnp.where(live, self.cols[slot], 0)
            block = lax.shift_right_logical(col, 7)
            weight = jnp.where(live, 1.0, 0.0).astype(f32)
            found.append((slot, weight, row, block, col - block * self.n))
        return found

    def lane(self):
        return lax.broadcasted_iota(jnp.int32, (self.n, self.n), 1)

    def window(self, plane, spot):
        n = self.n
        _, _, row, block, shift = spot
        back = jnp.bitwise_and(n - shift, n - 1)
        near = pltpu.roll(self.extended[plane % 2][plane // 2, block, pl.ds(row, n), :], back, 1)
        far = pltpu.roll(self.extended[plane % 2][plane // 2, block + 1, pl.ds(row, n), :], back, 1)
        return jnp.where(self.lane() < n - shift, near, far)

    def propagate(self, step):
        spots, beams = self.spots(step), self.beams()
        first = [(self.window(0, s), self.window(2, s)) for s in spots]
        for spot, field in zip(spots, first):
            self.windows[spot[0], 0], self.windows[spot[0], 1] = field
            result = two_sided([times(b, field) for b in beams], self.table, A_MINUS, A_PLUS)
            for m in self.modes:
                self.spread[spot[0], m, 0], self.spread[spot[0], m, 1] = result[m]

    def diffract(self, step):
        spots = self.spots(step)
        spread = [
            [(self.spread[s[0], m, 0], self.spread[s[0], m, 1]) for m in self.modes] for s in spots
        ]
        second = [(self.window(1, s), self.window(3, s)) for s in spots]
        far = [
            two_sided([times(o, x) for x in fields], self.table, F_MINUS, F_PLUS)
            for o, fields in zip(second, spread)
        ]
        residual = []
        for spot, fields in zip(spots, far):
            intensity = sum(y[0] * y[0] + y[1] * y[1] for y in fields)
            residual.append((intensity - self.measured[spot[0]]) * spot[1])
        back = [
            two_sided([(r * y[0], r * y[1]) for y in fields], self.table, F_PLUS, F_MINUS)
            for r, fields in zip(residual, far)
        ]
        patches = [
            total([conj_times(x, g) for x, g in zip(fields, backs)])
            for fields, backs in zip(spread, back)
        ]
        for spot, o, backs in zip(spots, second, back):
            for m in self.modes:
                self.back[spot[0], m, 0], self.back[spot[0], m, 1] = conj_times(o, backs[m])
        for spot, patch in zip(spots, patches):
            self.patches[spot[0], 1], self.patches[spot[0], 3] = patch

    def return_back(self, step):
        spots, beams = self.spots(step), self.beams()
        n, part = self.n, len(self.modes) * self.n
        back = []
        for spot in spots:
            fields = [(self.back[spot[0], m, 0], self.back[spot[0], m, 1]) for m in self.modes]
            back.append(two_sided(fields, self.table, A_PLUS, A_MINUS))
        first = [(self.windows[s[0], 0], self.windows[s[0], 1]) for s in spots]
        for m in self.modes:
            terms = total([conj_times(o, backs[m]) for o, backs in zip(first, back)])
            for term, start in zip(terms, (m * n, part + m * n)):
                if step == 0:
                    self.grad_beam[pl.ds(start, n)] = term
                else:
                    self.grad_beam[pl.ds(start, n)] += term
        for spot, backs in zip(spots, back):
            patch = total([conj_times(b, g) for b, g in zip(beams, backs)])
            self.patches[spot[0], 0], self.patches[spot[0], 2] = patch

    def place_patches(self, step, planes):
        spots = self.spots(step)
        patches = [[self.patches[s[0], p] for p in planes] for s in spots]
        self.put(spots, patches, planes, step == 0)

    def put(self, spots, patches, planes, fresh):
        n = self.n
        count, tall = self.grad.shape[1:3]
        offset = lax.broadcasted_iota(jnp.int32, (tall, n), 0) - lax.broadcasted_iota(
            jnp.int32, (tall, n), 1
        )
        ones, pieces = [], [[] for _ in range(count)]
        for (_, _, row, block, shift), patch in zip(spots, patches):
            ones += [jnp.where(offset == row, 1.0, 0.0).astype(bf16)] * 2
            kept = self.lane() >= shift
            beside = [[] for _ in range(count)]
            for value in patch:
                moved = pltpu.roll(value, shift, 1)
                near, over = jnp.where(kept, moved, 0.0), jnp.where(kept, 0.0, moved)
                for b in range(count):
                    if b == 0:
                        placed = jnp.where(block == 0, near, 0.0)
                    elif b == count - 1:
                        placed = jnp.where(block == b - 1, over, 0.0)
                    else:
                        placed = jnp.where(block == b, near, jnp.where(block == b - 1, over, 0.0))
                    beside[b].append(placed)
            for b in range(count):
                pieces[b] += split(jnp.concatenate(beside[b], axis=1))
        ones = jnp.concatenate(ones, axis=1)
        for b in range(count):
            sums = jnp.dot(ones, jnp.concatenate(pieces[b], axis=0), preferred_element_type=f32)
            for k, p in enumerate(planes):
                if fresh:
                    self.grad[p, b] = sums[:, k * n : k * n + n]
                else:
                    self.grad[p, b] += sums[:, k * n : k * n + n]


class Place:
    def __init__(self, tiles, cols):
        self.tiles, self.cols = tiles, cols
        self.t, self.c = lax.axis_index("tiles"), lax.axis_index("cols")

    def at(self, down, right):
        return (
            lax.rem(self.t + (down + self.tiles), self.tiles),
            lax.rem(self.c + (right + self.cols), self.cols),
        )


def greet(devices):
    barrier = pltpu.get_barrier_semaphore()
    for device in devices:
        pl.semaphore_signal(barrier, inc=1, device_id=device, device_id_type=MESH)
    pl.semaphore_wait(barrier, len(devices))


class Copies:
    def __init__(self, send, recv):
        self.send, self.recv, self.used, self.started = send, recv, 0, []

    def start(self, source, target, device):
        k = self.used
        self.used += 1
        copy = pltpu.make_async_remote_copy(
            src_ref=source,
            dst_ref=target,
            send_sem=self.send.at[k],
            recv_sem=self.recv.at[k],
            device_id=device,
            device_id_type=MESH,
        )
        copy.start()
        self.started.append(copy)
        return copy

    def sent(self, copy):
        copy.wait_send()
        self.started = [other for other in self.started if other is not copy]

    def finish(self):
        for copy in self.started:
            copy.wait_send()
        self.started = []


class ProbeSum:
    def __init__(self, place, copies, grad, pair, pieces, column, halves):
        self.place, self.copies = place, copies
        self.grad, self.pair, self.pieces, self.column, self.halves = grad, pair, pieces, column, halves
        self.half = grad.shape[0] // 2
        self.piece = self.half // (pieces.shape[0] + 1)
        self.core = lax.rem(place.c, 2)
        self.partner = (place.t, place.c + 1 - 2 * self.core)
        self.mine = pl.ds(self.core * self.half, self.half)
        self.others = pl.ds((1 - self.core) * self.half, self.half)

    @staticmethod
    def plane(place):
        found = []
        chips = place.cols // 2
        for k in range(1, place.tiles // LINE * chips):
            t, c = place.at(k // chips * LINE, 2 * (k % chips))
            found.append((t // LINE * chips + c // 2, (t, c)))
        return found

    @staticmethod
    def line(place):
        start = place.t // LINE * LINE
        return [(start + lax.rem(place.t + k, LINE), place.c) for k in range(1, LINE)]

    def part(self, number):
        return pl.ds(self.core * self.half + number * self.piece, self.piece)

    def number(self):
        return self.place.t // LINE * (self.place.cols // 2) + self.place.c // 2

    def scatter_pair(self):
        self.step = self.copies.start(self.grad.at[self.others], self.pair, self.partner)

    def scatter_plane(self):
        self.step.wait_recv()
        self.grad[self.mine] += self.pair[...]
        self.steps = [
            self.copies.start(self.grad.at[self.part(number)], self.pieces.at[k], device)
            for k, (number, device) in enumerate(self.plane(self.place))
        ]

    def sum_line(self):
        value = self.grad[self.part(self.number())]
        for k, step in enumerate(self.steps):
            step.wait_recv()
            value += self.pieces[k]
        spot = lax.rem(self.place.t, LINE)
        self.column[spot] = value
        self.steps = [
            self.copies.start(self.column.at[spot], self.column.at[spot], device)
            for device in self.line(self.place)
        ]

    def gather_plane(self):
        for step in self.steps:
            step.wait_recv()
        value = self.column[0]
        for k in range(1, LINE):
            value += self.column[k]
        own = self.part(self.number())
        self.halves[own] = value
        self.steps = [
            self.copies.start(self.halves.at[own], self.halves.at[own], device)
            for _, device in self.plane(self.place)
        ]

    def gather_pair(self):
        for step in self.steps:
            step.wait_recv()
        self.step = self.copies.start(
            self.halves.at[self.mine], self.halves.at[self.mine], self.partner
        )

    def result(self):
        self.step.wait_recv()
        return self.halves[...]

    @staticmethod
    def copies_needed(tiles, cols):
        return tiles * cols // (2 * LINE) * 2 + LINE - 1

    @staticmethod
    def scratch(rows, lanes, tiles, cols):
        half = rows // 2
        parts = tiles * cols // (2 * LINE)
        piece = half // parts
        return [
            pltpu.VMEM((half, lanes), f32),
            pltpu.VMEM((parts - 1, piece, lanes), f32),
            pltpu.VMEM((LINE, piece, lanes), f32),
            pltpu.VMEM((rows, lanes), f32),
        ]


def met(place):
    sides = [place.at(*way) for way in ((-1, 0), (1, 0), (0, -1), (0, 1))]
    return [device for _, device in ProbeSum.plane(place)] + ProbeSum.line(place) + sides


class Overlap:
    def __init__(self, place, copies, planes, grad, extended, buffers, final):
        self.place, self.copies, self.planes, self.final = place, copies, planes, final
        self.grad, self.extended = grad, extended
        self.from_left, self.from_up, self.from_right, self.from_down, self.from_corner = buffers
        count, tall, size = grad.shape[1:]
        self.last, height = count - 1, tall - size
        self.top, self.middle = pl.ds(0, size), pl.ds(size, height - size)
        self.below, self.own = pl.ds(height, size), pl.ds(0, height)
        self.block = [pl.ds(j * size, size) for j in range(self.last)]
        self.ups, self.downs = {}, {}

    def rows(self, j):
        up, down = self.place.at(-1, 0), self.place.at(1, 0)
        for p in self.planes:
            self.ups[p, j] = self.copies.start(
                self.grad.at[p, j, self.below], self.from_up.at[p, j], down
            )
            if not self.final:
                self.downs[p, j] = self.copies.start(
                    self.grad.at[p, j, self.top], self.from_down.at[p, j], up
                )

    def start(self):
        right = self.place.at(0, 1)
        self.sides = [
            self.copies.start(self.grad.at[p, self.last], self.from_left.at[p], right)
            for p in self.planes
        ]
        for j in range(1, self.last):
            self.rows(j)

    def first(self):
        for p, side in zip(self.planes, self.sides):
            side.wait_recv()
            self.grad[p, 0] += self.from_left[p]
        self.rows(0)
        if not self.final:
            left = self.place.at(0, -1)
            self.middles = [
                self.copies.start(self.grad.at[p, 0, self.middle], self.from_right.at[p], left)
                for p in self.planes
            ]

    def corner(self):
        left = self.place.at(0, -1)
        self.corners = {}
        for p in self.planes:
            self.copies.sent(self.ups[p, 0])
            self.copies.sent(self.downs[p, 0])
            self.ups[p, 0].wait_recv()
            self.grad[p, 0, self.top] += self.from_up[p, 0]
            self.downs[p, 0].wait_recv()
            self.grad[p, 0, self.below] += self.from_down[p, 0]
            for k, lines in enumerate((self.top, self.below)):
                self.corners[p, k] = self.copies.start(
                    self.grad.at[p, 0, lines], self.from_corner.at[p, k], left
                )

    def update(self):
        grad, extended, last = self.grad, self.extended, self.last
        top, middle, below = self.top, self.middle, self.below
        for p in self.planes:
            extended[p % 2][p // 2, 0] -= STEP_OBJECT * grad[p, 0]
        for j in range(1, last):
            for p in self.planes:
                self.ups[p, j].wait_recv()
                self.downs[p, j].wait_recv()
                extended[p % 2][p // 2, j, middle] -= STEP_OBJECT * grad[p, j, middle]
                extended[p % 2][p // 2, j, top] -= STEP_OBJECT * (grad[p, j, top] + self.from_up[p, j])
                extended[p % 2][p // 2, j, below] -= STEP_OBJECT * (grad[p, j, below] + self.from_down[p, j])
        for p, copy in zip(self.planes, self.middles):
            copy.wait_recv()
            extended[p % 2][p // 2, last, middle] -= STEP_OBJECT * self.from_right[p]
            for k, lines in enumerate((top, below)):
                self.corners[p, k].wait_recv()
                extended[p % 2][p // 2, last, lines] -= STEP_OBJECT * self.from_corner[p, k]

    def keep(self, new_field):
        for j in range(self.last):
            for p in self.planes:
                new_field[p, :, self.block[j]] = (
                    self.extended[p % 2][p // 2, j, self.own] - STEP_OBJECT * self.grad[p, j, self.own]
                )

    def complete(self, new_field):
        for j in list(range(1, self.last)) + [0]:
            for p in self.planes:
                self.ups[p, j].wait_recv()
                new_field[p, self.top, self.block[j]] -= STEP_OBJECT * self.from_up[p, j]


SLICE_PLANES = ((0, 2), (1, 3))


def program_kernel(
    tiles,
    cols,
    rows,
    columns,
    counts,
    field,
    probe_hbm,
    measured_hbm,
    table_hbm,
    new_field,
    new_probe,
    object_first,
    object_second,
    grad,
    beam,
    grad_beam,
    measured,
    table,
    windows,
    spread,
    back,
    patches,
    from_left,
    from_up,
    from_right,
    from_down,
    from_corner,
    *rest,
):
    sums, (local_sem, send, recv) = rest[:-3], rest[-3:]
    sums = [sums[: len(sums) // 2], sums[len(sums) // 2 :]]
    extended = (object_first, object_second)
    planes, count, tall, size = grad.shape
    last = count - 1
    height = tall - size
    slots = measured.shape[0]
    step_probe = 1.0 / (slots * tiles * cols)
    top, below, own = pl.ds(0, size), pl.ds(height, size), pl.ds(0, height)
    block = [pl.ds(j * size, size) for j in range(last)]
    place = Place(tiles, cols)
    copies = Copies(send, recv)
    up, left = place.at(-1, 0), place.at(0, -1)

    loads = [
        (field.at[p, :, block[j]], extended[p % 2].at[p // 2, j, own])
        for p in range(planes)
        for j in range(last)
    ]
    loads += [(probe_hbm, beam), (table_hbm, table), (measured_hbm, measured)]
    loads = [
        pltpu.make_async_copy(source, target, local_sem.at[k])
        for k, (source, target) in enumerate(loads)
    ]
    for load in loads:
        load.start()
    greet(met(place))

    halos, sides, corners = {}, {}, {}

    def send_halo(p, j):
        halos[p, j] = copies.start(
            field.at[p, top, block[j]], extended[p % 2].at[p // 2, j, below], up
        )

    def pass_corners(which):
        for p in SLICE_PLANES[which]:
            halos[p, 0].wait_recv()
            corners[p] = copies.start(
                extended[p % 2].at[p // 2, 0, below], extended[p % 2].at[p // 2, last, below], left
            )

    def take_halo(which):
        for p in SLICE_PLANES[which]:
            for copy in [halos[p, j] for j in range(1, last)] + [sides[p], corners[p]]:
                copy.wait_recv()

    for which in SLICE_PLANES:
        for p in which:
            send_halo(p, 0)
        for p in which:
            sides[p] = copies.start(
                field.at[p, :, block[0]], extended[p % 2].at[p // 2, last, own], left
            )
        for j in range(1, last):
            for p in which:
                send_halo(p, j)
    pass_corners(0)
    for load in loads:
        load.wait()
    take_halo(0)

    refs = (rows, columns, counts, measured, extended, beam, table, grad, grad_beam)
    work = Positions(refs + (windows, spread, back, patches), size, slots)
    waiting = None
    for sweep in range(ITERS):
        final = sweep == ITERS - 1
        landed = (from_left.at[sweep], from_up.at[sweep], from_right, from_down, from_corner)
        zeroth, first = [
            Overlap(place, copies, which, grad, extended, landed, final) for which in SLICE_PLANES
        ]
        for step in range(work.groups):
            work.propagate(step)
            if step == 0 and sweep == 0:
                pass_corners(1)
        if sweep == 0:
            take_halo(1)
        else:
            waiting.update()
        copies.finish()
        lax.fori_loop(0, work.groups, lambda step, carry: (work.diffract(step), carry)[1], 0)
        for step in range(work.groups):
            work.return_back(step)
        reduce = ProbeSum(place, copies, grad_beam, *sums[sweep])
        reduce.scatter_pair()
        for step in range(work.groups):
            work.place_patches(step, SLICE_PLANES[0])
            if step == 0:
                reduce.scatter_plane()
        zeroth.start()
        for step in range(work.groups):
            work.place_patches(step, SLICE_PLANES[1])
        first.start()
        zeroth.first()
        reduce.sum_line()
        first.first()
        if final:
            first.keep(new_field)
            zeroth.keep(new_field)
            reduce.gather_plane()
            zeroth.complete(new_field)
            first.complete(new_field)
            reduce.gather_pair()
            new_probe[...] = beam[...] - step_probe * reduce.result()
            copies.finish()
        else:
            reduce.gather_plane()
            zeroth.corner()
            first.corner()
            reduce.gather_pair()
            zeroth.update()
            beam[...] -= step_probe * reduce.result()
            waiting = first


def local(table, tiles, cols, object_field, probe, row_offsets, col_offsets, counts, measured):
    size = probe.shape[-1]
    height, width = object_field.shape[2:]
    slots = row_offsets.shape[-1]
    field = object_field.reshape(4, height, width)
    flat = (probe.shape[0] * probe.shape[1] * size, size)
    planes, last, tall = 4, width // size, height + size
    needed = planes * (2 * last + 2) + ITERS * ProbeSum.copies_needed(tiles, cols)
    needed += planes * (1 + 2 * last + 1 + 2) + planes * (1 + last)
    work = ITERS * slots * probe.shape[1] * 8 * 3 * 2 * 256 * 256 * 128
    smem = pl.BlockSpec(memory_space=pltpu.SMEM)
    hbm = pl.BlockSpec(memory_space=pl.ANY)
    vmem = pl.BlockSpec(memory_space=pltpu.VMEM)
    new_field, new_probe = pl.pallas_call(
        functools.partial(program_kernel, tiles, cols),
        out_shape=[jax.ShapeDtypeStruct(field.shape, f32), jax.ShapeDtypeStruct(flat, f32)],
        in_specs=[smem] * 3 + [hbm] * 4,
        out_specs=[vmem] * 2,
        scratch_shapes=[
            pltpu.VMEM((planes // 2, last + 1, tall, size), f32),
            pltpu.VMEM((planes // 2, last + 1, tall, size), f32),
            pltpu.VMEM((planes, last + 1, tall, size), f32),
            pltpu.VMEM(flat, f32),
            pltpu.VMEM(flat, f32),
            pltpu.VMEM((slots, size, size), f32),
            pltpu.VMEM(table.shape, bf16),
            pltpu.VMEM((slots, 2, size, size), f32),
            pltpu.VMEM((slots, probe.shape[1], 2, size, size), f32),
            pltpu.VMEM((slots, probe.shape[1], 2, size, size), f32),
            pltpu.VMEM((slots, planes, size, size), f32),
            pltpu.VMEM((ITERS, planes, tall, size), f32),
            pltpu.VMEM((ITERS, planes, last, size, size), f32),
            pltpu.VMEM((planes, height - size, size), f32),
            pltpu.VMEM((planes, last, size, size), f32),
            pltpu.VMEM((planes, 2, size, size), f32),
            *ProbeSum.scratch(*flat, tiles, cols),
            *ProbeSum.scratch(*flat, tiles, cols),
            pltpu.SemaphoreType.DMA((planes * last + 3,)),
            pltpu.SemaphoreType.DMA((needed,)),
            pltpu.SemaphoreType.DMA((needed,)),
        ],
        compiler_params=pltpu.CompilerParams(
            collective_id=0, has_side_effects=True, vmem_limit_bytes=VMEM_LIMIT
        ),
        cost_estimate=pl.CostEstimate(flops=work, bytes_accessed=5 * 2**20, transcendentals=0),
        name="ptychography",
    )(
        row_offsets.reshape(slots),
        col_offsets.reshape(slots),
        counts.reshape(1),
        field,
        probe.reshape(flat),
        measured.reshape(slots, size, size),
        table,
    )
    return new_field.reshape(object_field.shape), new_probe.reshape(probe.shape)


def solution(mesh):
    table = jnp.asarray(transform_tables(128))
    tiles, cols = mesh.shape["tiles"], mesh.shape["cols"]
    in_specs = (
        P(None, None, "tiles", "cols"),
        P(),
        P("tiles", "cols", None),
        P("tiles", "cols", None),
        P("tiles", "cols"),
        P("tiles", "cols", None, None, None),
    )
    out_specs = (P(None, None, "tiles", "cols"), P())
    body = functools.partial(local, table, tiles, cols)
    return jax.shard_map(body, mesh=mesh, in_specs=in_specs, out_specs=out_specs, check_vma=False)
```

```python
import functools
import math

import jax
import jax.numpy as jnp
import ml_dtypes
import numpy as np
from jax import lax
from jax.experimental import pallas as pl
from jax.experimental.pallas import tpu as pltpu
from jax.sharding import PartitionSpec as P

ITERS = 2
STEP_OBJECT = 0.25
f32, bf16 = jnp.float32, jnp.bfloat16
MESH = pl.DeviceIdType.MESH
VMEM_LIMIT = 56 * 2**20

A_PLUS, A_MINUS, F_PLUS, F_MINUS = 0, 2, 4, 6


def split_table(table):
    high = table.astype(np.float32).astype(ml_dtypes.bfloat16)
    low = (table - high.astype(np.float64)).astype(np.float32).astype(ml_dtypes.bfloat16)
    return [high, low]


def transform_tables(size):
    line = np.arange(size)
    dft = np.exp(-2j * np.pi * (np.outer(line, line) % size) / size) / math.sqrt(size)
    freq = np.where(line < size // 2, line, line - size)
    chirp = np.exp(-2j * np.pi * ((freq * freq) % (4 * size)) / (4 * size))
    propagator = np.conj(dft) @ (chirp[:, None] * dft)
    parts = []
    for matrix in (propagator, dft):
        real, imag = matrix.real, matrix.imag
        plus = np.block([[real, imag], [-imag, real]])
        parts += split_table(plus) + split_table(plus.T)
    return np.stack(parts)


def split(value):
    high = value.astype(bf16)
    return high, (value - high.astype(f32)).astype(bf16)


def product(first, second):
    dot = functools.partial(jnp.dot, preferred_element_type=f32)
    return dot(first[0], second[0]) + (dot(first[1], second[0]) + dot(first[0], second[1]))


def two_sided(fields, table, left, right):
    n = fields[0][0].shape[0]
    modes = range(len(fields))
    stacked = [jnp.concatenate(field, axis=0) for field in fields]
    middle = product((table[left], table[left + 1]), split(jnp.concatenate(stacked, axis=1)))
    columns = [middle[:, n * m : n * m + n] for m in modes]
    beside = [jnp.concatenate([c[:n], c[n:]], axis=1) for c in columns]
    result = product(split(jnp.concatenate(beside, axis=0)), (table[right], table[right + 1]))
    rows = [result[n * m : n * m + n] for m in modes]
    return [(row[:, :n], row[:, n:]) for row in rows]


def times(a, b):
    return (a[0] * b[0] - a[1] * b[1], a[0] * b[1] + a[1] * b[0])


def conj_times(a, b):
    return (a[0] * b[0] + a[1] * b[1], a[0] * b[1] - a[1] * b[0])


def total(terms):
    real, imag = terms[0]
    for term in terms[1:]:
        real, imag = real + term[0], imag + term[1]
    return real, imag


GROUP = 4
LINE = 4


class Positions:
    def __init__(self, refs, n, slots):
        self.rows, self.cols, self.counts, self.measured = refs[:4]
        self.extended, self.beam, self.table, self.grad, self.grad_beam = refs[4:9]
        self.windows, self.spread, self.back, self.patches = refs[9:]
        self.n, self.slots = n, slots
        self.modes = range(self.spread.shape[1])
        self.groups = slots // GROUP

    def beams(self):
        n, part = self.n, len(self.modes) * self.n
        return [(self.beam[pl.ds(m * n, n)], self.beam[pl.ds(part + m * n, n)]) for m in self.modes]

    def spots(self, step):
        found = []
        for k in range(GROUP):
            slot = step * GROUP + k
            live = slot < self.counts[0]
            row = jnp.where(live, self.rows[slot], 0)
            col = jnp.where(live, self.cols[slot], 0)
            block = lax.shift_right_logical(col, 7)
            weight = jnp.where(live, 1.0, 0.0).astype(f32)
            found.append((slot, weight, row, block, col - block * self.n))
        return found

    def lane(self):
        return lax.broadcasted_iota(jnp.int32, (self.n, self.n), 1)

    def window(self, plane, spot):
        n = self.n
        _, _, row, block, shift = spot
        back = jnp.bitwise_and(n - shift, n - 1)
        near = pltpu.roll(self.extended[plane % 2][plane // 2, block, pl.ds(row, n), :], back, 1)
        far = pltpu.roll(self.extended[plane % 2][plane // 2, block + 1, pl.ds(row, n), :], back, 1)
        return jnp.where(self.lane() < n - shift, near, far)

    def propagate(self, step):
        spots, beams = self.spots(step), self.beams()
        first = [(self.window(0, s), self.window(2, s)) for s in spots]
        for spot, field in zip(spots, first):
            self.windows[spot[0], 0], self.windows[spot[0], 1] = field
            result = two_sided([times(b, field) for b in beams], self.table, A_MINUS, A_PLUS)
            for m in self.modes:
                self.spread[spot[0], m, 0], self.spread[spot[0], m, 1] = result[m]

    def diffract(self, step):
        spots = self.spots(step)
        spread = [
            [(self.spread[s[0], m, 0], self.spread[s[0], m, 1]) for m in self.modes] for s in spots
        ]
        second = [(self.window(1, s), self.window(3, s)) for s in spots]
        far = [
            two_sided([times(o, x) for x in fields], self.table, F_MINUS, F_PLUS)
            for o, fields in zip(second, spread)
        ]
        residual = []
        for spot, fields in zip(spots, far):
            intensity = sum(y[0] * y[0] + y[1] * y[1] for y in fields)
            residual.append((intensity - self.measured[spot[0]]) * spot[1])
        back = [
            two_sided([(r * y[0], r * y[1]) for y in fields], self.table, F_PLUS, F_MINUS)
            for r, fields in zip(residual, far)
        ]
        patches = [
            total([conj_times(x, g) for x, g in zip(fields, backs)])
            for fields, backs in zip(spread, back)
        ]
        for spot, o, backs in zip(spots, second, back):
            for m in self.modes:
                self.back[spot[0], m, 0], self.back[spot[0], m, 1] = conj_times(o, backs[m])
        for spot, patch in zip(spots, patches):
            self.patches[spot[0], 1], self.patches[spot[0], 3] = patch

    def return_back(self, step):
        spots, beams = self.spots(step), self.beams()
        n, part = self.n, len(self.modes) * self.n
        back = []
        for spot in spots:
            fields = [(self.back[spot[0], m, 0], self.back[spot[0], m, 1]) for m in self.modes]
            back.append(two_sided(fields, self.table, A_PLUS, A_MINUS))
        first = [(self.windows[s[0], 0], self.windows[s[0], 1]) for s in spots]
        for m in self.modes:
            terms = total([conj_times(o, backs[m]) for o, backs in zip(first, back)])
            for term, start in zip(terms, (m * n, part + m * n)):
                if step == 0:
                    self.grad_beam[pl.ds(start, n)] = term
                else:
                    self.grad_beam[pl.ds(start, n)] += term
        for spot, backs in zip(spots, back):
            patch = total([conj_times(b, g) for b, g in zip(beams, backs)])
            self.patches[spot[0], 0], self.patches[spot[0], 2] = patch

    def place_patches(self, step, planes):
        spots = self.spots(step)
        patches = [[self.patches[s[0], p] for p in planes] for s in spots]
        self.put(spots, patches, planes, step == 0)

    def put(self, spots, patches, planes, fresh):
        n = self.n
        count, tall = self.grad.shape[1:3]
        offset = lax.broadcasted_iota(jnp.int32, (tall, n), 0) - lax.broadcasted_iota(
            jnp.int32, (tall, n), 1
        )
        ones, pieces = [], [[] for _ in range(count)]
        for (_, _, row, block, shift), patch in zip(spots, patches):
            ones += [jnp.where(offset == row, 1.0, 0.0).astype(bf16)] * 2
            kept = self.lane() >= shift
            beside = [[] for _ in range(count)]
            for value in patch:
                moved = pltpu.roll(value, shift, 1)
                near, over = jnp.where(kept, moved, 0.0), jnp.where(kept, 0.0, moved)
                for b in range(count):
                    if b == 0:
                        placed = jnp.where(block == 0, near, 0.0)
                    elif b == count - 1:
                        placed = jnp.where(block == b - 1, over, 0.0)
                    else:
                        placed = jnp.where(block == b, near, jnp.where(block == b - 1, over, 0.0))
                    beside[b].append(placed)
            for b in range(count):
                pieces[b] += split(jnp.concatenate(beside[b], axis=1))
        ones = jnp.concatenate(ones, axis=1)
        for b in range(count):
            sums = jnp.dot(ones, jnp.concatenate(pieces[b], axis=0), preferred_element_type=f32)
            for k, p in enumerate(planes):
                if fresh:
                    self.grad[p, b] = sums[:, k * n : k * n + n]
                else:
                    self.grad[p, b] += sums[:, k * n : k * n + n]


class Place:
    def __init__(self, tiles, cols):
        self.tiles, self.cols = tiles, cols
        self.t, self.c = lax.axis_index("tiles"), lax.axis_index("cols")

    def at(self, down, right):
        return (
            lax.rem(self.t + (down + self.tiles), self.tiles),
            lax.rem(self.c + (right + self.cols), self.cols),
        )


def greet(devices):
    barrier = pltpu.get_barrier_semaphore()
    for device in devices:
        pl.semaphore_signal(barrier, inc=1, device_id=device, device_id_type=MESH)
    pl.semaphore_wait(barrier, len(devices))


class Copies:
    def __init__(self, send, recv):
        self.send, self.recv, self.used, self.started = send, recv, 0, []

    def start(self, source, target, device):
        k = self.used
        self.used += 1
        copy = pltpu.make_async_remote_copy(
            src_ref=source,
            dst_ref=target,
            send_sem=self.send.at[k],
            recv_sem=self.recv.at[k],
            device_id=device,
            device_id_type=MESH,
        )
        copy.start()
        self.started.append(copy)
        return copy

    def sent(self, copy):
        copy.wait_send()
        self.started = [other for other in self.started if other is not copy]

    def finish(self):
        for copy in self.started:
            copy.wait_send()
        self.started = []


class ProbeSum:
    def __init__(self, place, copies, grad, pair, pieces, column, halves):
        self.place, self.copies = place, copies
        self.grad, self.pair, self.pieces, self.column, self.halves = grad, pair, pieces, column, halves
        self.half = grad.shape[0] // 2
        self.piece = self.half // (pieces.shape[0] + 1)
        self.core = lax.rem(place.c, 2)
        self.partner = (place.t, place.c + 1 - 2 * self.core)
        self.mine = pl.ds(self.core * self.half, self.half)
        self.others = pl.ds((1 - self.core) * self.half, self.half)

    @staticmethod
    def plane(place):
        found = []
        chips = place.cols // 2
        for k in range(1, place.tiles // LINE * chips):
            t, c = place.at(k // chips * LINE, 2 * (k % chips))
            found.append((t // LINE * chips + c // 2, (t, c)))
        return found

    @staticmethod
    def line(place):
        start = place.t // LINE * LINE
        return [(start + lax.rem(place.t + k, LINE), place.c) for k in range(1, LINE)]

    def part(self, number):
        return pl.ds(self.core * self.half + number * self.piece, self.piece)

    def number(self):
        return self.place.t // LINE * (self.place.cols // 2) + self.place.c // 2

    def scatter_pair(self):
        self.step = self.copies.start(self.grad.at[self.others], self.pair, self.partner)

    def scatter_plane(self):
        self.step.wait_recv()
        self.grad[self.mine] += self.pair[...]
        self.steps = [
            self.copies.start(self.grad.at[self.part(number)], self.pieces.at[k], device)
            for k, (number, device) in enumerate(self.plane(self.place))
        ]

    def sum_line(self):
        value = self.grad[self.part(self.number())]
        for k, step in enumerate(self.steps):
            step.wait_recv()
            value += self.pieces[k]
        spot = lax.rem(self.place.t, LINE)
        self.column[spot] = value
        self.steps = [
            self.copies.start(self.column.at[spot], self.column.at[spot], device)
            for device in self.line(self.place)
        ]

    def gather_plane(self):
        for step in self.steps:
            step.wait_recv()
        value = self.column[0]
        for k in range(1, LINE):
            value += self.column[k]
        own = self.part(self.number())
        self.halves[own] = value
        self.steps = [
            self.copies.start(self.halves.at[own], self.halves.at[own], device)
            for _, device in self.plane(self.place)
        ]

    def gather_pair(self):
        for step in self.steps:
            step.wait_recv()
        self.step = self.copies.start(
            self.halves.at[self.mine], self.halves.at[self.mine], self.partner
        )

    def result(self):
        self.step.wait_recv()
        return self.halves[...]

    @staticmethod
    def copies_needed(tiles, cols):
        return tiles * cols // (2 * LINE) * 2 + LINE - 1

    @staticmethod
    def scratch(rows, lanes, tiles, cols):
        half = rows // 2
        parts = tiles * cols // (2 * LINE)
        piece = half // parts
        return [
            pltpu.VMEM((half, lanes), f32),
            pltpu.VMEM((parts - 1, piece, lanes), f32),
            pltpu.VMEM((LINE, piece, lanes), f32),
            pltpu.VMEM((rows, lanes), f32),
        ]


def met(place):
    sides = [place.at(*way) for way in ((-1, 0), (1, 0), (0, -1), (0, 1))]
    return [device for _, device in ProbeSum.plane(place)] + ProbeSum.line(place) + sides


class Overlap:
    def __init__(self, place, copies, planes, grad, extended, buffers, final):
        self.place, self.copies, self.planes, self.final = place, copies, planes, final
        self.grad, self.extended = grad, extended
        self.from_left, self.from_up, self.from_right, self.from_down, self.from_corner = buffers
        count, tall, size = grad.shape[1:]
        self.last, height = count - 1, tall - size
        self.top, self.middle = pl.ds(0, size), pl.ds(size, height - size)
        self.below, self.own = pl.ds(height, size), pl.ds(0, height)
        self.block = [pl.ds(j * size, size) for j in range(self.last)]
        self.ups, self.downs = {}, {}

    def rows(self, j):
        up, down = self.place.at(-1, 0), self.place.at(1, 0)
        for p in self.planes:
            self.ups[p, j] = self.copies.start(
                self.grad.at[p, j, self.below], self.from_up.at[p, j], down
            )
            if not self.final:
                self.downs[p, j] = self.copies.start(
                    self.grad.at[p, j, self.top], self.from_down.at[p, j], up
                )

    def start(self):
        right = self.place.at(0, 1)
        self.edges = {
            (p, k): self.copies.start(
                self.grad.at[p, self.last, lines], self.from_left.at[p, lines], right
            )
            for p in self.planes
            for k, lines in enumerate((self.top, self.below))
        }
        for j in range(1, self.last):
            self.rows(j)

    def start_inner(self):
        right = self.place.at(0, 1)
        self.sides = [
            self.copies.start(
                self.grad.at[p, self.last, self.middle], self.from_left.at[p, self.middle], right
            )
            for p in self.planes
        ]

    def first(self):
        for p in self.planes:
            for k, lines in enumerate((self.top, self.below)):
                self.edges[p, k].wait_recv()
                self.grad[p, 0, lines] += self.from_left[p, lines]
        self.rows(0)

    def inner(self):
        left = self.place.at(0, -1)
        self.middles = []
        for p, side in zip(self.planes, self.sides):
            side.wait_recv()
            self.grad[p, 0, self.middle] += self.from_left[p, self.middle]
            if not self.final:
                self.middles.append(
                    self.copies.start(self.grad.at[p, 0, self.middle], self.from_right.at[p], left)
                )

    def corner(self):
        left = self.place.at(0, -1)
        self.corners = {}
        for p in self.planes:
            self.copies.sent(self.ups[p, 0])
            self.copies.sent(self.downs[p, 0])
            self.ups[p, 0].wait_recv()
            self.grad[p, 0, self.top] += self.from_up[p, 0]
            self.downs[p, 0].wait_recv()
            self.grad[p, 0, self.below] += self.from_down[p, 0]
            for k, lines in enumerate((self.top, self.below)):
                self.corners[p, k] = self.copies.start(
                    self.grad.at[p, 0, lines], self.from_corner.at[p, k], left
                )

    def update(self):
        grad, extended, last = self.grad, self.extended, self.last
        top, middle, below = self.top, self.middle, self.below
        for p in self.planes:
            extended[p % 2][p // 2, 0] -= STEP_OBJECT * grad[p, 0]
        for j in range(1, last):
            for p in self.planes:
                self.ups[p, j].wait_recv()
                self.downs[p, j].wait_recv()
                extended[p % 2][p // 2, j, middle] -= STEP_OBJECT * grad[p, j, middle]
                extended[p % 2][p // 2, j, top] -= STEP_OBJECT * (grad[p, j, top] + self.from_up[p, j])
                extended[p % 2][p // 2, j, below] -= STEP_OBJECT * (grad[p, j, below] + self.from_down[p, j])
        for p, copy in zip(self.planes, self.middles):
            copy.wait_recv()
            extended[p % 2][p // 2, last, middle] -= STEP_OBJECT * self.from_right[p]
            for k, lines in enumerate((top, below)):
                self.corners[p, k].wait_recv()
                extended[p % 2][p // 2, last, lines] -= STEP_OBJECT * self.from_corner[p, k]

    def keep(self, new_field):
        for j in range(self.last):
            for p in self.planes:
                new_field[p, :, self.block[j]] = (
                    self.extended[p % 2][p // 2, j, self.own] - STEP_OBJECT * self.grad[p, j, self.own]
                )

    def complete(self, new_field):
        for j in list(range(1, self.last)) + [0]:
            for p in self.planes:
                self.ups[p, j].wait_recv()
                new_field[p, self.top, self.block[j]] -= STEP_OBJECT * self.from_up[p, j]


SLICE_PLANES = ((0, 2), (1, 3))


def program_kernel(
    tiles,
    cols,
    rows,
    columns,
    counts,
    field,
    probe_hbm,
    measured_hbm,
    table_hbm,
    new_field,
    new_probe,
    object_first,
    object_second,
    grad,
    beam,
    grad_beam,
    measured,
    table,
    windows,
    spread,
    back,
    patches,
    from_left,
    from_up,
    from_right,
    from_down,
    from_corner,
    *rest,
):
    sums, (local_sem, send, recv) = rest[:-3], rest[-3:]
    sums = [sums[: len(sums) // 2], sums[len(sums) // 2 :]]
    extended = (object_first, object_second)
    planes, count, tall, size = grad.shape
    last = count - 1
    height = tall - size
    slots = measured.shape[0]
    step_probe = 1.0 / (slots * tiles * cols)
    top, below, own = pl.ds(0, size), pl.ds(height, size), pl.ds(0, height)
    block = [pl.ds(j * size, size) for j in range(last)]
    place = Place(tiles, cols)
    copies = Copies(send, recv)
    up, left = place.at(-1, 0), place.at(0, -1)

    loads = [
        (field.at[p, :, block[j]], extended[p % 2].at[p // 2, j, own])
        for p in range(planes)
        for j in range(last)
    ]
    loads += [(probe_hbm, beam), (table_hbm, table), (measured_hbm, measured)]
    loads = [
        pltpu.make_async_copy(source, target, local_sem.at[k])
        for k, (source, target) in enumerate(loads)
    ]
    for load in loads:
        load.start()
    greet(met(place))

    halos, sides, corners = {}, {}, {}

    def send_halo(p, j):
        halos[p, j] = copies.start(
            field.at[p, top, block[j]], extended[p % 2].at[p // 2, j, below], up
        )

    def pass_corners(which):
        for p in SLICE_PLANES[which]:
            halos[p, 0].wait_recv()
            corners[p] = copies.start(
                extended[p % 2].at[p // 2, 0, below], extended[p % 2].at[p // 2, last, below], left
            )

    def take_halo(which):
        for p in SLICE_PLANES[which]:
            for copy in [halos[p, j] for j in range(1, last)] + [sides[p], corners[p]]:
                copy.wait_recv()

    for which in SLICE_PLANES:
        for p in which:
            send_halo(p, 0)
        for p in which:
            sides[p] = copies.start(
                field.at[p, :, block[0]], extended[p % 2].at[p // 2, last, own], left
            )
        for j in range(1, last):
            for p in which:
                send_halo(p, j)
    pass_corners(0)
    for load in loads:
        load.wait()
    take_halo(0)

    refs = (rows, columns, counts, measured, extended, beam, table, grad, grad_beam)
    work = Positions(refs + (windows, spread, back, patches), size, slots)
    waiting = None
    for sweep in range(ITERS):
        final = sweep == ITERS - 1
        landed = (from_left.at[sweep], from_up.at[sweep], from_right, from_down, from_corner)
        zeroth, first = [
            Overlap(place, copies, which, grad, extended, landed, final) for which in SLICE_PLANES
        ]
        for step in range(work.groups):
            work.propagate(step)
            if step == 0 and sweep == 0:
                pass_corners(1)
        if sweep == 0:
            take_halo(1)
        else:
            waiting.update()
        copies.finish()
        lax.fori_loop(0, work.groups, lambda step, carry: (work.diffract(step), carry)[1], 0)
        for step in range(work.groups):
            work.return_back(step)
        reduce = ProbeSum(place, copies, grad_beam, *sums[sweep])
        reduce.scatter_pair()
        for step in range(work.groups):
            work.place_patches(step, SLICE_PLANES[0])
            if step == 0:
                reduce.scatter_plane()
        zeroth.start()
        for step in range(work.groups):
            work.place_patches(step, SLICE_PLANES[1])
        first.start()
        zeroth.start_inner()
        first.start_inner()
        reduce.sum_line()
        zeroth.first()
        reduce.gather_plane()
        first.first()
        zeroth.inner()
        if final:
            first.inner()
            zeroth.keep(new_field)
            first.keep(new_field)
            zeroth.complete(new_field)
            reduce.gather_pair()
            first.complete(new_field)
            new_probe[...] = beam[...] - step_probe * reduce.result()
            copies.finish()
        else:
            zeroth.corner()
            first.inner()
            reduce.gather_pair()
            first.corner()
            zeroth.update()
            beam[...] -= step_probe * reduce.result()
            waiting = first


def local(table, tiles, cols, object_field, probe, row_offsets, col_offsets, counts, measured):
    size = probe.shape[-1]
    height, width = object_field.shape[2:]
    slots = row_offsets.shape[-1]
    field = object_field.reshape(4, height, width)
    flat = (probe.shape[0] * probe.shape[1] * size, size)
    planes, last, tall = 4, width // size, height + size
    needed = planes * (2 * last + 2) + ITERS * ProbeSum.copies_needed(tiles, cols)
    needed += planes * (3 + 2 * last + 1 + 2) + planes * (3 + last)
    work = ITERS * slots * probe.shape[1] * 8 * 3 * 2 * 256 * 256 * 128
    smem = pl.BlockSpec(memory_space=pltpu.SMEM)
    hbm = pl.BlockSpec(memory_space=pl.ANY)
    vmem = pl.BlockSpec(memory_space=pltpu.VMEM)
    new_field, new_probe = pl.pallas_call(
        functools.partial(program_kernel, tiles, cols),
        out_shape=[jax.ShapeDtypeStruct(field.shape, f32), jax.ShapeDtypeStruct(flat, f32)],
        in_specs=[smem] * 3 + [hbm] * 4,
        out_specs=[vmem] * 2,
        scratch_shapes=[
            pltpu.VMEM((planes // 2, last + 1, tall, size), f32),
            pltpu.VMEM((planes // 2, last + 1, tall, size), f32),
            pltpu.VMEM((planes, last + 1, tall, size), f32),
            pltpu.VMEM(flat, f32),
            pltpu.VMEM(flat, f32),
            pltpu.VMEM((slots, size, size), f32),
            pltpu.VMEM(table.shape, bf16),
            pltpu.VMEM((slots, 2, size, size), f32),
            pltpu.VMEM((slots, probe.shape[1], 2, size, size), f32),
            pltpu.VMEM((slots, probe.shape[1], 2, size, size), f32),
            pltpu.VMEM((slots, planes, size, size), f32),
            pltpu.VMEM((ITERS, planes, tall, size), f32),
            pltpu.VMEM((ITERS, planes, last, size, size), f32),
            pltpu.VMEM((planes, height - size, size), f32),
            pltpu.VMEM((planes, last, size, size), f32),
            pltpu.VMEM((planes, 2, size, size), f32),
            *ProbeSum.scratch(*flat, tiles, cols),
            *ProbeSum.scratch(*flat, tiles, cols),
            pltpu.SemaphoreType.DMA((planes * last + 3,)),
            pltpu.SemaphoreType.DMA((needed,)),
            pltpu.SemaphoreType.DMA((needed,)),
        ],
        compiler_params=pltpu.CompilerParams(
            collective_id=0, has_side_effects=True, vmem_limit_bytes=VMEM_LIMIT
        ),
        cost_estimate=pl.CostEstimate(flops=work, bytes_accessed=5 * 2**20, transcendentals=0),
        name="ptychography",
    )(
        row_offsets.reshape(slots),
        col_offsets.reshape(slots),
        counts.reshape(1),
        field,
        probe.reshape(flat),
        measured.reshape(slots, size, size),
        table,
    )
    return new_field.reshape(object_field.shape), new_probe.reshape(probe.shape)


def solution(mesh):
    table = jnp.asarray(transform_tables(128))
    tiles, cols = mesh.shape["tiles"], mesh.shape["cols"]
    in_specs = (
        P(None, None, "tiles", "cols"),
        P(),
        P("tiles", "cols", None),
        P("tiles", "cols", None),
        P("tiles", "cols"),
        P("tiles", "cols", None, None, None),
    )
    out_specs = (P(None, None, "tiles", "cols"), P())
    body = functools.partial(local, table, tiles, cols)
    return jax.shard_map(body, mesh=mesh, in_specs=in_specs, out_specs=out_specs, check_vma=False)
```

```python
import functools
import math

import jax
import jax.numpy as jnp
import ml_dtypes
import numpy as np
from jax import lax
from jax.experimental import pallas as pl
from jax.experimental.pallas import tpu as pltpu
from jax.sharding import PartitionSpec as P

ITERS = 2
STEP_OBJECT = 0.25
f32, bf16 = jnp.float32, jnp.bfloat16
MESH = pl.DeviceIdType.MESH
VMEM_LIMIT = 56 * 2**20

A_PLUS, A_MINUS, F_PLUS, F_MINUS = 0, 2, 4, 6


def split_table(table):
    high = table.astype(np.float32).astype(ml_dtypes.bfloat16)
    low = (table - high.astype(np.float64)).astype(np.float32).astype(ml_dtypes.bfloat16)
    return [high, low]


def transform_tables(size):
    line = np.arange(size)
    dft = np.exp(-2j * np.pi * (np.outer(line, line) % size) / size) / math.sqrt(size)
    freq = np.where(line < size // 2, line, line - size)
    chirp = np.exp(-2j * np.pi * ((freq * freq) % (4 * size)) / (4 * size))
    propagator = np.conj(dft) @ (chirp[:, None] * dft)
    parts = []
    for matrix in (propagator, dft):
        real, imag = matrix.real, matrix.imag
        plus = np.block([[real, imag], [-imag, real]])
        parts += split_table(plus) + split_table(plus.T)
    return np.stack(parts)


def split(value):
    high = value.astype(bf16)
    return high, (value - high.astype(f32)).astype(bf16)


def product(first, second):
    dot = functools.partial(jnp.dot, preferred_element_type=f32)
    return dot(first[0], second[0]) + (dot(first[1], second[0]) + dot(first[0], second[1]))


def two_sided(groups, table, left, right):
    n = groups[0][0][0].shape[0]
    modes = range(len(groups[0]))
    middles = []
    for fields in groups:
        stacked = [jnp.concatenate(field, axis=0) for field in fields]
        middles.append(
            product((table[left], table[left + 1]), split(jnp.concatenate(stacked, axis=1)))
        )
    results = []
    for middle in middles:
        columns = [middle[:, n * m : n * m + n] for m in modes]
        beside = [jnp.concatenate([c[:n], c[n:]], axis=1) for c in columns]
        result = product(split(jnp.concatenate(beside, axis=0)), (table[right], table[right + 1]))
        rows = [result[n * m : n * m + n] for m in modes]
        results.append([(row[:, :n], row[:, n:]) for row in rows])
    return results


def times(a, b):
    return (a[0] * b[0] - a[1] * b[1], a[0] * b[1] + a[1] * b[0])


def conj_times(a, b):
    return (a[0] * b[0] + a[1] * b[1], a[0] * b[1] - a[1] * b[0])


def total(terms):
    real, imag = terms[0]
    for term in terms[1:]:
        real, imag = real + term[0], imag + term[1]
    return real, imag


GROUP = 4
LINE = 4


class Positions:
    def __init__(self, refs, n, slots):
        self.rows, self.cols, self.counts, self.measured = refs[:4]
        self.extended, self.beam, self.table, self.grad, self.grad_beam = refs[4:9]
        self.windows, self.spread, self.patches = refs[9:]
        self.n, self.slots = n, slots
        self.modes = range(self.spread.shape[1])
        self.groups = slots // GROUP

    def beams(self):
        n, part = self.n, len(self.modes) * self.n
        return [(self.beam[pl.ds(m * n, n)], self.beam[pl.ds(part + m * n, n)]) for m in self.modes]

    def spots(self, step):
        found = []
        for k in range(GROUP):
            slot = step * GROUP + k
            live = slot < self.counts[0]
            row = jnp.where(live, self.rows[slot], 0)
            col = jnp.where(live, self.cols[slot], 0)
            block = lax.shift_right_logical(col, 7)
            weight = jnp.where(live, 1.0, 0.0).astype(f32)
            found.append((slot, weight, row, block, col - block * self.n))
        return found

    def lane(self):
        return lax.broadcasted_iota(jnp.int32, (self.n, self.n), 1)

    def window(self, plane, spot):
        n = self.n
        _, _, row, block, shift = spot
        back = jnp.bitwise_and(n - shift, n - 1)
        near = pltpu.roll(self.extended[plane % 2][plane // 2, block, pl.ds(row, n), :], back, 1)
        far = pltpu.roll(self.extended[plane % 2][plane // 2, block + 1, pl.ds(row, n), :], back, 1)
        return jnp.where(self.lane() < n - shift, near, far)

    def propagate(self, step):
        spots, beams = self.spots(step), self.beams()
        first = [(self.window(0, s), self.window(2, s)) for s in spots]
        for spot, field in zip(spots, first):
            self.windows[spot[0], 0], self.windows[spot[0], 1] = field
        fields = [[times(b, field) for b in beams] for field in first]
        results = two_sided(fields, self.table, A_MINUS, A_PLUS)
        for spot, result in zip(spots, results):
            for m in self.modes:
                self.spread[spot[0], m, 0], self.spread[spot[0], m, 1] = result[m]

    def diffract(self, step):
        spots = self.spots(step)
        spread = [
            [(self.spread[s[0], m, 0], self.spread[s[0], m, 1]) for m in self.modes] for s in spots
        ]
        second = [(self.window(1, s), self.window(3, s)) for s in spots]
        leaving = [[times(o, x) for x in fields] for o, fields in zip(second, spread)]
        far = two_sided(leaving, self.table, F_MINUS, F_PLUS)
        residual = []
        for spot, fields in zip(spots, far):
            intensity = sum(y[0] * y[0] + y[1] * y[1] for y in fields)
            residual.append((intensity - self.measured[spot[0]]) * spot[1])
        weighed = [[(r * y[0], r * y[1]) for y in fields] for r, fields in zip(residual, far)]
        back = two_sided(weighed, self.table, F_PLUS, F_MINUS)
        patches = [
            total([conj_times(x, g) for x, g in zip(fields, backs)])
            for fields, backs in zip(spread, back)
        ]
        for spot, patch in zip(spots, patches):
            self.patches[spot[0], 1], self.patches[spot[0], 3] = patch
        entering = [[conj_times(o, g) for g in backs] for o, backs in zip(second, back)]
        back = two_sided(entering, self.table, A_PLUS, A_MINUS)
        beams = self.beams()
        n, part = self.n, len(self.modes) * self.n
        first = [(self.windows[s[0], 0], self.windows[s[0], 1]) for s in spots]
        for m in self.modes:
            terms = total([conj_times(o, backs[m]) for o, backs in zip(first, back)])
            for term, start in zip(terms, (m * n, part + m * n)):
                self.grad_beam[pl.ds(start, n)] += term
        for spot, backs in zip(spots, back):
            patch = total([conj_times(b, g) for b, g in zip(beams, backs)])
            self.patches[spot[0], 0], self.patches[spot[0], 2] = patch

    def place_patches(self, step, planes):
        spots = self.spots(step)
        patches = [[self.patches[s[0], p] for p in planes] for s in spots]
        self.put(spots, patches, planes, step == 0)

    def put(self, spots, patches, planes, fresh):
        n = self.n
        count, tall = self.grad.shape[1:3]
        offset = lax.broadcasted_iota(jnp.int32, (tall, n), 0) - lax.broadcasted_iota(
            jnp.int32, (tall, n), 1
        )
        ones, pieces = [], [[] for _ in range(count)]
        for (_, _, row, block, shift), patch in zip(spots, patches):
            ones += [jnp.where(offset == row, 1.0, 0.0).astype(bf16)] * 2
            kept = self.lane() >= shift
            beside = [[] for _ in range(count)]
            for value in patch:
                moved = pltpu.roll(value, shift, 1)
                near, over = jnp.where(kept, moved, 0.0), jnp.where(kept, 0.0, moved)
                for b in range(count):
                    if b == 0:
                        placed = jnp.where(block == 0, near, 0.0)
                    elif b == count - 1:
                        placed = jnp.where(block == b - 1, over, 0.0)
                    else:
                        placed = jnp.where(block == b, near, jnp.where(block == b - 1, over, 0.0))
                    beside[b].append(placed)
            for b in range(count):
                pieces[b] += split(jnp.concatenate(beside[b], axis=1))
        ones = jnp.concatenate(ones, axis=1)
        for b in range(count):
            sums = jnp.dot(ones, jnp.concatenate(pieces[b], axis=0), preferred_element_type=f32)
            for k, p in enumerate(planes):
                if fresh:
                    self.grad[p, b] = sums[:, k * n : k * n + n]
                else:
                    self.grad[p, b] += sums[:, k * n : k * n + n]


class Place:
    def __init__(self, tiles, cols):
        self.tiles, self.cols = tiles, cols
        self.t, self.c = lax.axis_index("tiles"), lax.axis_index("cols")

    def at(self, down, right):
        return (
            lax.rem(self.t + (down + self.tiles), self.tiles),
            lax.rem(self.c + (right + self.cols), self.cols),
        )


def greet(devices):
    barrier = pltpu.get_barrier_semaphore()
    for device in devices:
        pl.semaphore_signal(barrier, inc=1, device_id=device, device_id_type=MESH)
    pl.semaphore_wait(barrier, len(devices))


class Copies:
    def __init__(self, send, recv):
        self.send, self.recv, self.used, self.started = send, recv, 0, []

    def start(self, source, target, device):
        k = self.used
        self.used += 1
        copy = pltpu.make_async_remote_copy(
            src_ref=source,
            dst_ref=target,
            send_sem=self.send.at[k],
            recv_sem=self.recv.at[k],
            device_id=device,
            device_id_type=MESH,
        )
        copy.start()
        self.started.append(copy)
        return copy

    def sent(self, copy):
        copy.wait_send()
        self.started = [other for other in self.started if other is not copy]

    def finish(self):
        for copy in self.started:
            copy.wait_send()
        self.started = []


class ProbeSum:
    def __init__(self, place, copies, grad, pair, pieces, column, halves):
        self.place, self.copies = place, copies
        self.grad, self.pair, self.pieces, self.column, self.halves = grad, pair, pieces, column, halves
        self.half = grad.shape[0] // 2
        self.piece = self.half // (pieces.shape[0] + 1)
        self.core = lax.rem(place.c, 2)
        self.partner = (place.t, place.c + 1 - 2 * self.core)
        self.mine = pl.ds(self.core * self.half, self.half)
        self.others = pl.ds((1 - self.core) * self.half, self.half)

    @staticmethod
    def plane(place):
        found = []
        chips = place.cols // 2
        for k in range(1, place.tiles // LINE * chips):
            t, c = place.at(k // chips * LINE, 2 * (k % chips))
            found.append((t // LINE * chips + c // 2, (t, c)))
        return found

    @staticmethod
    def line(place):
        start = place.t // LINE * LINE
        return [(start + lax.rem(place.t + k, LINE), place.c) for k in range(1, LINE)]

    def part(self, number):
        return pl.ds(self.core * self.half + number * self.piece, self.piece)

    def number(self):
        return self.place.t // LINE * (self.place.cols // 2) + self.place.c // 2

    def scatter_pair(self):
        self.step = self.copies.start(self.grad.at[self.others], self.pair, self.partner)

    def scatter_plane(self):
        self.step.wait_recv()
        self.grad[self.mine] += self.pair[...]
        self.steps = [
            self.copies.start(self.grad.at[self.part(number)], self.pieces.at[k], device)
            for k, (number, device) in enumerate(self.plane(self.place))
        ]

    def sum_line(self):
        value = self.grad[self.part(self.number())]
        for k, step in enumerate(self.steps):
            step.wait_recv()
            value += self.pieces[k]
        spot = lax.rem(self.place.t, LINE)
        self.column[spot] = value
        self.steps = [
            self.copies.start(self.column.at[spot], self.column.at[spot], device)
            for device in self.line(self.place)
        ]

    def gather_plane(self):
        for step in self.steps:
            step.wait_recv()
        value = self.column[0]
        for k in range(1, LINE):
            value += self.column[k]
        own = self.part(self.number())
        self.halves[own] = value
        self.steps = [
            self.copies.start(self.halves.at[own], self.halves.at[own], device)
            for _, device in self.plane(self.place)
        ]

    def gather_pair(self):
        for step in self.steps:
            step.wait_recv()
        self.step = self.copies.start(
            self.halves.at[self.mine], self.halves.at[self.mine], self.partner
        )

    def result(self):
        self.step.wait_recv()
        return self.halves[...]

    @staticmethod
    def copies_needed(tiles, cols):
        return tiles * cols // (2 * LINE) * 2 + LINE - 1

    @staticmethod
    def scratch(rows, lanes, tiles, cols):
        half = rows // 2
        parts = tiles * cols // (2 * LINE)
        piece = half // parts
        return [
            pltpu.VMEM((half, lanes), f32),
            pltpu.VMEM((parts - 1, piece, lanes), f32),
            pltpu.VMEM((LINE, piece, lanes), f32),
            pltpu.VMEM((rows, lanes), f32),
        ]


def met(place):
    sides = [place.at(*way) for way in ((-1, 0), (1, 0), (0, -1), (0, 1))]
    return [device for _, device in ProbeSum.plane(place)] + ProbeSum.line(place) + sides


class Overlap:
    def __init__(self, place, copies, planes, grad, extended, buffers, final):
        self.place, self.copies, self.planes, self.final = place, copies, planes, final
        self.grad, self.extended = grad, extended
        self.from_left, self.from_up, self.from_right, self.from_down, self.from_corner = buffers
        count, tall, size = grad.shape[1:]
        self.last, height = count - 1, tall - size
        self.top, self.middle = pl.ds(0, size), pl.ds(size, height - size)
        self.below, self.own = pl.ds(height, size), pl.ds(0, height)
        self.block = [pl.ds(j * size, size) for j in range(self.last)]
        self.ups, self.downs = {}, {}

    def rows(self, j):
        up, down = self.place.at(-1, 0), self.place.at(1, 0)
        for p in self.planes:
            self.ups[p, j] = self.copies.start(
                self.grad.at[p, j, self.below], self.from_up.at[p, j], down
            )
            if not self.final:
                self.downs[p, j] = self.copies.start(
                    self.grad.at[p, j, self.top], self.from_down.at[p, j], up
                )

    def start(self):
        right = self.place.at(0, 1)
        self.edges = {
            (p, k): self.copies.start(
                self.grad.at[p, self.last, lines], self.from_left.at[p, lines], right
            )
            for p in self.planes
            for k, lines in enumerate((self.top, self.below))
        }
        for j in range(1, self.last):
            self.rows(j)

    def start_inner(self):
        right = self.place.at(0, 1)
        self.sides = [
            self.copies.start(
                self.grad.at[p, self.last, self.middle], self.from_left.at[p, self.middle], right
            )
            for p in self.planes
        ]

    def first(self):
        for p in self.planes:
            for k, lines in enumerate((self.top, self.below)):
                self.edges[p, k].wait_recv()
                self.grad[p, 0, lines] += self.from_left[p, lines]
        self.rows(0)

    def inner(self):
        left = self.place.at(0, -1)
        self.middles = []
        for p, side in zip(self.planes, self.sides):
            side.wait_recv()
            self.grad[p, 0, self.middle] += self.from_left[p, self.middle]
            if not self.final:
                self.middles.append(
                    self.copies.start(self.grad.at[p, 0, self.middle], self.from_right.at[p], left)
                )

    def corner(self):
        left = self.place.at(0, -1)
        self.corners = {}
        for p in self.planes:
            self.copies.sent(self.ups[p, 0])
            self.copies.sent(self.downs[p, 0])
            self.ups[p, 0].wait_recv()
            self.grad[p, 0, self.top] += self.from_up[p, 0]
            self.downs[p, 0].wait_recv()
            self.grad[p, 0, self.below] += self.from_down[p, 0]
            for k, lines in enumerate((self.top, self.below)):
                self.corners[p, k] = self.copies.start(
                    self.grad.at[p, 0, lines], self.from_corner.at[p, k], left
                )

    def update(self):
        grad, extended, last = self.grad, self.extended, self.last
        top, middle, below = self.top, self.middle, self.below
        for p in self.planes:
            extended[p % 2][p // 2, 0] -= STEP_OBJECT * grad[p, 0]
        for j in range(1, last):
            for p in self.planes:
                self.ups[p, j].wait_recv()
                self.downs[p, j].wait_recv()
                extended[p % 2][p // 2, j, middle] -= STEP_OBJECT * grad[p, j, middle]
                extended[p % 2][p // 2, j, top] -= STEP_OBJECT * (grad[p, j, top] + self.from_up[p, j])
                extended[p % 2][p // 2, j, below] -= STEP_OBJECT * (grad[p, j, below] + self.from_down[p, j])
        for p, copy in zip(self.planes, self.middles):
            copy.wait_recv()
            extended[p % 2][p // 2, last, middle] -= STEP_OBJECT * self.from_right[p]
            for k, lines in enumerate((top, below)):
                self.corners[p, k].wait_recv()
                extended[p % 2][p // 2, last, lines] -= STEP_OBJECT * self.from_corner[p, k]

    def keep(self, new_field):
        for j in range(self.last):
            for p in self.planes:
                new_field[p, :, self.block[j]] = (
                    self.extended[p % 2][p // 2, j, self.own] - STEP_OBJECT * self.grad[p, j, self.own]
                )

    def complete(self, new_field):
        for j in list(range(1, self.last)) + [0]:
            for p in self.planes:
                self.ups[p, j].wait_recv()
                new_field[p, self.top, self.block[j]] -= STEP_OBJECT * self.from_up[p, j]


SLICE_PLANES = ((0, 2), (1, 3))


def program_kernel(
    tiles,
    cols,
    rows,
    columns,
    counts,
    field,
    probe_hbm,
    measured_hbm,
    table_hbm,
    new_field,
    new_probe,
    object_first,
    object_second,
    grad,
    beam,
    grad_beam,
    measured,
    table,
    windows,
    spread,
    patches,
    from_left,
    from_up,
    from_right,
    from_down,
    from_corner,
    *rest,
):
    sums, (local_sem, send, recv) = rest[:-3], rest[-3:]
    sums = [sums[: len(sums) // 2], sums[len(sums) // 2 :]]
    extended = (object_first, object_second)
    planes, count, tall, size = grad.shape
    last = count - 1
    height = tall - size
    slots = measured.shape[0]
    step_probe = 1.0 / (slots * tiles * cols)
    top, below, own = pl.ds(0, size), pl.ds(height, size), pl.ds(0, height)
    block = [pl.ds(j * size, size) for j in range(last)]
    place = Place(tiles, cols)
    copies = Copies(send, recv)
    up, left = place.at(-1, 0), place.at(0, -1)

    loads = [
        (field.at[p, :, block[j]], extended[p % 2].at[p // 2, j, own])
        for p in range(planes)
        for j in range(last)
    ]
    loads += [(probe_hbm, beam), (table_hbm, table), (measured_hbm, measured)]
    loads = [
        pltpu.make_async_copy(source, target, local_sem.at[k])
        for k, (source, target) in enumerate(loads)
    ]
    for load in loads:
        load.start()
    greet(met(place))

    halos, sides, corners = {}, {}, {}

    def send_halo(p, j):
        halos[p, j] = copies.start(
            field.at[p, top, block[j]], extended[p % 2].at[p // 2, j, below], up
        )

    def pass_corners(which):
        for p in SLICE_PLANES[which]:
            halos[p, 0].wait_recv()
            corners[p] = copies.start(
                extended[p % 2].at[p // 2, 0, below], extended[p % 2].at[p // 2, last, below], left
            )

    def take_halo(which):
        for p in SLICE_PLANES[which]:
            for copy in [halos[p, j] for j in range(1, last)] + [sides[p], corners[p]]:
                copy.wait_recv()

    for which in SLICE_PLANES:
        for p in which:
            send_halo(p, 0)
        for p in which:
            sides[p] = copies.start(
                field.at[p, :, block[0]], extended[p % 2].at[p // 2, last, own], left
            )
        for j in range(1, last):
            for p in which:
                send_halo(p, j)
    pass_corners(0)
    for load in loads:
        load.wait()
    take_halo(0)

    refs = (rows, columns, counts, measured, extended, beam, table, grad, grad_beam)
    work = Positions(refs + (windows, spread, patches), size, slots)
    waiting = None
    for sweep in range(ITERS):
        final = sweep == ITERS - 1
        landed = (from_left.at[sweep], from_up.at[sweep], from_right, from_down, from_corner)
        zeroth, first = [
            Overlap(place, copies, which, grad, extended, landed, final) for which in SLICE_PLANES
        ]
        for step in range(work.groups):
            work.propagate(step)
            if step == 0 and sweep == 0:
                pass_corners(1)
        if sweep == 0:
            take_halo(1)
        else:
            waiting.update()
        copies.finish()
        grad_beam[...] = jnp.zeros_like(grad_beam)
        for step in range(work.groups):
            work.diffract(step)
        reduce = ProbeSum(place, copies, grad_beam, *sums[sweep])
        reduce.scatter_pair()
        for step in range(work.groups):
            work.place_patches(step, SLICE_PLANES[0])
            if step == 0:
                reduce.scatter_plane()
        zeroth.start()
        for step in range(work.groups):
            work.place_patches(step, SLICE_PLANES[1])
        first.start()
        zeroth.start_inner()
        first.start_inner()
        reduce.sum_line()
        zeroth.first()
        reduce.gather_plane()
        first.first()
        zeroth.inner()
        if final:
            first.inner()
            zeroth.keep(new_field)
            first.keep(new_field)
            zeroth.complete(new_field)
            reduce.gather_pair()
            first.complete(new_field)
            new_probe[...] = beam[...] - step_probe * reduce.result()
            copies.finish()
        else:
            zeroth.corner()
            first.inner()
            reduce.gather_pair()
            first.corner()
            zeroth.update()
            beam[...] -= step_probe * reduce.result()
            waiting = first


def local(table, tiles, cols, object_field, probe, row_offsets, col_offsets, counts, measured):
    size = probe.shape[-1]
    height, width = object_field.shape[2:]
    slots = row_offsets.shape[-1]
    field = object_field.reshape(4, height, width)
    flat = (probe.shape[0] * probe.shape[1] * size, size)
    planes, last, tall = 4, width // size, height + size
    needed = planes * (2 * last + 2) + ITERS * ProbeSum.copies_needed(tiles, cols)
    needed += planes * (3 + 2 * last + 1 + 2) + planes * (3 + last)
    work = ITERS * slots * probe.shape[1] * 8 * 3 * 2 * 256 * 256 * 128
    smem = pl.BlockSpec(memory_space=pltpu.SMEM)
    hbm = pl.BlockSpec(memory_space=pl.ANY)
    vmem = pl.BlockSpec(memory_space=pltpu.VMEM)
    new_field, new_probe = pl.pallas_call(
        functools.partial(program_kernel, tiles, cols),
        out_shape=[jax.ShapeDtypeStruct(field.shape, f32), jax.ShapeDtypeStruct(flat, f32)],
        in_specs=[smem] * 3 + [hbm] * 4,
        out_specs=[vmem] * 2,
        scratch_shapes=[
            pltpu.VMEM((planes // 2, last + 1, tall, size), f32),
            pltpu.VMEM((planes // 2, last + 1, tall, size), f32),
            pltpu.VMEM((planes, last + 1, tall, size), f32),
            pltpu.VMEM(flat, f32),
            pltpu.VMEM(flat, f32),
            pltpu.VMEM((slots, size, size), f32),
            pltpu.VMEM(table.shape, bf16),
            pltpu.VMEM((slots, 2, size, size), f32),
            pltpu.VMEM((slots, probe.shape[1], 2, size, size), f32),
            pltpu.VMEM((slots, planes, size, size), f32),
            pltpu.VMEM((ITERS, planes, tall, size), f32),
            pltpu.VMEM((ITERS, planes, last, size, size), f32),
            pltpu.VMEM((planes, height - size, size), f32),
            pltpu.VMEM((planes, last, size, size), f32),
            pltpu.VMEM((planes, 2, size, size), f32),
            *ProbeSum.scratch(*flat, tiles, cols),
            *ProbeSum.scratch(*flat, tiles, cols),
            pltpu.SemaphoreType.DMA((planes * last + 3,)),
            pltpu.SemaphoreType.DMA((needed,)),
            pltpu.SemaphoreType.DMA((needed,)),
        ],
        compiler_params=pltpu.CompilerParams(
            collective_id=0, has_side_effects=True, vmem_limit_bytes=VMEM_LIMIT
        ),
        cost_estimate=pl.CostEstimate(flops=work, bytes_accessed=5 * 2**20, transcendentals=0),
        name="ptychography",
    )(
        row_offsets.reshape(slots),
        col_offsets.reshape(slots),
        counts.reshape(1),
        field,
        probe.reshape(flat),
        measured.reshape(slots, size, size),
        table,
    )
    return new_field.reshape(object_field.shape), new_probe.reshape(probe.shape)


def solution(mesh):
    table = jnp.asarray(transform_tables(128))
    tiles, cols = mesh.shape["tiles"], mesh.shape["cols"]
    in_specs = (
        P(None, None, "tiles", "cols"),
        P(),
        P("tiles", "cols", None),
        P("tiles", "cols", None),
        P("tiles", "cols"),
        P("tiles", "cols", None, None, None),
    )
    out_specs = (P(None, None, "tiles", "cols"), P())
    body = functools.partial(local, table, tiles, cols)
    return jax.shard_map(body, mesh=mesh, in_specs=in_specs, out_specs=out_specs, check_vma=False)
```

```python
import functools
import math

import jax
import jax.numpy as jnp
import ml_dtypes
import numpy as np
from jax import lax
from jax.experimental import pallas as pl
from jax.experimental.pallas import tpu as pltpu
from jax.sharding import PartitionSpec as P

ITERS = 2
STEP_OBJECT = 0.25
f32, bf16 = jnp.float32, jnp.bfloat16
MESH = pl.DeviceIdType.MESH
VMEM_LIMIT = 56 * 2**20

A_PLUS, A_MINUS, F_PLUS, F_MINUS = 0, 2, 4, 6


def split_table(table):
    high = table.astype(np.float32).astype(ml_dtypes.bfloat16)
    low = (table - high.astype(np.float64)).astype(np.float32).astype(ml_dtypes.bfloat16)
    return [high, low]


def transform_tables(size):
    line = np.arange(size)
    dft = np.exp(-2j * np.pi * (np.outer(line, line) % size) / size) / math.sqrt(size)
    freq = np.where(line < size // 2, line, line - size)
    chirp = np.exp(-2j * np.pi * ((freq * freq) % (4 * size)) / (4 * size))
    propagator = np.conj(dft) @ (chirp[:, None] * dft)
    parts = []
    for matrix in (propagator, dft):
        real, imag = matrix.real, matrix.imag
        plus = np.block([[real, imag], [-imag, real]])
        parts += split_table(plus) + split_table(plus.T)
    return np.stack(parts)


def split(value):
    high = value.astype(bf16)
    return high, (value - high.astype(f32)).astype(bf16)


def product(first, second):
    dot = functools.partial(jnp.dot, preferred_element_type=f32)
    return dot(first[0], second[0]) + (dot(first[1], second[0]) + dot(first[0], second[1]))


def two_sided(groups, table, left, right):
    n = groups[0][0][0].shape[0]
    modes = range(len(groups[0]))
    middles = []
    for fields in groups:
        stacked = [jnp.concatenate(field, axis=0) for field in fields]
        middles.append(
            product((table[left], table[left + 1]), split(jnp.concatenate(stacked, axis=1)))
        )
    results = []
    for middle in middles:
        columns = [middle[:, n * m : n * m + n] for m in modes]
        beside = [jnp.concatenate([c[:n], c[n:]], axis=1) for c in columns]
        result = product(split(jnp.concatenate(beside, axis=0)), (table[right], table[right + 1]))
        rows = [result[n * m : n * m + n] for m in modes]
        results.append([(row[:, :n], row[:, n:]) for row in rows])
    return results


def times(a, b):
    return (a[0] * b[0] - a[1] * b[1], a[0] * b[1] + a[1] * b[0])


def conj_times(a, b):
    return (a[0] * b[0] + a[1] * b[1], a[0] * b[1] - a[1] * b[0])


def total(terms):
    real, imag = terms[0]
    for term in terms[1:]:
        real, imag = real + term[0], imag + term[1]
    return real, imag


GROUP = 4
LINE = 4


class Positions:
    def __init__(self, refs, n, slots):
        self.rows, self.cols, self.counts, self.measured = refs[:4]
        self.extended, self.beam, self.table, self.grad, self.grad_beam = refs[4:9]
        self.windows, self.spread, self.patches = refs[9:]
        self.n, self.slots = n, slots
        self.modes = range(self.spread.shape[1])
        self.groups = slots // GROUP

    def beams(self):
        n, part = self.n, len(self.modes) * self.n
        return [(self.beam[pl.ds(m * n, n)], self.beam[pl.ds(part + m * n, n)]) for m in self.modes]

    def spots(self, step):
        found = []
        for k in range(GROUP):
            slot = step * GROUP + k
            live = slot < self.counts[0]
            row = jnp.where(live, self.rows[slot], 0)
            col = jnp.where(live, self.cols[slot], 0)
            block = lax.shift_right_logical(col, 7)
            weight = jnp.where(live, 1.0, 0.0).astype(f32)
            found.append((slot, weight, row, block, col - block * self.n))
        return found

    def lane(self):
        return lax.broadcasted_iota(jnp.int32, (self.n, self.n), 1)

    def window(self, plane, spot):
        n = self.n
        _, _, row, block, shift = spot
        back = jnp.bitwise_and(n - shift, n - 1)
        near = pltpu.roll(self.extended[plane % 2][plane // 2, block, pl.ds(row, n), :], back, 1)
        far = pltpu.roll(self.extended[plane % 2][plane // 2, block + 1, pl.ds(row, n), :], back, 1)
        return jnp.where(self.lane() < n - shift, near, far)

    def propagate(self, step):
        spots, beams = self.spots(step), self.beams()
        first = [(self.window(0, s), self.window(2, s)) for s in spots]
        for spot, field in zip(spots, first):
            self.windows[spot[0], 0], self.windows[spot[0], 1] = field
        fields = [[times(b, field) for b in beams] for field in first]
        results = two_sided(fields, self.table, A_MINUS, A_PLUS)
        for spot, result in zip(spots, results):
            for m in self.modes:
                self.spread[spot[0], m, 0], self.spread[spot[0], m, 1] = result[m]

    def diffract(self, step):
        spots = self.spots(step)
        spread = [
            [(self.spread[s[0], m, 0], self.spread[s[0], m, 1]) for m in self.modes] for s in spots
        ]
        second = [(self.window(1, s), self.window(3, s)) for s in spots]
        leaving = [[times(o, x) for x in fields] for o, fields in zip(second, spread)]
        far = two_sided(leaving, self.table, F_MINUS, F_PLUS)
        residual = []
        for spot, fields in zip(spots, far):
            intensity = sum(y[0] * y[0] + y[1] * y[1] for y in fields)
            residual.append((intensity - self.measured[spot[0]]) * spot[1])
        weighed = [[(r * y[0], r * y[1]) for y in fields] for r, fields in zip(residual, far)]
        back = two_sided(weighed, self.table, F_PLUS, F_MINUS)
        patches = [
            total([conj_times(x, g) for x, g in zip(fields, backs)])
            for fields, backs in zip(spread, back)
        ]
        for spot, patch in zip(spots, patches):
            self.patches[spot[0], 1], self.patches[spot[0], 3] = patch
        entering = [[conj_times(o, g) for g in backs] for o, backs in zip(second, back)]
        back = two_sided(entering, self.table, A_PLUS, A_MINUS)
        beams = self.beams()
        n, part = self.n, len(self.modes) * self.n
        first = [(self.windows[s[0], 0], self.windows[s[0], 1]) for s in spots]
        for m in self.modes:
            terms = total([conj_times(o, backs[m]) for o, backs in zip(first, back)])
            for term, start in zip(terms, (m * n, part + m * n)):
                self.grad_beam[pl.ds(start, n)] += term
        for spot, backs in zip(spots, back):
            patch = total([conj_times(b, g) for b, g in zip(beams, backs)])
            self.patches[spot[0], 0], self.patches[spot[0], 2] = patch

    def place_patches(self, step, planes):
        spots = self.spots(step)
        patches = [[self.patches[s[0], p] for p in planes] for s in spots]
        self.put(spots, patches, planes, step == 0)

    def put(self, spots, patches, planes, fresh):
        n = self.n
        count, tall = self.grad.shape[1:3]
        offset = lax.broadcasted_iota(jnp.int32, (tall, n), 0) - lax.broadcasted_iota(
            jnp.int32, (tall, n), 1
        )
        ones, pieces = [], [[] for _ in range(count)]
        for (_, _, row, block, shift), patch in zip(spots, patches):
            ones += [jnp.where(offset == row, 1.0, 0.0).astype(bf16)] * 2
            kept = self.lane() >= shift
            beside = [[] for _ in range(count)]
            for value in patch:
                moved = pltpu.roll(value, shift, 1)
                near, over = jnp.where(kept, moved, 0.0), jnp.where(kept, 0.0, moved)
                for b in range(count):
                    if b == 0:
                        placed = jnp.where(block == 0, near, 0.0)
                    elif b == count - 1:
                        placed = jnp.where(block == b - 1, over, 0.0)
                    else:
                        placed = jnp.where(block == b, near, jnp.where(block == b - 1, over, 0.0))
                    beside[b].append(placed)
            for b in range(count):
                pieces[b] += split(jnp.concatenate(beside[b], axis=1))
        ones = jnp.concatenate(ones, axis=1)
        for b in range(count):
            sums = jnp.dot(ones, jnp.concatenate(pieces[b], axis=0), preferred_element_type=f32)
            for k, p in enumerate(planes):
                if fresh:
                    self.grad[p, b] = sums[:, k * n : k * n + n]
                else:
                    self.grad[p, b] += sums[:, k * n : k * n + n]


class Place:
    def __init__(self, tiles, cols):
        self.tiles, self.cols = tiles, cols
        self.t, self.c = lax.axis_index("tiles"), lax.axis_index("cols")

    def at(self, down, right):
        return (
            lax.rem(self.t + (down + self.tiles), self.tiles),
            lax.rem(self.c + (right + self.cols), self.cols),
        )


def greet(devices):
    barrier = pltpu.get_barrier_semaphore()
    for device in devices:
        pl.semaphore_signal(barrier, inc=1, device_id=device, device_id_type=MESH)
    pl.semaphore_wait(barrier, len(devices))


class Copies:
    def __init__(self, send, recv):
        self.send, self.recv, self.used, self.started = send, recv, 0, []

    def start(self, source, target, device):
        k = self.used
        self.used += 1
        copy = pltpu.make_async_remote_copy(
            src_ref=source,
            dst_ref=target,
            send_sem=self.send.at[k],
            recv_sem=self.recv.at[k],
            device_id=device,
            device_id_type=MESH,
        )
        copy.start()
        self.started.append(copy)
        return copy

    def sent(self, copy):
        copy.wait_send()
        self.started = [other for other in self.started if other is not copy]

    def finish(self):
        for copy in self.started:
            copy.wait_send()
        self.started = []


class ProbeSum:
    def __init__(self, place, copies, grad, pair, pieces, column, halves):
        self.place, self.copies = place, copies
        self.grad, self.pair, self.pieces, self.column, self.halves = grad, pair, pieces, column, halves
        self.half = grad.shape[0] // 2
        self.piece = self.half // (pieces.shape[0] + 1)
        self.core = lax.rem(place.c, 2)
        self.partner = (place.t, place.c + 1 - 2 * self.core)
        self.mine = pl.ds(self.core * self.half, self.half)
        self.others = pl.ds((1 - self.core) * self.half, self.half)

    @staticmethod
    def plane(place):
        found = []
        chips = place.cols // 2
        for k in range(1, place.tiles // LINE * chips):
            t, c = place.at(k // chips * LINE, 2 * (k % chips))
            found.append((t // LINE * chips + c // 2, (t, c)))
        return found

    @staticmethod
    def line(place):
        start = place.t // LINE * LINE
        return [(start + lax.rem(place.t + k, LINE), place.c) for k in range(1, LINE)]

    def part(self, number):
        return pl.ds(self.core * self.half + number * self.piece, self.piece)

    def number(self):
        return self.place.t // LINE * (self.place.cols // 2) + self.place.c // 2

    def scatter_pair(self):
        self.step = self.copies.start(self.grad.at[self.others], self.pair, self.partner)

    def scatter_plane(self):
        self.step.wait_recv()
        self.grad[self.mine] += self.pair[...]
        self.steps = [
            self.copies.start(self.grad.at[self.part(number)], self.pieces.at[k], device)
            for k, (number, device) in enumerate(self.plane(self.place))
        ]

    def sum_line(self):
        value = self.grad[self.part(self.number())]
        for k, step in enumerate(self.steps):
            step.wait_recv()
            value += self.pieces[k]
        spot = lax.rem(self.place.t, LINE)
        self.column[spot] = value
        self.steps = [
            self.copies.start(self.column.at[spot], self.column.at[spot], device)
            for device in self.line(self.place)
        ]

    def gather_plane(self):
        for step in self.steps:
            step.wait_recv()
        value = self.column[0]
        for k in range(1, LINE):
            value += self.column[k]
        own = self.part(self.number())
        self.halves[own] = value
        self.steps = [
            self.copies.start(self.halves.at[own], self.halves.at[own], device)
            for _, device in self.plane(self.place)
        ]

    def gather_pair(self):
        for step in self.steps:
            step.wait_recv()
        self.step = self.copies.start(
            self.halves.at[self.mine], self.halves.at[self.mine], self.partner
        )

    def result(self):
        self.step.wait_recv()
        return self.halves[...]

    @staticmethod
    def copies_needed(tiles, cols):
        return tiles * cols // (2 * LINE) * 2 + LINE - 1

    @staticmethod
    def scratch(rows, lanes, tiles, cols):
        half = rows // 2
        parts = tiles * cols // (2 * LINE)
        piece = half // parts
        return [
            pltpu.VMEM((half, lanes), f32),
            pltpu.VMEM((parts - 1, piece, lanes), f32),
            pltpu.VMEM((LINE, piece, lanes), f32),
            pltpu.VMEM((rows, lanes), f32),
        ]


def met(place):
    sides = [place.at(*way) for way in ((-1, 0), (1, 0), (0, -1), (0, 1))]
    return [device for _, device in ProbeSum.plane(place)] + ProbeSum.line(place) + sides


class Overlap:
    def __init__(self, place, copies, planes, grad, extended, buffers, final):
        self.place, self.copies, self.planes, self.final = place, copies, planes, final
        self.grad, self.extended = grad, extended
        self.from_left, self.from_up, self.from_right, self.from_down, self.from_corner = buffers
        count, tall, size = grad.shape[1:]
        self.last, height = count - 1, tall - size
        self.top, self.middle = pl.ds(0, size), pl.ds(size, height - size)
        self.below, self.own = pl.ds(height, size), pl.ds(0, height)
        self.block = [pl.ds(j * size, size) for j in range(self.last)]
        self.ups, self.downs = {}, {}

    def rows(self, j):
        up, down = self.place.at(-1, 0), self.place.at(1, 0)
        for p in self.planes:
            self.ups[p, j] = self.copies.start(
                self.grad.at[p, j, self.below], self.from_up.at[p, j], down
            )
            if not self.final:
                self.downs[p, j] = self.copies.start(
                    self.grad.at[p, j, self.top], self.from_down.at[p, j], up
                )

    def start(self):
        right = self.place.at(0, 1)
        self.edges = {
            (p, k): self.copies.start(
                self.grad.at[p, self.last, lines], self.from_left.at[p, lines], right
            )
            for p in self.planes
            for k, lines in enumerate((self.top, self.below))
        }
        for j in range(1, self.last):
            self.rows(j)

    def start_inner(self):
        right = self.place.at(0, 1)
        self.sides = [
            self.copies.start(
                self.grad.at[p, self.last, self.middle], self.from_left.at[p, self.middle], right
            )
            for p in self.planes
        ]

    def first(self):
        for p in self.planes:
            for k, lines in enumerate((self.top, self.below)):
                self.edges[p, k].wait_recv()
                self.grad[p, 0, lines] += self.from_left[p, lines]
        self.rows(0)

    def inner(self):
        left = self.place.at(0, -1)
        self.middles = []
        for p, side in zip(self.planes, self.sides):
            side.wait_recv()
            self.grad[p, 0, self.middle] += self.from_left[p, self.middle]
            if not self.final:
                self.middles.append(
                    self.copies.start(self.grad.at[p, 0, self.middle], self.from_right.at[p], left)
                )

    def corner(self):
        left = self.place.at(0, -1)
        self.corners = {}
        for p in self.planes:
            self.copies.sent(self.ups[p, 0])
            self.copies.sent(self.downs[p, 0])
            self.ups[p, 0].wait_recv()
            self.grad[p, 0, self.top] += self.from_up[p, 0]
            self.downs[p, 0].wait_recv()
            self.grad[p, 0, self.below] += self.from_down[p, 0]
            for k, lines in enumerate((self.top, self.below)):
                self.corners[p, k] = self.copies.start(
                    self.grad.at[p, 0, lines], self.from_corner.at[p, k], left
                )

    def update(self):
        grad, extended, last = self.grad, self.extended, self.last
        top, middle, below = self.top, self.middle, self.below
        for p in self.planes:
            extended[p % 2][p // 2, 0] -= STEP_OBJECT * grad[p, 0]
        for j in range(1, last):
            for p in self.planes:
                self.ups[p, j].wait_recv()
                self.downs[p, j].wait_recv()
                extended[p % 2][p // 2, j, middle] -= STEP_OBJECT * grad[p, j, middle]
                extended[p % 2][p // 2, j, top] -= STEP_OBJECT * (grad[p, j, top] + self.from_up[p, j])
                extended[p % 2][p // 2, j, below] -= STEP_OBJECT * (grad[p, j, below] + self.from_down[p, j])
        for p, copy in zip(self.planes, self.middles):
            copy.wait_recv()
            extended[p % 2][p // 2, last, middle] -= STEP_OBJECT * self.from_right[p]
            for k, lines in enumerate((top, below)):
                self.corners[p, k].wait_recv()
                extended[p % 2][p // 2, last, lines] -= STEP_OBJECT * self.from_corner[p, k]

    def keep(self, new_field):
        for j in range(self.last):
            for p in self.planes:
                new_field[p, :, self.block[j]] = (
                    self.extended[p % 2][p // 2, j, self.own] - STEP_OBJECT * self.grad[p, j, self.own]
                )

    def complete(self, new_field):
        for j in list(range(1, self.last)) + [0]:
            for p in self.planes:
                self.ups[p, j].wait_recv()
                new_field[p, self.top, self.block[j]] -= STEP_OBJECT * self.from_up[p, j]


SLICE_PLANES = ((0, 2), (1, 3))


def program_kernel(
    tiles,
    cols,
    rows,
    columns,
    counts,
    field,
    probe_hbm,
    measured_hbm,
    table_hbm,
    new_field,
    new_probe,
    object_first,
    object_second,
    grad,
    beam,
    grad_beam,
    measured,
    table,
    windows,
    spread,
    patches,
    from_left,
    from_up,
    from_right,
    from_down,
    from_corner,
    *rest,
):
    sums, (local_sem, send, recv) = rest[:-3], rest[-3:]
    sums = [sums[: len(sums) // 2], sums[len(sums) // 2 :]]
    extended = (object_first, object_second)
    planes, count, tall, size = grad.shape
    last = count - 1
    height = tall - size
    slots = measured.shape[0]
    step_probe = 1.0 / (slots * tiles * cols)
    top, below, own = pl.ds(0, size), pl.ds(height, size), pl.ds(0, height)
    block = [pl.ds(j * size, size) for j in range(last)]
    place = Place(tiles, cols)
    copies = Copies(send, recv)
    up, left = place.at(-1, 0), place.at(0, -1)

    loads = [
        (field.at[p, :, block[j]], extended[p % 2].at[p // 2, j, own])
        for p in range(planes)
        for j in range(last)
    ]
    loads += [(probe_hbm, beam), (table_hbm, table), (measured_hbm, measured)]
    loads = [
        pltpu.make_async_copy(source, target, local_sem.at[k])
        for k, (source, target) in enumerate(loads)
    ]
    for load in loads:
        load.start()
    greet(met(place))

    halos, sides, corners = {}, {}, {}

    def send_halo(p, j):
        halos[p, j] = copies.start(
            field.at[p, top, block[j]], extended[p % 2].at[p // 2, j, below], up
        )

    def pass_corners(which):
        for p in SLICE_PLANES[which]:
            halos[p, 0].wait_recv()
            corners[p] = copies.start(
                extended[p % 2].at[p // 2, 0, below], extended[p % 2].at[p // 2, last, below], left
            )

    def take_halo(which):
        for p in SLICE_PLANES[which]:
            for copy in [halos[p, j] for j in range(1, last)] + [sides[p], corners[p]]:
                copy.wait_recv()

    for which in SLICE_PLANES:
        for p in which:
            send_halo(p, 0)
        for p in which:
            sides[p] = copies.start(
                field.at[p, :, block[0]], extended[p % 2].at[p // 2, last, own], left
            )
        for j in range(1, last):
            for p in which:
                send_halo(p, j)
    pass_corners(0)
    for load in loads:
        load.wait()
    take_halo(0)

    refs = (rows, columns, counts, measured, extended, beam, table, grad, grad_beam)
    work = Positions(refs + (windows, spread, patches), size, slots)
    waiting = None
    for sweep in range(ITERS):
        final = sweep == ITERS - 1
        landed = (from_left.at[sweep], from_up.at[sweep], from_right, from_down, from_corner)
        zeroth, first = [
            Overlap(place, copies, which, grad, extended, landed, final) for which in SLICE_PLANES
        ]
        for step in range(work.groups):
            work.propagate(step)
            if step == 0 and sweep == 0:
                pass_corners(1)
        if sweep == 0:
            take_halo(1)
        else:
            waiting.update()
        copies.finish()
        grad_beam[...] = jnp.zeros_like(grad_beam)
        lax.fori_loop(0, work.groups, lambda step, carry: (work.diffract(step), carry)[1], 0)
        reduce = ProbeSum(place, copies, grad_beam, *sums[sweep])
        reduce.scatter_pair()
        for step in range(work.groups):
            work.place_patches(step, SLICE_PLANES[0])
            if step == 0:
                reduce.scatter_plane()
        zeroth.start()
        for step in range(work.groups):
            work.place_patches(step, SLICE_PLANES[1])
        first.start()
        zeroth.start_inner()
        first.start_inner()
        reduce.sum_line()
        zeroth.first()
        reduce.gather_plane()
        first.first()
        zeroth.inner()
        if final:
            first.inner()
            zeroth.keep(new_field)
            first.keep(new_field)
            zeroth.complete(new_field)
            reduce.gather_pair()
            first.complete(new_field)
            new_probe[...] = beam[...] - step_probe * reduce.result()
            copies.finish()
        else:
            zeroth.corner()
            first.inner()
            reduce.gather_pair()
            first.corner()
            zeroth.update()
            beam[...] -= step_probe * reduce.result()
            waiting = first


def local(table, tiles, cols, object_field, probe, row_offsets, col_offsets, counts, measured):
    size = probe.shape[-1]
    height, width = object_field.shape[2:]
    slots = row_offsets.shape[-1]
    field = object_field.reshape(4, height, width)
    flat = (probe.shape[0] * probe.shape[1] * size, size)
    planes, last, tall = 4, width // size, height + size
    needed = planes * (2 * last + 2) + ITERS * ProbeSum.copies_needed(tiles, cols)
    needed += planes * (3 + 2 * last + 1 + 2) + planes * (3 + last)
    work = ITERS * slots * probe.shape[1] * 8 * 3 * 2 * 256 * 256 * 128
    smem = pl.BlockSpec(memory_space=pltpu.SMEM)
    hbm = pl.BlockSpec(memory_space=pl.ANY)
    vmem = pl.BlockSpec(memory_space=pltpu.VMEM)
    new_field, new_probe = pl.pallas_call(
        functools.partial(program_kernel, tiles, cols),
        out_shape=[jax.ShapeDtypeStruct(field.shape, f32), jax.ShapeDtypeStruct(flat, f32)],
        in_specs=[smem] * 3 + [hbm] * 4,
        out_specs=[vmem] * 2,
        scratch_shapes=[
            pltpu.VMEM((planes // 2, last + 1, tall, size), f32),
            pltpu.VMEM((planes // 2, last + 1, tall, size), f32),
            pltpu.VMEM((planes, last + 1, tall, size), f32),
            pltpu.VMEM(flat, f32),
            pltpu.VMEM(flat, f32),
            pltpu.VMEM((slots, size, size), f32),
            pltpu.VMEM(table.shape, bf16),
            pltpu.VMEM((slots, 2, size, size), f32),
            pltpu.VMEM((slots, probe.shape[1], 2, size, size), f32),
            pltpu.VMEM((slots, planes, size, size), f32),
            pltpu.VMEM((ITERS, planes, tall, size), f32),
            pltpu.VMEM((ITERS, planes, last, size, size), f32),
            pltpu.VMEM((planes, height - size, size), f32),
            pltpu.VMEM((planes, last, size, size), f32),
            pltpu.VMEM((planes, 2, size, size), f32),
            *ProbeSum.scratch(*flat, tiles, cols),
            *ProbeSum.scratch(*flat, tiles, cols),
            pltpu.SemaphoreType.DMA((planes * last + 3,)),
            pltpu.SemaphoreType.DMA((needed,)),
            pltpu.SemaphoreType.DMA((needed,)),
        ],
        compiler_params=pltpu.CompilerParams(
            collective_id=0, has_side_effects=True, vmem_limit_bytes=VMEM_LIMIT
        ),
        cost_estimate=pl.CostEstimate(flops=work, bytes_accessed=5 * 2**20, transcendentals=0),
        name="ptychography",
    )(
        row_offsets.reshape(slots),
        col_offsets.reshape(slots),
        counts.reshape(1),
        field,
        probe.reshape(flat),
        measured.reshape(slots, size, size),
        table,
    )
    return new_field.reshape(object_field.shape), new_probe.reshape(probe.shape)


def solution(mesh):
    table = jnp.asarray(transform_tables(128))
    tiles, cols = mesh.shape["tiles"], mesh.shape["cols"]
    in_specs = (
        P(None, None, "tiles", "cols"),
        P(),
        P("tiles", "cols", None),
        P("tiles", "cols", None),
        P("tiles", "cols"),
        P("tiles", "cols", None, None, None),
    )
    out_specs = (P(None, None, "tiles", "cols"), P())
    body = functools.partial(local, table, tiles, cols)
    return jax.shard_map(body, mesh=mesh, in_specs=in_specs, out_specs=out_specs, check_vma=False)
```

```python
import functools
import math

import jax
import jax.numpy as jnp
import ml_dtypes
import numpy as np
from jax import lax
from jax.experimental import pallas as pl
from jax.experimental.pallas import tpu as pltpu
from jax.sharding import PartitionSpec as P

ITERS = 2
STEP_OBJECT = 0.25
f32, bf16 = jnp.float32, jnp.bfloat16
MESH = pl.DeviceIdType.MESH
VMEM_LIMIT = 56 * 2**20

A_PLUS, A_MINUS, F_PLUS, F_MINUS = 0, 2, 4, 6


def split_table(table):
    high = table.astype(np.float32).astype(ml_dtypes.bfloat16)
    low = (table - high.astype(np.float64)).astype(np.float32).astype(ml_dtypes.bfloat16)
    return [high, low]


def transform_tables(size):
    line = np.arange(size)
    dft = np.exp(-2j * np.pi * (np.outer(line, line) % size) / size) / math.sqrt(size)
    freq = np.where(line < size // 2, line, line - size)
    chirp = np.exp(-2j * np.pi * ((freq * freq) % (4 * size)) / (4 * size))
    propagator = np.conj(dft) @ (chirp[:, None] * dft)
    parts = []
    for matrix in (propagator, dft):
        real, imag = matrix.real, matrix.imag
        plus = np.block([[real, imag], [-imag, real]])
        parts += split_table(plus) + split_table(plus.T)
    return np.stack(parts)


def split(value):
    high = value.astype(bf16)
    return high, (value - high.astype(f32)).astype(bf16)


def product(first, second):
    dot = functools.partial(jnp.dot, preferred_element_type=f32)
    return dot(first[0], second[0]) + (dot(first[1], second[0]) + dot(first[0], second[1]))


def two_sided(groups, table, left, right):
    n = groups[0][0][0].shape[0]
    modes = range(len(groups[0]))
    middles = []
    for fields in groups:
        stacked = [jnp.concatenate(field, axis=0) for field in fields]
        middles.append(
            product((table[left], table[left + 1]), split(jnp.concatenate(stacked, axis=1)))
        )
    results = []
    for middle in middles:
        columns = [middle[:, n * m : n * m + n] for m in modes]
        beside = [jnp.concatenate([c[:n], c[n:]], axis=1) for c in columns]
        result = product(split(jnp.concatenate(beside, axis=0)), (table[right], table[right + 1]))
        rows = [result[n * m : n * m + n] for m in modes]
        results.append([(row[:, :n], row[:, n:]) for row in rows])
    return results


def times(a, b):
    return (a[0] * b[0] - a[1] * b[1], a[0] * b[1] + a[1] * b[0])


def conj_times(a, b):
    return (a[0] * b[0] + a[1] * b[1], a[0] * b[1] - a[1] * b[0])


def total(terms):
    real, imag = terms[0]
    for term in terms[1:]:
        real, imag = real + term[0], imag + term[1]
    return real, imag


GROUP = 4
LINE = 4


class Positions:
    def __init__(self, refs, n, slots):
        self.rows, self.cols, self.counts, self.measured = refs[:4]
        self.extended, self.beam, self.table, self.grad, self.grad_beam = refs[4:9]
        self.windows, self.spread, self.patches = refs[9:]
        self.n, self.slots = n, slots
        self.modes = range(self.spread.shape[1])
        self.groups = slots // GROUP

    def beams(self):
        n, part = self.n, len(self.modes) * self.n
        return [(self.beam[pl.ds(m * n, n)], self.beam[pl.ds(part + m * n, n)]) for m in self.modes]

    def spots(self, step):
        found = []
        for k in range(GROUP):
            slot = step * GROUP + k
            live = slot < self.counts[0]
            row = jnp.where(live, self.rows[slot], 0)
            col = jnp.where(live, self.cols[slot], 0)
            block = lax.shift_right_logical(col, 7)
            weight = jnp.where(live, 1.0, 0.0).astype(f32)
            found.append((slot, weight, row, block, col - block * self.n))
        return found

    def lane(self):
        return lax.broadcasted_iota(jnp.int32, (self.n, self.n), 1)

    def window(self, plane, spot):
        n = self.n
        _, _, row, block, shift = spot
        back = jnp.bitwise_and(n - shift, n - 1)
        near = pltpu.roll(self.extended[plane % 2][plane // 2, block, pl.ds(row, n), :], back, 1)
        far = pltpu.roll(self.extended[plane % 2][plane // 2, block + 1, pl.ds(row, n), :], back, 1)
        return jnp.where(self.lane() < n - shift, near, far)

    def propagate(self, step):
        spots, beams = self.spots(step), self.beams()
        first = [(self.window(0, s), self.window(2, s)) for s in spots]
        for spot, field in zip(spots, first):
            self.windows[spot[0], 0], self.windows[spot[0], 1] = field
        fields = [[times(b, field) for b in beams] for field in first]
        results = two_sided(fields, self.table, A_MINUS, A_PLUS)
        for spot, result in zip(spots, results):
            for m in self.modes:
                self.spread[spot[0], m, 0], self.spread[spot[0], m, 1] = result[m]

    def diffract(self, step):
        spots = self.spots(step)
        spread = [
            [(self.spread[s[0], m, 0], self.spread[s[0], m, 1]) for m in self.modes] for s in spots
        ]
        second = [(self.window(1, s), self.window(3, s)) for s in spots]
        leaving = [[times(o, x) for x in fields] for o, fields in zip(second, spread)]
        far = two_sided(leaving, self.table, F_MINUS, F_PLUS)
        residual = []
        for spot, fields in zip(spots, far):
            intensity = sum(y[0] * y[0] + y[1] * y[1] for y in fields)
            residual.append((intensity - self.measured[spot[0]]) * spot[1])
        weighed = [[(r * y[0], r * y[1]) for y in fields] for r, fields in zip(residual, far)]
        back = two_sided(weighed, self.table, F_PLUS, F_MINUS)
        patches = [
            total([conj_times(x, g) for x, g in zip(fields, backs)])
            for fields, backs in zip(spread, back)
        ]
        for spot, patch in zip(spots, patches):
            self.patches[spot[0], 1], self.patches[spot[0], 3] = patch
        entering = [[conj_times(o, g) for g in backs] for o, backs in zip(second, back)]
        back = two_sided(entering, self.table, A_PLUS, A_MINUS)
        beams = self.beams()
        n, part = self.n, len(self.modes) * self.n
        first = [(self.windows[s[0], 0], self.windows[s[0], 1]) for s in spots]
        for m in self.modes:
            terms = total([conj_times(o, backs[m]) for o, backs in zip(first, back)])
            for term, start in zip(terms, (m * n, part + m * n)):
                self.grad_beam[pl.ds(start, n)] += term
        for spot, backs in zip(spots, back):
            patch = total([conj_times(b, g) for b, g in zip(beams, backs)])
            self.patches[spot[0], 0], self.patches[spot[0], 2] = patch

    def place_patches(self, step, planes):
        spots = self.spots(step)
        patches = [[self.patches[s[0], p] for p in planes] for s in spots]
        self.put(spots, patches, planes, isinstance(step, int) and step == 0)

    def put(self, spots, patches, planes, fresh):
        n = self.n
        count, tall = self.grad.shape[1:3]
        offset = lax.broadcasted_iota(jnp.int32, (tall, n), 0) - lax.broadcasted_iota(
            jnp.int32, (tall, n), 1
        )
        ones, pieces = [], [[] for _ in range(count)]
        for (_, _, row, block, shift), patch in zip(spots, patches):
            ones += [jnp.where(offset == row, 1.0, 0.0).astype(bf16)] * 2
            kept = self.lane() >= shift
            beside = [[] for _ in range(count)]
            for value in patch:
                moved = pltpu.roll(value, shift, 1)
                near, over = jnp.where(kept, moved, 0.0), jnp.where(kept, 0.0, moved)
                for b in range(count):
                    if b == 0:
                        placed = jnp.where(block == 0, near, 0.0)
                    elif b == count - 1:
                        placed = jnp.where(block == b - 1, over, 0.0)
                    else:
                        placed = jnp.where(block == b, near, jnp.where(block == b - 1, over, 0.0))
                    beside[b].append(placed)
            for b in range(count):
                pieces[b] += split(jnp.concatenate(beside[b], axis=1))
        ones = jnp.concatenate(ones, axis=1)
        for b in range(count):
            sums = jnp.dot(ones, jnp.concatenate(pieces[b], axis=0), preferred_element_type=f32)
            for k, p in enumerate(planes):
                if fresh:
                    self.grad[p, b] = sums[:, k * n : k * n + n]
                else:
                    self.grad[p, b] += sums[:, k * n : k * n + n]


class Place:
    def __init__(self, tiles, cols):
        self.tiles, self.cols = tiles, cols
        self.t, self.c = lax.axis_index("tiles"), lax.axis_index("cols")

    def at(self, down, right):
        return (
            lax.rem(self.t + (down + self.tiles), self.tiles),
            lax.rem(self.c + (right + self.cols), self.cols),
        )


def greet(devices):
    barrier = pltpu.get_barrier_semaphore()
    for device in devices:
        pl.semaphore_signal(barrier, inc=1, device_id=device, device_id_type=MESH)
    pl.semaphore_wait(barrier, len(devices))


class Copies:
    def __init__(self, send, recv):
        self.send, self.recv, self.used, self.started = send, recv, 0, []

    def start(self, source, target, device):
        k = self.used
        self.used += 1
        copy = pltpu.make_async_remote_copy(
            src_ref=source,
            dst_ref=target,
            send_sem=self.send.at[k],
            recv_sem=self.recv.at[k],
            device_id=device,
            device_id_type=MESH,
        )
        copy.start()
        self.started.append(copy)
        return copy

    def sent(self, copy):
        copy.wait_send()
        self.started = [other for other in self.started if other is not copy]

    def finish(self):
        for copy in self.started:
            copy.wait_send()
        self.started = []


class ProbeSum:
    def __init__(self, place, copies, grad, pair, pieces, column, halves):
        self.place, self.copies = place, copies
        self.grad, self.pair, self.pieces, self.column, self.halves = grad, pair, pieces, column, halves
        self.half = grad.shape[0] // 2
        self.piece = self.half // (pieces.shape[0] + 1)
        self.core = lax.rem(place.c, 2)
        self.partner = (place.t, place.c + 1 - 2 * self.core)
        self.mine = pl.ds(self.core * self.half, self.half)
        self.others = pl.ds((1 - self.core) * self.half, self.half)

    @staticmethod
    def plane(place):
        found = []
        chips = place.cols // 2
        for k in range(1, place.tiles // LINE * chips):
            t, c = place.at(k // chips * LINE, 2 * (k % chips))
            found.append((t // LINE * chips + c // 2, (t, c)))
        return found

    @staticmethod
    def line(place):
        start = place.t // LINE * LINE
        return [(start + lax.rem(place.t + k, LINE), place.c) for k in range(1, LINE)]

    def part(self, number):
        return pl.ds(self.core * self.half + number * self.piece, self.piece)

    def number(self):
        return self.place.t // LINE * (self.place.cols // 2) + self.place.c // 2

    def scatter_pair(self):
        self.step = self.copies.start(self.grad.at[self.others], self.pair, self.partner)

    def scatter_plane(self):
        self.step.wait_recv()
        self.grad[self.mine] += self.pair[...]
        self.steps = [
            self.copies.start(self.grad.at[self.part(number)], self.pieces.at[k], device)
            for k, (number, device) in enumerate(self.plane(self.place))
        ]

    def sum_line(self):
        value = self.grad[self.part(self.number())]
        for k, step in enumerate(self.steps):
            step.wait_recv()
            value += self.pieces[k]
        spot = lax.rem(self.place.t, LINE)
        self.column[spot] = value
        self.steps = [
            self.copies.start(self.column.at[spot], self.column.at[spot], device)
            for device in self.line(self.place)
        ]

    def gather_plane(self):
        for step in self.steps:
            step.wait_recv()
        value = self.column[0]
        for k in range(1, LINE):
            value += self.column[k]
        own = self.part(self.number())
        self.halves[own] = value
        self.steps = [
            self.copies.start(self.halves.at[own], self.halves.at[own], device)
            for _, device in self.plane(self.place)
        ]

    def gather_pair(self):
        for step in self.steps:
            step.wait_recv()
        self.step = self.copies.start(
            self.halves.at[self.mine], self.halves.at[self.mine], self.partner
        )

    def result(self):
        self.step.wait_recv()
        return self.halves[...]

    @staticmethod
    def copies_needed(tiles, cols):
        return tiles * cols // (2 * LINE) * 2 + LINE - 1

    @staticmethod
    def scratch(rows, lanes, tiles, cols):
        half = rows // 2
        parts = tiles * cols // (2 * LINE)
        piece = half // parts
        return [
            pltpu.VMEM((half, lanes), f32),
            pltpu.VMEM((parts - 1, piece, lanes), f32),
            pltpu.VMEM((LINE, piece, lanes), f32),
            pltpu.VMEM((rows, lanes), f32),
        ]


def met(place):
    sides = [place.at(*way) for way in ((-1, 0), (1, 0), (0, -1), (0, 1))]
    return [device for _, device in ProbeSum.plane(place)] + ProbeSum.line(place) + sides


class Overlap:
    def __init__(self, place, copies, planes, grad, extended, buffers, final):
        self.place, self.copies, self.planes, self.final = place, copies, planes, final
        self.grad, self.extended = grad, extended
        self.from_left, self.from_up, self.from_right, self.from_down, self.from_corner = buffers
        count, tall, size = grad.shape[1:]
        self.last, height = count - 1, tall - size
        self.top, self.middle = pl.ds(0, size), pl.ds(size, height - size)
        self.below, self.own = pl.ds(height, size), pl.ds(0, height)
        self.block = [pl.ds(j * size, size) for j in range(self.last)]
        self.ups, self.downs = {}, {}

    def rows(self, j):
        up, down = self.place.at(-1, 0), self.place.at(1, 0)
        for p in self.planes:
            self.ups[p, j] = self.copies.start(
                self.grad.at[p, j, self.below], self.from_up.at[p, j], down
            )
            if not self.final:
                self.downs[p, j] = self.copies.start(
                    self.grad.at[p, j, self.top], self.from_down.at[p, j], up
                )

    def start(self):
        right = self.place.at(0, 1)
        self.edges = {
            (p, k): self.copies.start(
                self.grad.at[p, self.last, lines], self.from_left.at[p, lines], right
            )
            for p in self.planes
            for k, lines in enumerate((self.top, self.below))
        }
        for j in range(1, self.last):
            self.rows(j)

    def start_inner(self):
        right = self.place.at(0, 1)
        self.sides = [
            self.copies.start(
                self.grad.at[p, self.last, self.middle], self.from_left.at[p, self.middle], right
            )
            for p in self.planes
        ]

    def first(self):
        for p in self.planes:
            for k, lines in enumerate((self.top, self.below)):
                self.edges[p, k].wait_recv()
                self.grad[p, 0, lines] += self.from_left[p, lines]
        self.rows(0)

    def inner(self):
        left = self.place.at(0, -1)
        self.middles = []
        for p, side in zip(self.planes, self.sides):
            side.wait_recv()
            self.grad[p, 0, self.middle] += self.from_left[p, self.middle]
            if not self.final:
                self.middles.append(
                    self.copies.start(self.grad.at[p, 0, self.middle], self.from_right.at[p], left)
                )

    def corner(self):
        left = self.place.at(0, -1)
        self.corners = {}
        for p in self.planes:
            self.copies.sent(self.ups[p, 0])
            self.copies.sent(self.downs[p, 0])
            self.ups[p, 0].wait_recv()
            self.grad[p, 0, self.top] += self.from_up[p, 0]
            self.downs[p, 0].wait_recv()
            self.grad[p, 0, self.below] += self.from_down[p, 0]
            for k, lines in enumerate((self.top, self.below)):
                self.corners[p, k] = self.copies.start(
                    self.grad.at[p, 0, lines], self.from_corner.at[p, k], left
                )

    def update(self):
        grad, extended, last = self.grad, self.extended, self.last
        top, middle, below = self.top, self.middle, self.below
        for p in self.planes:
            extended[p % 2][p // 2, 0] -= STEP_OBJECT * grad[p, 0]
        for j in range(1, last):
            for p in self.planes:
                self.ups[p, j].wait_recv()
                self.downs[p, j].wait_recv()
                extended[p % 2][p // 2, j, middle] -= STEP_OBJECT * grad[p, j, middle]
                extended[p % 2][p // 2, j, top] -= STEP_OBJECT * (grad[p, j, top] + self.from_up[p, j])
                extended[p % 2][p // 2, j, below] -= STEP_OBJECT * (grad[p, j, below] + self.from_down[p, j])
        for p, copy in zip(self.planes, self.middles):
            copy.wait_recv()
            extended[p % 2][p // 2, last, middle] -= STEP_OBJECT * self.from_right[p]
            for k, lines in enumerate((top, below)):
                self.corners[p, k].wait_recv()
                extended[p % 2][p // 2, last, lines] -= STEP_OBJECT * self.from_corner[p, k]

    def keep(self, new_field):
        for j in range(self.last):
            for p in self.planes:
                new_field[p, :, self.block[j]] = (
                    self.extended[p % 2][p // 2, j, self.own] - STEP_OBJECT * self.grad[p, j, self.own]
                )

    def complete(self, new_field):
        for j in list(range(1, self.last)) + [0]:
            for p in self.planes:
                self.ups[p, j].wait_recv()
                new_field[p, self.top, self.block[j]] -= STEP_OBJECT * self.from_up[p, j]


SLICE_PLANES = ((0, 2), (1, 3))


def program_kernel(
    tiles,
    cols,
    rows,
    columns,
    counts,
    field,
    probe_hbm,
    measured_hbm,
    table_hbm,
    new_field,
    new_probe,
    object_first,
    object_second,
    grad,
    beam,
    grad_beam,
    measured,
    table,
    windows,
    spread,
    patches,
    from_left,
    from_up,
    from_right,
    from_down,
    from_corner,
    *rest,
):
    sums, (local_sem, send, recv) = rest[:-3], rest[-3:]
    sums = [sums[: len(sums) // 2], sums[len(sums) // 2 :]]
    extended = (object_first, object_second)
    planes, count, tall, size = grad.shape
    last = count - 1
    height = tall - size
    slots = measured.shape[0]
    step_probe = 1.0 / (slots * tiles * cols)
    top, below, own = pl.ds(0, size), pl.ds(height, size), pl.ds(0, height)
    block = [pl.ds(j * size, size) for j in range(last)]
    place = Place(tiles, cols)
    copies = Copies(send, recv)
    up, left = place.at(-1, 0), place.at(0, -1)

    loads = [
        (field.at[p, :, block[j]], extended[p % 2].at[p // 2, j, own])
        for p in range(planes)
        for j in range(last)
    ]
    loads += [(probe_hbm, beam), (table_hbm, table), (measured_hbm, measured)]
    loads = [
        pltpu.make_async_copy(source, target, local_sem.at[k])
        for k, (source, target) in enumerate(loads)
    ]
    for load in loads:
        load.start()
    greet(met(place))

    halos, sides, corners = {}, {}, {}

    def send_halo(p, j):
        halos[p, j] = copies.start(
            field.at[p, top, block[j]], extended[p % 2].at[p // 2, j, below], up
        )

    def pass_corners(which):
        for p in SLICE_PLANES[which]:
            halos[p, 0].wait_recv()
            corners[p] = copies.start(
                extended[p % 2].at[p // 2, 0, below], extended[p % 2].at[p // 2, last, below], left
            )

    def take_halo(which):
        for p in SLICE_PLANES[which]:
            for copy in [halos[p, j] for j in range(1, last)] + [sides[p], corners[p]]:
                copy.wait_recv()

    for which in SLICE_PLANES:
        for p in which:
            send_halo(p, 0)
        for p in which:
            sides[p] = copies.start(
                field.at[p, :, block[0]], extended[p % 2].at[p // 2, last, own], left
            )
        for j in range(1, last):
            for p in which:
                send_halo(p, j)
    pass_corners(0)
    for load in loads:
        load.wait()
    take_halo(0)

    refs = (rows, columns, counts, measured, extended, beam, table, grad, grad_beam)
    work = Positions(refs + (windows, spread, patches), size, slots)
    waiting = None
    for sweep in range(ITERS):
        final = sweep == ITERS - 1
        landed = (from_left.at[sweep], from_up.at[sweep], from_right, from_down, from_corner)
        zeroth, first = [
            Overlap(place, copies, which, grad, extended, landed, final) for which in SLICE_PLANES
        ]
        if sweep == 0:
            for step in range(work.groups):
                work.propagate(step)
                if step == 0:
                    pass_corners(1)
            take_halo(1)
        else:
            lax.fori_loop(0, work.groups, lambda k, carry: (work.propagate(k), carry)[1], 0)
            waiting.update()
        copies.finish()
        grad_beam[...] = jnp.zeros_like(grad_beam)
        lax.fori_loop(0, work.groups, lambda step, carry: (work.diffract(step), carry)[1], 0)
        reduce = ProbeSum(place, copies, grad_beam, *sums[sweep])
        reduce.scatter_pair()
        for step in range(work.groups):
            work.place_patches(step, SLICE_PLANES[0])
            if step == 0:
                reduce.scatter_plane()
        zeroth.start()
        for p in SLICE_PLANES[1]:
            grad[p] = jnp.zeros(grad.shape[1:], f32)
        lax.fori_loop(
            0, work.groups, lambda k, carry: (work.place_patches(k, SLICE_PLANES[1]), carry)[1], 0
        )
        first.start()
        zeroth.start_inner()
        first.start_inner()
        reduce.sum_line()
        zeroth.first()
        reduce.gather_plane()
        first.first()
        zeroth.inner()
        if final:
            first.inner()
            zeroth.keep(new_field)
            first.keep(new_field)
            zeroth.complete(new_field)
            reduce.gather_pair()
            first.complete(new_field)
            new_probe[...] = beam[...] - step_probe * reduce.result()
            copies.finish()
        else:
            zeroth.corner()
            first.inner()
            reduce.gather_pair()
            first.corner()
            zeroth.update()
            beam[...] -= step_probe * reduce.result()
            waiting = first


def local(table, tiles, cols, object_field, probe, row_offsets, col_offsets, counts, measured):
    size = probe.shape[-1]
    height, width = object_field.shape[2:]
    slots = row_offsets.shape[-1]
    field = object_field.reshape(4, height, width)
    flat = (probe.shape[0] * probe.shape[1] * size, size)
    planes, last, tall = 4, width // size, height + size
    needed = planes * (2 * last + 2) + ITERS * ProbeSum.copies_needed(tiles, cols)
    needed += planes * (3 + 2 * last + 1 + 2) + planes * (3 + last)
    work = ITERS * slots * probe.shape[1] * 8 * 3 * 2 * 256 * 256 * 128
    smem = pl.BlockSpec(memory_space=pltpu.SMEM)
    hbm = pl.BlockSpec(memory_space=pl.ANY)
    vmem = pl.BlockSpec(memory_space=pltpu.VMEM)
    new_field, new_probe = pl.pallas_call(
        functools.partial(program_kernel, tiles, cols),
        out_shape=[jax.ShapeDtypeStruct(field.shape, f32), jax.ShapeDtypeStruct(flat, f32)],
        in_specs=[smem] * 3 + [hbm] * 4,
        out_specs=[vmem] * 2,
        scratch_shapes=[
            pltpu.VMEM((planes // 2, last + 1, tall, size), f32),
            pltpu.VMEM((planes // 2, last + 1, tall, size), f32),
            pltpu.VMEM((planes, last + 1, tall, size), f32),
            pltpu.VMEM(flat, f32),
            pltpu.VMEM(flat, f32),
            pltpu.VMEM((slots, size, size), f32),
            pltpu.VMEM(table.shape, bf16),
            pltpu.VMEM((slots, 2, size, size), f32),
            pltpu.VMEM((slots, probe.shape[1], 2, size, size), f32),
            pltpu.VMEM((slots, planes, size, size), f32),
            pltpu.VMEM((ITERS, planes, tall, size), f32),
            pltpu.VMEM((ITERS, planes, last, size, size), f32),
            pltpu.VMEM((planes, height - size, size), f32),
            pltpu.VMEM((planes, last, size, size), f32),
            pltpu.VMEM((planes, 2, size, size), f32),
            *ProbeSum.scratch(*flat, tiles, cols),
            *ProbeSum.scratch(*flat, tiles, cols),
            pltpu.SemaphoreType.DMA((planes * last + 3,)),
            pltpu.SemaphoreType.DMA((needed,)),
            pltpu.SemaphoreType.DMA((needed,)),
        ],
        compiler_params=pltpu.CompilerParams(
            collective_id=0, has_side_effects=True, vmem_limit_bytes=VMEM_LIMIT
        ),
        cost_estimate=pl.CostEstimate(flops=work, bytes_accessed=5 * 2**20, transcendentals=0),
        name="ptychography",
    )(
        row_offsets.reshape(slots),
        col_offsets.reshape(slots),
        counts.reshape(1),
        field,
        probe.reshape(flat),
        measured.reshape(slots, size, size),
        table,
    )
    return new_field.reshape(object_field.shape), new_probe.reshape(probe.shape)


def solution(mesh):
    table = jnp.asarray(transform_tables(128))
    tiles, cols = mesh.shape["tiles"], mesh.shape["cols"]
    in_specs = (
        P(None, None, "tiles", "cols"),
        P(),
        P("tiles", "cols", None),
        P("tiles", "cols", None),
        P("tiles", "cols"),
        P("tiles", "cols", None, None, None),
    )
    out_specs = (P(None, None, "tiles", "cols"), P())
    body = functools.partial(local, table, tiles, cols)
    return jax.shard_map(body, mesh=mesh, in_specs=in_specs, out_specs=out_specs, check_vma=False)
```
